32 devices in a mesh: groups: 2 (over y), dp: 4 (over z), tensor: 4 (over x, core).
Axes of the slice: x: 2, y: 2, z: 4, core: 2. Of those that a mesh axis runs over, the one named last changes fastest.
Arguments:
- patches: bfloat16 [8192, 1280], P(('groups', 'dp')), parts along dimension 0, may hold values from -64 to 64
- grids: int32 [8, 2], P(('groups', 'dp')), parts along dimension 0, may hold values from 16 to 32, as said below
- dest: int32 [8, 256], P(('groups', 'dp')), parts along dimension 0, may hold values from 0 to 1535, as said below
- norm_gain: float32 [1280], replicated, may hold values from 0.1 to 1.9
- qkv_weight: bfloat16 [3, 1280, 1280], P(None, None, 'tensor'), may hold values from -8 to 8
- qkv_bias: float32 [3, 1280], P(None, 'tensor'), may hold values from -3 to 3
- proj_weight: bfloat16 [1280, 1280], P('tensor'), may hold values from -0.15625 to 0.15625
- proj_bias: float32 [1280], replicated, may hold values from -3 to 3
- merge_gain: float32 [1280], replicated, may hold values from 0.1 to 1.9
- w_first: bfloat16 [5120, 5120], P('dp', 'tensor'), may hold values from -0.078125 to 0.078125
- b_first: float32 [5120], P('tensor'), may hold values from -3 to 3
- w_second: bfloat16 [5120, 8192], P('tensor', 'dp'), may hold values from -0.078125 to 0.078125
- b_second: float32 [8192], P('tensor'), may hold values from -3 to 3
- text_embed: bfloat16 [3072, 8192], P(('groups', 'dp'), 'tensor'), parts along dimension 0, may hold values from -6 to 6
Outputs:
- sequence: bfloat16 [3072, 8192], P(('groups', 'dp'), 'tensor'), parts along dimension 0
The draws below stay inside these ranges and needn't reach their ends.
There are 2 independent parts, one for each index of `groups`. The reference program is written for one: setup_inputs(seed, part) draws one part's arguments, and reference() takes and returns one part's arrays. A program takes and returns all parts, laid end to end along the dimension named above; an argument that names none is the same for every part. Nothing has to cross between parts.
Inputs may be any that keep to these rules, and one draw needn't show every extreme that they name: `grids`: both sides of every grid are even, at least 16 and at most 32; in each part along `groups`, the first image (the one on dp index 0) has the full 32 x 32 grid. The rows dest[i, j] with j < grids[i, 0] * grids[i, 1] / 4 are distinct over all images; the live rows of one image reach at most 64 rows in each aligned block of 384 sequence rows, and exactly that many for a full grid.
All inputs are finite; a program needn't handle non-finite values.
Results may differ from the reference program's by a relative error of at most 0.014.
Values may be sent and summed in bfloat16 or wider, within the bound.
No kernel may reach another device: no remote copies, remote signals or barrier semaphores. Data moves between devices by JAX's collectives and lax.ppermute only.
A program may use at most 128 MiB of HBM per device.

```python
import math
import jax
import jax.numpy as jnp
from jax import lax

V = 1280
HEADS = 16
HEAD_DIM = 80
D_LM = 8192
SIDE = 32
IMG_DEV = 1
IMAGES = 4
PATCHES = 1024
MERGED = 256
MERGE_W = 5120
ROWS = 4096
VIS = 1024
GAP = 128
SEQ_DP = 384
SEQ = 1536
BLOCK = 64
N_DP = 4
N_TENSOR = 4


def layout_helper(key):
    base = jax.random.fold_in(key, 4711)
    side_key, offset_key, order_key = jax.random.split(base, 3)
    halves = jax.random.randint(side_key, (IMAGES, 2), SIDE // 4, SIDE // 2 + 1)
    forced = jnp.arange(IMAGES)[:, None] < IMG_DEV
    halves = jnp.where(forced, SIDE // 2, halves)
    grid_sides = (2 * halves).astype(jnp.int32)
    offsets = jax.random.randint(offset_key, (IMAGES,), 0, GAP + 1)
    regions = jax.random.permutation(order_key, IMAGES)
    starts = regions * (MERGED + GAP) + offsets
    positions = starts[:, None] + jnp.arange(MERGED)[None, :]
    block_index = positions // BLOCK
    shard_index = block_index % N_DP
    local_row = block_index // N_DP * BLOCK + positions % BLOCK
    rows_out = (shard_index * SEQ_DP + local_row).astype(jnp.int32)
    return (grid_sides, rows_out)


def draw_grids(key, part):
    return layout_helper(key)[0]


def draw_dest(key, part):
    return layout_helper(key)[1]


def draw_patches(key, part):
    base_key = jax.random.fold_in(jax.random.fold_in(key, 31), 0)
    values = jax.random.normal(base_key, (ROWS, V), jnp.float32)
    return jnp.clip(values, -64.0, 64.0).astype(jnp.bfloat16)


def draw_qkv_weight(key, part):
    base_key = jax.random.fold_in(jax.random.fold_in(key, 57), 0)
    values = jax.random.normal(base_key, (3, V, V), jnp.float32) * V ** (-0.5)
    return jnp.clip(values, -8.0, 8.0).astype(jnp.bfloat16)


def levels(own_key, extent, pieces, low, top_value):
    def one(axis_at, parts):
        heights = jax.random.uniform(jax.random.fold_in(jax.random.fold_in(own_key, 6), axis_at), (parts,), jnp.float32, low / len(pieces), top_value / len(pieces))
        return jnp.repeat(jnp.exp(heights), extent[axis_at] // parts).reshape((-1,) + (1,) * (len(extent) - axis_at - 1))

    level = one(*pieces[0])
    for cut in pieces[1:]:
        level = level * one(*cut)
    return level


def centred(key, dims, spread, limit, shards=(), kind=jnp.bfloat16):
    result = spread * jax.random.normal(key, dims, jnp.float32)
    if shards:
        result = result * levels(key, dims, shards, -0.22, 0.18)
    return jnp.clip(result, -limit, limit).astype(kind)


def setup_inputs(seed: int = 0, part: int = 0) -> dict:
    key_list = jax.random.split(jax.random.key(seed), 15)
    part_splits = jax.random.split(jax.random.fold_in(key_list[14], part), 15)
    patches = draw_patches(jax.random.fold_in(jax.random.fold_in(key_list[14], part), 71), part)
    grids = draw_grids(jax.random.fold_in(jax.random.fold_in(key_list[14], part), 71), part)
    dest = draw_dest(jax.random.fold_in(jax.random.fold_in(key_list[14], part), 71), part)
    norm_gain = jnp.clip(1.0 + 0.18 * jax.random.normal(key_list[3], (V,), jnp.float32), 0.1, 1.9)
    qkv_weight = draw_qkv_weight(jax.random.fold_in(key_list[14], 71), part)
    qkv_bias = centred(key_list[5], (3, V), 0.5, 3.0, ((1, 4),), jnp.float32)
    proj_weight = centred(key_list[6], (V, V), V ** -0.5, 0.15625, ((0, 4),))
    proj_bias = centred(key_list[7], (V,), 0.5, 3.0, (), jnp.float32)
    merge_gain = jnp.clip(1.0 + 0.18 * jax.random.normal(key_list[8], (V,), jnp.float32), 0.1, 1.9)
    w_first = centred(key_list[9], (MERGE_W, MERGE_W), MERGE_W ** -0.5, 0.078125, ((0, 4), (1, 4)))
    b_first = centred(key_list[10], (MERGE_W,), 0.5, 3.0, ((0, 4),), jnp.float32)
    w_second = centred(key_list[11], (MERGE_W, D_LM), MERGE_W ** -0.5, 0.078125, ((0, 4), (1, 4)))
    b_second = centred(key_list[12], (D_LM,), 0.5, 3.0, ((0, 4),), jnp.float32)
    text_embed = centred(part_splits[13], (SEQ, D_LM), 1.0, 6.0, ((0, 4), (1, 4)))
    return dict(patches=patches, grids=grids, dest=dest, norm_gain=norm_gain, qkv_weight=qkv_weight, qkv_bias=qkv_bias, proj_weight=proj_weight, proj_bias=proj_bias, merge_gain=merge_gain, w_first=w_first, b_first=b_first, w_second=w_second, b_second=b_second, text_embed=text_embed)


def rms_scale(values, gain):
    return values * lax.rsqrt(lax.optimization_barrier(jnp.mean(values * values, axis=-1, keepdims=True)) + 1e-06) * gain

def reference(patches, grids, dest, norm_gain, qkv_weight, qkv_bias, proj_weight, proj_bias, merge_gain, w_first, b_first, w_second, b_second, text_embed):
    live_count = grids[:, 0] * grids[:, 1]
    image_rows = patches.reshape(IMAGES, PATCHES, V)

    def encode(image_item):
        rows_in, count_in = image_item
        normed = rms_scale(rows_in.astype(jnp.float32), norm_gain).astype(jnp.bfloat16)
        projected = jnp.einsum('rv,jvc->jrc', normed.astype(jnp.float32), qkv_weight.astype(jnp.float32)) + qkv_bias[:, None, :]
        projected = projected.astype(jnp.bfloat16).reshape(3, PATCHES, HEADS, HEAD_DIM)
        queries = projected[0].astype(jnp.float32)
        key_rows = projected[1].astype(jnp.float32)
        value_rows = projected[2].astype(jnp.float32)
        scores = jnp.einsum('qhd,khd->hqk', queries, key_rows) / math.sqrt(HEAD_DIM)
        live_keys = jnp.arange(PATCHES, dtype=jnp.int32) < count_in
        scores = jnp.where(live_keys[None, None, :], scores, jnp.float32(-1e+30))
        peak_score = lax.optimization_barrier(jnp.max(scores, axis=-1, keepdims=True))
        exponent = jnp.exp(scores - peak_score)
        weights = (exponent / lax.optimization_barrier(jnp.sum(exponent, axis=-1, keepdims=True))).astype(jnp.bfloat16)
        attended = jnp.einsum('hqk,khd->qhd', weights.astype(jnp.float32), value_rows)
        return attended.astype(jnp.bfloat16).reshape(PATCHES, V)
    attended = lax.map(encode, (image_rows, live_count)).reshape(ROWS, V)
    group_width = V // N_TENSOR
    summed = jnp.zeros((ROWS, V), jnp.float32)
    for group in range(N_TENSOR):
        part_rows = jnp.dot(attended[:, group * group_width:(group + 1) * group_width], proj_weight[group * group_width:(group + 1) * group_width], preferred_element_type=jnp.float32)
        summed = summed + part_rows.astype(jnp.bfloat16).astype(jnp.float32)
    resid = patches.astype(jnp.float32) + summed + proj_bias
    merged_in = rms_scale(resid, merge_gain).astype(jnp.bfloat16).reshape(VIS, MERGE_W)
    first_out = jnp.dot(merged_in, w_first, preferred_element_type=jnp.float32) + b_first
    hidden = jax.nn.gelu(first_out, approximate=False).astype(jnp.bfloat16)
    hidden_width = MERGE_W // N_TENSOR
    visual = jnp.zeros((VIS, D_LM), jnp.float32)
    for group in range(N_TENSOR):
        second_rows = jnp.dot(hidden[:, group * hidden_width:(group + 1) * hidden_width], w_second[group * hidden_width:(group + 1) * hidden_width], preferred_element_type=jnp.float32)
        visual = visual + second_rows.astype(jnp.bfloat16).astype(jnp.float32)
    visual = (visual + b_second).astype(jnp.bfloat16)
    live_rows = jnp.arange(MERGED, dtype=jnp.int32)[None, :] < (live_count // 4)[:, None]
    target = jnp.where(live_rows, dest, SEQ).astype(jnp.int32).reshape(VIS)
    sequence = text_embed.at[target].set(visual, mode='drop')
    return sequence
```

```python
import math

import jax
import jax.numpy as jnp
from jax import lax
from jax.sharding import PartitionSpec as P

HEAD_DIM = 80
MERGE = 4


def rms_scale(values, gain):
    return values * lax.rsqrt(jnp.mean(values * values, axis=-1, keepdims=True) + 1e-06) * gain


def dot32(a, b):
    return jnp.dot(a, b, preferred_element_type=jnp.float32)


def swap(x, axis, k):
    n = lax.axis_size(axis)
    return lax.ppermute(x, axis, [(a, a ^ k) for a in range(n)])


def gather_xor(x, axis):
    n = lax.axis_size(axis)
    blocks = {0: x}
    step = n // 2
    while step:
        for k in list(blocks):
            blocks[k | step] = swap(blocks[k], axis, step)
        step //= 2
    return [blocks[k] for k in range(n)]


def scatter_sum_xor(blocks, axis):
    n = lax.axis_size(axis)
    blocks = dict(enumerate(blocks))
    step = 1
    while step < n:
        for k in sorted(blocks):
            if k & step:
                got = swap(blocks[k], axis, step)
                mine = k ^ step
                blocks[mine] = (
                    blocks[mine].astype(jnp.float32) + got.astype(jnp.float32)
                ).astype(got.dtype)
        blocks = {k: v for k, v in blocks.items() if not k & step}
        step *= 2
    return blocks[0]


def slots(target, seq_rows, shards):
    shard = jnp.where(target >= 0, target // seq_rows, shards)
    same = shard[..., :, None] == shard[..., None, :]
    count = target.shape[-1]
    earlier = jnp.arange(count)[None, :] < jnp.arange(count)[:, None]
    rank = jnp.sum((same & earlier).astype(jnp.int32), axis=-1)
    return shard, rank


def local(
    patches,
    grids,
    dest,
    norm_gain,
    qkv_weight,
    qkv_bias,
    proj_weight,
    proj_bias,
    merge_gain,
    w_first,
    b_first,
    w_second,
    b_second,
    text_embed,
):
    dps, tensors = lax.axis_size("dp"), lax.axis_size("tensor")
    tensor_at, dp_at = lax.axis_index("tensor"), lax.axis_index("dp")
    rows, width = patches.shape
    merged = dest.shape[1]
    seq_rows = text_embed.shape[0]
    heads = qkv_weight.shape[2] // HEAD_DIM
    cap = merged // dps
    part = cap // tensors

    live = grids[0, 0] * grids[0, 1]
    target = jnp.where(jnp.arange(merged, dtype=jnp.int32) < live // MERGE, dest[0], -1)
    targets = lax.all_gather(target, "dp", axis=0)
    proj_blocks = gather_xor(proj_weight, "tensor")

    shard, rank = slots(target, seq_rows, dps)
    order = jnp.arange(rows, dtype=jnp.int32)
    slot_of = order % part
    shard_of = order // part % dps
    patch_of = order // (part * dps) % MERGE
    rank_of = order // (part * dps * MERGE) * part + slot_of
    row_shard = jnp.repeat(shard, MERGE)
    row_rank = jnp.repeat(rank, MERGE)
    row_patch = jnp.tile(jnp.arange(MERGE, dtype=jnp.int32), merged)
    place = (
        (shard_of[:, None] == row_shard[None, :])
        & (rank_of[:, None] == row_rank[None, :])
        & (patch_of[:, None] == row_patch[None, :])
    ).astype(jnp.bfloat16)

    normed = rms_scale(patches.astype(jnp.float32), norm_gain).astype(jnp.bfloat16)
    projected = (
        jnp.einsum("rv,jvc->jrc", normed, qkv_weight, preferred_element_type=jnp.float32)
        + qkv_bias[:, None, :]
    )
    projected = projected.astype(jnp.bfloat16).reshape(3, rows, heads, HEAD_DIM)
    scores = jnp.einsum(
        "qhd,khd->hqk", projected[0], projected[1], preferred_element_type=jnp.float32
    ) / math.sqrt(HEAD_DIM)
    live_keys = jnp.arange(rows, dtype=jnp.int32) < live
    scores = jnp.where(live_keys[None, None, :], scores, jnp.float32(-1e30))
    peak_score = jnp.max(scores, axis=-1, keepdims=True)
    exponent = jnp.exp(scores - peak_score)
    weights = (exponent / jnp.sum(exponent, axis=-1, keepdims=True)).astype(jnp.bfloat16)
    attended = jnp.einsum("hqk,khd->qhd", weights, projected[2], preferred_element_type=jnp.float32)
    attended = attended.astype(jnp.bfloat16).reshape(rows, heads * HEAD_DIM)

    attended = dot32(place, attended).astype(jnp.bfloat16)
    attended = attended.reshape(tensors, rows // tensors, heads * HEAD_DIM)
    place = place.reshape(tensors, rows // tensors, rows)
    summed = None
    for k in range(tensors):
        block = lax.dynamic_index_in_dim(attended, tensor_at ^ k, 0, keepdims=False)
        if k:
            block = swap(block, "tensor", k)
        term = dot32(block, proj_blocks[k])
        summed = term if summed is None else summed + term
    own = dot32(lax.dynamic_index_in_dim(place, tensor_at, 0, keepdims=False), patches)
    resid = own + summed + proj_bias
    merged_in = rms_scale(resid, merge_gain).astype(jnp.bfloat16)

    piece = w_first.shape[0]
    splits = width // piece
    merged_in = merged_in.reshape(MERGE, dps * part, splits, piece).transpose(0, 2, 1, 3)
    merged_in = merged_in.reshape(dps, dps * part, piece)
    received = lax.all_to_all(merged_in, "dp", split_axis=0, concat_axis=0, tiled=True)
    received = received.reshape(dps * dps * part, piece)
    received = jnp.concatenate(gather_xor(received, "tensor"), axis=0)

    first_part = dot32(received, w_first).astype(jnp.bfloat16)
    first_out = lax.psum(first_part, "dp").astype(jnp.float32)
    hidden = jax.nn.gelu(first_out + b_first, approximate=False).astype(jnp.bfloat16)

    second_part = dot32(hidden, w_second).astype(jnp.bfloat16)
    columns = w_second.shape[1]
    second_part = second_part.reshape(tensors, dps * dps * part, columns)
    visual = scatter_sum_xor([second_part[k] for k in range(tensors)], "tensor")
    visual = visual.reshape(dps, dps, part, columns).transpose(1, 0, 2, 3)
    visual = lax.all_to_all(visual, "dp", split_axis=0, concat_axis=0, tiled=True)
    shares = dps // tensors
    visual = visual.reshape(tensors, shares, dps * part, columns).transpose(0, 2, 1, 3)
    visual = visual.reshape(tensors, dps * part, shares * columns)
    visual = lax.all_to_all(visual, "tensor", split_axis=0, concat_axis=0, tiled=True)
    visual = visual.reshape(tensors * dps * part, shares * columns)

    all_shard, all_rank = slots(targets, seq_rows, dps)
    mine = all_shard == dp_at
    slot_rows = jnp.sum(
        jnp.where(
            mine[:, None, :] & (all_rank[:, None, :] == jnp.arange(cap)[None, :, None]),
            targets[:, None, :] % seq_rows + 1,
            0,
        ),
        axis=-1,
    )
    slot_rows = slot_rows.reshape(dps, tensors, part).transpose(1, 0, 2).reshape(-1) - 1
    hit = jnp.arange(seq_rows, dtype=jnp.int32)[:, None] == slot_rows[None, :]
    covered = jnp.any(hit, axis=1)
    placed = dot32(hit.astype(jnp.bfloat16), visual) + b_second
    return jnp.where(covered[:, None], placed.astype(jnp.bfloat16), text_embed)


def solution(mesh):
    in_specs = (
        P(("groups", "dp"), None),
        P(("groups", "dp"), None),
        P(("groups", "dp"), None),
        P(),
        P(None, None, "tensor"),
        P(None, "tensor"),
        P("tensor", None),
        P(),
        P(),
        P("dp", "tensor"),
        P("tensor"),
        P("tensor", "dp"),
        P("tensor"),
        P(("groups", "dp"), "tensor"),
    )
    out_specs = P(("groups", "dp"), "tensor")
    return jax.shard_map(local, mesh=mesh, in_specs=in_specs, out_specs=out_specs, check_vma=False)
```

```python
import math

import jax
import jax.numpy as jnp
from jax import lax
from jax.sharding import PartitionSpec as P

HEAD_DIM = 80
MERGE = 4
BATCHES = 4


def rms_scale(values, gain):
    return values * lax.rsqrt(jnp.mean(values * values, axis=-1, keepdims=True) + 1e-06) * gain


def dot32(a, b):
    return jnp.dot(a, b, preferred_element_type=jnp.float32)


def swap(x, axis, k):
    n = lax.axis_size(axis)
    return lax.ppermute(x, axis, [(a, a ^ k) for a in range(n)])


def gather_xor(x, axis):
    n = lax.axis_size(axis)
    blocks = {0: x}
    step = n // 2
    while step:
        for k in list(blocks):
            blocks[k | step] = swap(blocks[k], axis, step)
        step //= 2
    return [blocks[k] for k in range(n)]


def gather_low(x, axis, count):
    blocks = {0: x}
    step = count // 2
    while step:
        for k in list(blocks):
            blocks[k | step] = swap(blocks[k], axis, step)
        step //= 2
    return [blocks[k] for k in range(count)]


def add16(a, b):
    return (a.astype(jnp.float32) + b.astype(jnp.float32)).astype(jnp.bfloat16)


def scatter_low(blocks, axis, count):
    step = 1
    blocks = {k: blocks[k] for k in range(count)}
    while step < count:
        kept = {}
        for k in blocks:
            if not k & step:
                kept[k] = add16(blocks[k], swap(blocks[k | step], axis, step))
        blocks = kept
        step *= 2
    return blocks[0]


def pick(x, at):
    return lax.dynamic_index_in_dim(x, at, 0, keepdims=False)


def line_sum(parts, axis):
    n = lax.axis_size(axis)
    here = lax.axis_index(axis)
    blocks = parts.shape[1]
    size = n // blocks

    def chain(place, step_to):
        sent, came = [], []
        for step in range(n + blocks - 1):
            block = jnp.clip(step - place, 0, blocks - 1) ^ (here // size)
            term = lax.dynamic_index_in_dim(parts, block, 1, keepdims=False)
            sent.append(add16(term, came[-1]) if came else term)
            pairs = [step_to(a) for a in range(n - 1) if 0 <= step - a < blocks]
            if pairs:
                came.append(lax.ppermute(sent[-1], axis, pairs))
        return sent, came

    up, _ = chain(here, lambda a: (a, a + 1))
    _, down = chain(n - 1 - here, lambda a: (n - 1 - a, n - 2 - a))
    sums = []
    for block in range(blocks):
        below, above = up[block + n - 1], jnp.zeros_like(up[0])
        for place in range(n - 1):
            below = jnp.where(here == place, up[block + place], below)
            above = jnp.where(here == place, down[block + n - 2 - place], above)
        sums.append(below.astype(jnp.float32) + above.astype(jnp.float32))
    return sums


def slots(target, seq_rows, shards):
    shard = jnp.where(target >= 0, target // seq_rows, shards)
    same = shard[..., :, None] == shard[..., None, :]
    count = target.shape[-1]
    earlier = jnp.arange(count)[None, :] < jnp.arange(count)[:, None]
    rank = jnp.sum((same & earlier).astype(jnp.int32), axis=-1)
    return shard, rank


def local(
    patches,
    grids,
    dest,
    norm_gain,
    qkv_weight,
    qkv_bias,
    proj_weight,
    proj_bias,
    merge_gain,
    w_first,
    b_first,
    w_second,
    b_second,
    text_embed,
):
    dps, tensors = lax.axis_size("dp"), lax.axis_size("tensor")
    tensor_at, dp_at = lax.axis_index("tensor"), lax.axis_index("dp")
    rows, width = patches.shape
    merged = dest.shape[1]
    seq_rows = text_embed.shape[0]
    heads = qkv_weight.shape[2] // HEAD_DIM
    cap = merged // dps
    part = cap // tensors

    live = grids[0, 0] * grids[0, 1]
    target = jnp.where(jnp.arange(merged, dtype=jnp.int32) < live // MERGE, dest[0], -1)
    targets = lax.all_gather(target, "dp", axis=0)
    proj_blocks = gather_xor(proj_weight, "tensor")

    shard, rank = slots(target, seq_rows, dps)
    order = jnp.arange(rows, dtype=jnp.int32)
    slot_of = order % part
    shard_of = order // part % dps
    patch_of = order // (part * dps) % MERGE
    rank_of = order // (part * dps * MERGE) * part + slot_of
    row_shard = jnp.repeat(shard, MERGE)
    row_rank = jnp.repeat(rank, MERGE)
    row_patch = jnp.tile(jnp.arange(MERGE, dtype=jnp.int32), merged)
    place = (
        (shard_of[:, None] == row_shard[None, :])
        & (rank_of[:, None] == row_rank[None, :])
        & (patch_of[:, None] == row_patch[None, :])
    ).astype(jnp.bfloat16)

    normed = rms_scale(patches.astype(jnp.float32), norm_gain).astype(jnp.bfloat16)
    projected = (
        jnp.einsum("rv,jvc->jrc", normed, qkv_weight, preferred_element_type=jnp.float32)
        + qkv_bias[:, None, :]
    )
    projected = projected.astype(jnp.bfloat16).reshape(3, rows, heads, HEAD_DIM)
    scores = jnp.einsum(
        "qhd,khd->hqk", projected[0], projected[1], preferred_element_type=jnp.float32
    ) / math.sqrt(HEAD_DIM)
    live_keys = jnp.arange(rows, dtype=jnp.int32) < live
    scores = jnp.where(live_keys[None, None, :], scores, jnp.float32(-1e30))
    peak_score = jnp.max(scores, axis=-1, keepdims=True)
    exponent = jnp.exp(scores - peak_score)
    weights = (exponent / jnp.sum(exponent, axis=-1, keepdims=True)).astype(jnp.bfloat16)
    attended = jnp.einsum("hqk,khd->qhd", weights, projected[2], preferred_element_type=jnp.float32)
    attended = attended.astype(jnp.bfloat16).reshape(rows, heads * HEAD_DIM)

    attended = dot32(place, attended).astype(jnp.bfloat16)
    attended = attended.reshape(tensors, rows // tensors, heads * HEAD_DIM)
    place = place.reshape(tensors, rows // tensors, rows)
    summed = None
    for k in range(tensors):
        block = lax.dynamic_index_in_dim(attended, tensor_at ^ k, 0, keepdims=False)
        if k:
            block = swap(block, "tensor", k)
        term = dot32(block, proj_blocks[k])
        summed = term if summed is None else summed + term
    own = dot32(lax.dynamic_index_in_dim(place, tensor_at, 0, keepdims=False), patches)
    resid = own + summed + proj_bias
    merged_in = rms_scale(resid, merge_gain).astype(jnp.bfloat16)

    piece = w_first.shape[0]
    splits = width // piece
    merged_in = merged_in.reshape(MERGE, dps * part, splits, piece).transpose(0, 2, 1, 3)
    merged_in = merged_in.reshape(dps, dps * part, piece)
    near, far = [], []
    for j in range(dps):
        block = pick(merged_in, dp_at ^ j)
        if j:
            block = swap(block, "dp", j)
        near.append(block)
        far.append(swap(block, "tensor", tensors // 2))
    near = gather_low(jnp.stack(near), "tensor", tensors // 2)
    far = gather_low(jnp.stack(far), "tensor", tensors // 2)

    totals = []
    batches = min(dps, BATCHES)
    images = dps // batches
    for stream in (near, far):
        lines = jnp.stack(stream)
        if images > 1:
            lines = lines.reshape(tensors // 2, batches, images, dps * part, piece)
            lines = lines[:, :, jnp.arange(images) ^ (dp_at % images)]
        first_part = dot32(lines.reshape(-1, piece), w_first).astype(jnp.bfloat16)
        first_part = first_part.reshape(tensors // 2, batches, images * dps * part, -1)
        totals.append(line_sum(first_part, "dp"))

    columns = w_second.shape[1]
    shares = dps // tensors
    visual = []
    for batch in range(batches):
        halves = []
        for total in totals:
            first_out = total[batch].astype(jnp.float32) + b_first
            hidden = jax.nn.gelu(first_out, approximate=False).astype(jnp.bfloat16)
            second_part = dot32(hidden.reshape(-1, hidden.shape[-1]), w_second).astype(jnp.bfloat16)
            second_part = second_part.reshape(tensors // 2, -1, columns)
            halves.append(scatter_low(second_part, "tensor", tensors // 2))
        block = add16(halves[0], swap(halves[1], "tensor", tensors // 2))
        block = block.reshape(images, dps, part, columns)
        shard_blocks = []
        for j in range(dps):
            moved = lax.dynamic_index_in_dim(block, dp_at ^ j, 1, keepdims=False)
            shard_blocks.append(swap(moved, "dp", j) if j else moved)
        shard_blocks = jnp.stack(shard_blocks).reshape(
            tensors, shares, images * part, columns
        )
        for k in range(tensors):
            moved = pick(shard_blocks, (tensor_at ^ k) ^ (dp_at // shares))
            moved = swap(moved, "tensor", k) if k else moved
            if shares > 1:
                moved = jnp.concatenate(
                    [pick(moved, (dp_at % shares) ^ j) for j in range(shares)], axis=-1
                )
            visual.append(moved.reshape(images * part, shares * columns))
    visual = jnp.concatenate(visual, axis=0)

    all_shard, all_rank = slots(targets, seq_rows, dps)
    mine = all_shard == dp_at
    slot_rows = jnp.sum(
        jnp.where(
            mine[:, None, :] & (all_rank[:, None, :] == jnp.arange(cap)[None, :, None]),
            targets[:, None, :] % seq_rows + 1,
            0,
        ),
        axis=-1,
    )
    slot_rows = slot_rows.reshape(batches, images, tensors, part).transpose(0, 2, 1, 3)
    slot_rows = slot_rows[:, jnp.arange(tensors) ^ tensor_at].reshape(-1) - 1
    hit = jnp.arange(seq_rows, dtype=jnp.int32)[:, None] == slot_rows[None, :]
    covered = jnp.any(hit, axis=1)
    placed = dot32(hit.astype(jnp.bfloat16), visual) + b_second
    return jnp.where(covered[:, None], placed.astype(jnp.bfloat16), text_embed)


def solution(mesh):
    in_specs = (
        P(("groups", "dp"), None),
        P(("groups", "dp"), None),
        P(("groups", "dp"), None),
        P(),
        P(None, None, "tensor"),
        P(None, "tensor"),
        P("tensor", None),
        P(),
        P(),
        P("dp", "tensor"),
        P("tensor"),
        P("tensor", "dp"),
        P("tensor"),
        P(("groups", "dp"), "tensor"),
    )
    out_specs = P(("groups", "dp"), "tensor")
    return jax.shard_map(local, mesh=mesh, in_specs=in_specs, out_specs=out_specs, check_vma=False)
```

```python
import functools
import math

import jax
import jax.numpy as jnp
from jax import lax
from jax.experimental import pallas as pl
from jax.experimental.pallas import tpu as pltpu
from jax.sharding import PartitionSpec as P

HEAD_DIM = 80
MERGE = 4
BATCHES = 4
LANES = 128
QUERY_ROWS = 256
VMEM_BYTES = 48 * 1024 * 1024


def rms_scale(values, gain):
    return values * lax.rsqrt(jnp.mean(values * values, axis=-1, keepdims=True) + 1e-06) * gain


def dot32(a, b):
    return jnp.dot(a, b, preferred_element_type=jnp.float32)


def swap(x, axis, k):
    n = lax.axis_size(axis)
    return lax.ppermute(x, axis, [(a, a ^ k) for a in range(n)])


def gather_xor(x, axis):
    n = lax.axis_size(axis)
    blocks = {0: x}
    step = n // 2
    while step:
        for k in list(blocks):
            blocks[k | step] = swap(blocks[k], axis, step)
        step //= 2
    return [blocks[k] for k in range(n)]


def gather_low(x, axis, count):
    blocks = {0: x}
    step = count // 2
    while step:
        for k in list(blocks):
            blocks[k | step] = swap(blocks[k], axis, step)
        step //= 2
    return [blocks[k] for k in range(count)]


def add16(a, b):
    return (a.astype(jnp.float32) + b.astype(jnp.float32)).astype(jnp.bfloat16)


def scatter_low(blocks, axis, count):
    step = 1
    blocks = {k: blocks[k] for k in range(count)}
    while step < count:
        kept = {}
        for k in blocks:
            if not k & step:
                kept[k] = add16(blocks[k], swap(blocks[k | step], axis, step))
        blocks = kept
        step *= 2
    return blocks[0]


def pick(x, at):
    return lax.dynamic_index_in_dim(x, at, 0, keepdims=False)


def line_sum(parts, axis):
    n = lax.axis_size(axis)
    here = lax.axis_index(axis)
    blocks = parts.shape[1]
    size = n // blocks

    def chain(place, step_to):
        sent, came = [], []
        for step in range(n + blocks - 1):
            block = jnp.clip(step - place, 0, blocks - 1) ^ (here // size)
            term = lax.dynamic_index_in_dim(parts, block, 1, keepdims=False)
            sent.append(add16(term, came[-1]) if came else term)
            pairs = [step_to(a) for a in range(n - 1) if 0 <= step - a < blocks]
            if pairs:
                came.append(lax.ppermute(sent[-1], axis, pairs))
        return sent, came

    up, _ = chain(here, lambda a: (a, a + 1))
    _, down = chain(n - 1 - here, lambda a: (n - 1 - a, n - 2 - a))
    sums = []
    for block in range(blocks):
        below, above = up[block + n - 1], jnp.zeros_like(up[0])
        for place in range(n - 1):
            below = jnp.where(here == place, up[block + place], below)
            above = jnp.where(here == place, down[block + n - 2 - place], above)
        sums.append(below.astype(jnp.float32) + above.astype(jnp.float32))
    return sums


def slots(target, seq_rows, shards):
    shard = jnp.where(target >= 0, target // seq_rows, shards)
    same = shard[..., :, None] == shard[..., None, :]
    count = target.shape[-1]
    earlier = jnp.arange(count)[None, :] < jnp.arange(count)[:, None]
    rank = jnp.sum((same & earlier).astype(jnp.int32), axis=-1)
    return shard, rank


def spread(count):
    row = lax.broadcasted_iota(jnp.int32, (count * HEAD_DIM, count * LANES), 0)
    col = lax.broadcasted_iota(jnp.int32, (count * HEAD_DIM, count * LANES), 1)
    lane = col % LANES
    return ((lane < HEAD_DIM) & (row == col // LANES * HEAD_DIM + lane)).astype(jnp.bfloat16)


def attend_kernel(
    live_ref, x_ref, gain_ref, w_ref, b_ref, dst_ref, own_ref, *rest
):
    outs, (q_ref, k_ref, v_ref, att_ref) = rest[:-4], rest[-4:]
    rows = x_ref.shape[0]
    heads = w_ref.shape[2] // HEAD_DIM
    live = live_ref[0]
    step = min(QUERY_ROWS, rows)
    to_lanes = spread(heads)
    lane = lax.broadcasted_iota(jnp.int32, (step, heads * LANES), 1) % LANES
    extra = lane == HEAD_DIM
    for at in range(0, rows, step):
        normed = rms_scale(x_ref[at : at + step, :].astype(jnp.float32), gain_ref[...])
        normed = normed.astype(jnp.bfloat16)
        key_row = at + lax.broadcasted_iota(jnp.int32, (step, heads * LANES), 0)
        masked = jnp.where(key_row < live, 0.0, -1e30)
        for j, (ref, fill) in enumerate(((q_ref, 1.0), (k_ref, masked), (v_ref, 1.0))):
            out = (dot32(normed, w_ref[j]) + b_ref[j : j + 1, :]).astype(jnp.bfloat16)
            out = dot32(out, to_lanes)
            ref[at : at + step, :] = jnp.where(extra, fill, out).astype(jnp.bfloat16)
    scale = math.log2(math.e) / math.sqrt(HEAD_DIM)
    for at in range(0, rows, step):
        for h in range(heads):
            lanes = slice(h * LANES, (h + 1) * LANES)
            scores = lax.dot_general(
                q_ref[at : at + step, lanes],
                k_ref[:, lanes],
                (((1,), (1,)), ((), ())),
                preferred_element_type=jnp.float32,
            )
            peak = jnp.max(scores, axis=-1, keepdims=True)
            weights = jnp.exp2((scores - peak) * scale).astype(jnp.bfloat16)
            mixed = dot32(weights, v_ref[:, lanes])
            mixed = mixed / mixed[:, HEAD_DIM : HEAD_DIM + 1]
            att_ref[at : at + step, lanes] = mixed.astype(jnp.bfloat16)
    quarter = outs[0].shape[0]
    index = lax.broadcasted_iota(jnp.int32, (quarter, rows), 0)
    for k, out_ref in enumerate(outs):
        place = (index + k * quarter == dst_ref[...]).astype(jnp.bfloat16)
        moved = dot32(place, att_ref[...]).astype(jnp.bfloat16)
        packed = lax.dot_general(
            moved, to_lanes, (((1,), (1,)), ((), ())), preferred_element_type=jnp.float32
        )
        out_ref[...] = packed.astype(jnp.bfloat16)
        if k == 0:
            own_ref[...] = dot32(place, x_ref[...]).astype(jnp.bfloat16)


def vmem():
    return pl.BlockSpec(memory_space=pltpu.VMEM)


def attend(live, x, gain, w, b, dst, parts):
    rows, width = x.shape
    cols = w.shape[2]
    padded = cols // HEAD_DIM * LANES
    part_rows = rows // parts
    scratch = pltpu.VMEM((rows, padded), jnp.bfloat16)
    return pl.pallas_call(
        attend_kernel,
        out_shape=[jax.ShapeDtypeStruct((part_rows, width), jnp.bfloat16)]
        + [jax.ShapeDtypeStruct((part_rows, cols), jnp.bfloat16)] * parts,
        in_specs=[pl.BlockSpec(memory_space=pltpu.SMEM)] + [vmem()] * 5,
        out_specs=[vmem()] * (parts + 1),
        scratch_shapes=[scratch] * 4,
        compiler_params=pltpu.CompilerParams(vmem_limit_bytes=VMEM_BYTES),
        cost_estimate=pl.CostEstimate(
            flops=2 * rows * (3 * width * cols + 2 * rows * cols),
            bytes_accessed=2 * (2 * rows * width + 3 * width * cols),
            transcendentals=rows * rows * cols // HEAD_DIM,
        ),
    )(live, x, gain, w, b, dst)


def project_kernel(count, own_ref, bias_ref, gain_ref, *rest):
    blocks, weights, out_ref = rest[:count], rest[count:-1], rest[-1]
    summed = own_ref[...].astype(jnp.float32) + bias_ref[...]
    for block, weight in zip(blocks, weights):
        summed = summed + dot32(block[...], weight[...])
    out_ref[...] = rms_scale(summed, gain_ref[...]).astype(jnp.bfloat16)


def project(own, bias, gain, blocks, weights):
    rows, width = own.shape
    count = len(blocks)
    return pl.pallas_call(
        functools.partial(project_kernel, count),
        out_shape=jax.ShapeDtypeStruct((rows, width), jnp.bfloat16),
        in_specs=[vmem()] * (3 + 2 * count),
        out_specs=vmem(),
        compiler_params=pltpu.CompilerParams(vmem_limit_bytes=VMEM_BYTES),
        cost_estimate=pl.CostEstimate(
            flops=2 * rows * width * width,
            bytes_accessed=2 * width * width + 6 * rows * width,
            transcendentals=rows,
        ),
    )(own, bias, gain, *blocks, *weights)


def local(
    patches,
    grids,
    dest,
    norm_gain,
    qkv_weight,
    qkv_bias,
    proj_weight,
    proj_bias,
    merge_gain,
    w_first,
    b_first,
    w_second,
    b_second,
    text_embed,
):
    dps, tensors = lax.axis_size("dp"), lax.axis_size("tensor")
    tensor_at, dp_at = lax.axis_index("tensor"), lax.axis_index("dp")
    rows, width = patches.shape
    merged = dest.shape[1]
    seq_rows = text_embed.shape[0]
    cap = merged // dps
    part = cap // tensors

    live = grids[0, 0] * grids[0, 1]
    target = jnp.where(jnp.arange(merged, dtype=jnp.int32) < live // MERGE, dest[0], -1)
    targets = lax.all_gather(target, "dp", axis=0)
    proj_blocks = gather_xor(proj_weight, "tensor")

    shard, rank = slots(target, seq_rows, dps)
    quarter = (rank // part) ^ tensor_at
    four = jnp.arange(MERGE, dtype=jnp.int32)[None, :]
    goes = ((quarter[:, None] * MERGE + four) * dps + shard[:, None]) * part + (rank % part)[:, None]
    goes = jnp.where((target >= 0)[:, None], goes, -1).reshape(1, rows)
    own, *blocks = attend(
        live[None],
        patches,
        norm_gain[None, :],
        qkv_weight,
        qkv_bias,
        goes,
        tensors,
    )
    blocks = [swap(block, "tensor", k) if k else block for k, block in enumerate(blocks)]
    merged_in = project(own, proj_bias[None, :], merge_gain[None, :], blocks, proj_blocks)

    piece = w_first.shape[0]
    splits = width // piece
    merged_in = merged_in.reshape(MERGE, dps * part, splits, piece).transpose(0, 2, 1, 3)
    merged_in = merged_in.reshape(dps, dps * part, piece)
    near, far = [], []
    for j in range(dps):
        block = pick(merged_in, dp_at ^ j)
        if j:
            block = swap(block, "dp", j)
        near.append(block)
        far.append(swap(block, "tensor", tensors // 2))
    near = gather_low(jnp.stack(near), "tensor", tensors // 2)
    far = gather_low(jnp.stack(far), "tensor", tensors // 2)

    totals = []
    batches = min(dps, BATCHES)
    images = dps // batches
    for stream in (near, far):
        lines = jnp.stack(stream)
        if images > 1:
            lines = lines.reshape(tensors // 2, batches, images, dps * part, piece)
            lines = lines[:, :, jnp.arange(images) ^ (dp_at % images)]
        first_part = dot32(lines.reshape(-1, piece), w_first).astype(jnp.bfloat16)
        first_part = first_part.reshape(tensors // 2, batches, images * dps * part, -1)
        totals.append(line_sum(first_part, "dp"))

    columns = w_second.shape[1]
    shares = dps // tensors
    held = []
    for batch in range(batches):
        halves = []
        for total in totals:
            first_out = total[batch].astype(jnp.float32) + b_first
            hidden = jax.nn.gelu(first_out, approximate=False).astype(jnp.bfloat16)
            second_part = dot32(hidden.reshape(-1, hidden.shape[-1]), w_second).astype(jnp.bfloat16)
            second_part = second_part.reshape(tensors // 2, -1, columns)
            halves.append(scatter_low(second_part, "tensor", tensors // 2))
        block = add16(halves[0], swap(halves[1], "tensor", tensors // 2))
        held.append(block.reshape(images, dps, part, columns))
    visual = []
    for at in range(0, batches, 2):
        group = held[at : at + 2]
        group, _ = lax.optimization_barrier((group, [total[-1] for total in totals]))
        group = jnp.stack(group).reshape(-1, dps, part, columns)
        count = group.shape[0] * part
        shard_blocks = []
        for j in range(dps):
            moved = lax.dynamic_index_in_dim(group, dp_at ^ j, 1, keepdims=False)
            shard_blocks.append(swap(moved, "dp", j) if j else moved)
        shard_blocks = jnp.stack(shard_blocks).reshape(tensors, shares, count, columns)
        for k in range(tensors):
            moved = pick(shard_blocks, (tensor_at ^ k) ^ (dp_at // shares))
            moved = swap(moved, "tensor", k) if k else moved
            if shares > 1:
                moved = jnp.concatenate(
                    [pick(moved, (dp_at % shares) ^ j) for j in range(shares)], axis=-1
                )
            visual.append(moved.reshape(count, shares * columns))
    visual = jnp.concatenate(visual, axis=0)

    all_shard, all_rank = slots(targets, seq_rows, dps)
    mine = all_shard == dp_at
    slot_rows = jnp.sum(
        jnp.where(
            mine[:, None, :] & (all_rank[:, None, :] == jnp.arange(cap)[None, :, None]),
            targets[:, None, :] % seq_rows + 1,
            0,
        ),
        axis=-1,
    )
    slot_rows = slot_rows.reshape(batches // 2, images * 2, tensors, part).transpose(0, 2, 1, 3)
    slot_rows = slot_rows[:, jnp.arange(tensors) ^ tensor_at].reshape(-1) - 1
    hit = jnp.arange(seq_rows, dtype=jnp.int32)[:, None] == slot_rows[None, :]
    covered = jnp.any(hit, axis=1)
    placed = dot32(hit.astype(jnp.bfloat16), visual) + b_second
    return jnp.where(covered[:, None], placed.astype(jnp.bfloat16), text_embed)


def solution(mesh):
    in_specs = (
        P(("groups", "dp"), None),
        P(("groups", "dp"), None),
        P(("groups", "dp"), None),
        P(),
        P(None, None, "tensor"),
        P(None, "tensor"),
        P("tensor", None),
        P(),
        P(),
        P("dp", "tensor"),
        P("tensor"),
        P("tensor", "dp"),
        P("tensor"),
        P(("groups", "dp"), "tensor"),
    )
    out_specs = P(("groups", "dp"), "tensor")
    return jax.shard_map(local, mesh=mesh, in_specs=in_specs, out_specs=out_specs, check_vma=False)
```

```python
import functools
import math

import jax
import jax.numpy as jnp
from jax import lax
from jax.experimental import pallas as pl
from jax.experimental.pallas import tpu as pltpu
from jax.sharding import PartitionSpec as P

HEAD_DIM = 80
MERGE = 4
BATCHES = 4
GROUPS = ((0, 1), (2,), (3,))
LANES = 128
QUERY_ROWS = 512
VMEM_BYTES = 48 * 1024 * 1024


def rms_scale(values, gain):
    return values * lax.rsqrt(jnp.mean(values * values, axis=-1, keepdims=True) + 1e-06) * gain


def dot32(a, b):
    return jnp.dot(a, b, preferred_element_type=jnp.float32)


def dot32t(a, b):
    return lax.dot_general(a, b, (((1,), (1,)), ((), ())), preferred_element_type=jnp.float32)


def swap(x, axis, k):
    n = lax.axis_size(axis)
    return lax.ppermute(x, axis, [(a, a ^ k) for a in range(n)])


def gather_xor(x, axis):
    n = lax.axis_size(axis)
    blocks = {0: x}
    step = n // 2
    while step:
        for k in list(blocks):
            blocks[k | step] = swap(blocks[k], axis, step)
        step //= 2
    return [blocks[k] for k in range(n)]


def gather_low(x, axis, count):
    blocks = {0: x}
    step = count // 2
    while step:
        for k in list(blocks):
            blocks[k | step] = swap(blocks[k], axis, step)
        step //= 2
    return [blocks[k] for k in range(count)]


def add16(a, b):
    return (a.astype(jnp.float32) + b.astype(jnp.float32)).astype(jnp.bfloat16)


def pick(x, at):
    return lax.dynamic_index_in_dim(x, at, 0, keepdims=False)


def line_sum(parts, axis):
    n = lax.axis_size(axis)
    here = lax.axis_index(axis)
    blocks = parts[0].shape[0]
    size = n // blocks

    def chain(place, step_to):
        sent, came = [], []
        for step in range(n + blocks - 1):
            block = jnp.clip(step - place, 0, blocks - 1) ^ (here // size)
            term = jnp.stack([pick(part, block) for part in parts])
            sent.append(add16(term, came[-1]) if came else term)
            pairs = [step_to(a) for a in range(n - 1) if 0 <= step - a < blocks]
            if pairs:
                came.append(lax.ppermute(sent[-1], axis, pairs))
        return sent, came

    up, _ = chain(here, lambda a: (a, a + 1))
    _, down = chain(n - 1 - here, lambda a: (n - 1 - a, n - 2 - a))
    sums = []
    for block in range(blocks):
        below, above = up[block + n - 1], jnp.zeros_like(up[0])
        for place in range(n - 1):
            below = jnp.where(here == place, up[block + place], below)
            above = jnp.where(here == place, down[block + n - 2 - place], above)
        sums.append(below.astype(jnp.float32) + above.astype(jnp.float32))
    return sums


def slots(target, seq_rows, shards):
    shard = jnp.where(target >= 0, target // seq_rows, shards)
    same = shard[..., :, None] == shard[..., None, :]
    count = target.shape[-1]
    earlier = jnp.arange(count)[None, :] < jnp.arange(count)[:, None]
    rank = jnp.sum((same & earlier).astype(jnp.int32), axis=-1)
    return shard, rank


def attend_kernel(at_ref, x_ref, gain_ref, w_ref, b_ref, own_ref, *rest):
    outs, (n_ref, pad_ref, q_ref, k_ref, v_ref, att_ref) = rest[:-6], rest[-6:]
    rows = x_ref.shape[0]
    heads = w_ref.shape[1] // HEAD_DIM
    live, tensor_at = at_ref[0], at_ref[1]
    for j in range(3):
        for h in range(heads):
            low = h * LANES
            pad_ref[j, low : low + HEAD_DIM, :] = w_ref[j, h * HEAD_DIM : (h + 1) * HEAD_DIM, :]
            pad_ref[j, low + HEAD_DIM : low + LANES, :] = jnp.zeros(
                (LANES - HEAD_DIM, w_ref.shape[2]), jnp.bfloat16
            )
    step = min(QUERY_ROWS, rows)
    scale = math.log2(math.e) / math.sqrt(HEAD_DIM)
    extra = lax.broadcasted_iota(jnp.int32, (step, heads * LANES), 1) % LANES == HEAD_DIM
    row = lax.broadcasted_iota(jnp.int32, (step, heads * LANES), 0)
    for at in range(0, rows, step):
        span = slice(at, at + step)
        normed = rms_scale(x_ref[span, :].astype(jnp.float32), gain_ref[...])
        n_ref[span, :] = normed.astype(jnp.bfloat16)
        for j, ref in enumerate((q_ref, k_ref, v_ref)):
            out = dot32t(n_ref[span, :], pad_ref[j]) + b_ref[j : j + 1, :]
            if j == 0:
                out = out * scale
            if j == 1:
                out = jnp.where(extra & (row + at >= live), -1e30, out)
            ref[span, :] = out.astype(jnp.bfloat16)
    for at in range(0, rows, step):
        span = slice(at, at + step)
        for h in range(heads):
            lanes = slice(h * LANES, (h + 1) * LANES)
            scores = dot32t(q_ref[span, lanes], k_ref[:, lanes])
            peak = jnp.max(scores, axis=-1, keepdims=True)
            weights = jnp.exp2(scores - peak).astype(jnp.bfloat16)
            mixed = dot32(weights, v_ref[:, lanes])
            mixed = mixed[:, :HEAD_DIM] / mixed[:, HEAD_DIM : HEAD_DIM + 1]
            att_ref[span, h * HEAD_DIM : (h + 1) * HEAD_DIM] = mixed.astype(jnp.bfloat16)
    quarter = outs[0].shape[0]
    for k, out_ref in enumerate(outs):
        low = pl.multiple_of((tensor_at ^ k) * quarter, quarter)
        out_ref[...] = att_ref[pl.ds(low, quarter), :]
        if k == 0:
            own_ref[...] = x_ref[pl.ds(low, quarter), :]


def vmem():
    return pl.BlockSpec(memory_space=pltpu.VMEM)


def attend(at, x, gain, w, b, parts):
    rows, width = x.shape
    cols = w.shape[1]
    padded = cols // HEAD_DIM * LANES
    part_rows = rows // parts
    return pl.pallas_call(
        attend_kernel,
        out_shape=[jax.ShapeDtypeStruct((part_rows, width), jnp.bfloat16)]
        + [jax.ShapeDtypeStruct((part_rows, cols), jnp.bfloat16)] * parts,
        in_specs=[pl.BlockSpec(memory_space=pltpu.SMEM)] + [vmem()] * 4,
        out_specs=[vmem()] * (parts + 1),
        scratch_shapes=[
            pltpu.VMEM((rows, width), jnp.bfloat16),
            pltpu.VMEM((3, padded, width), jnp.bfloat16),
            pltpu.VMEM((rows, padded), jnp.bfloat16),
            pltpu.VMEM((rows, padded), jnp.bfloat16),
            pltpu.VMEM((rows, padded), jnp.bfloat16),
            pltpu.VMEM((rows, cols), jnp.bfloat16),
        ],
        compiler_params=pltpu.CompilerParams(vmem_limit_bytes=VMEM_BYTES),
        cost_estimate=pl.CostEstimate(
            flops=2 * rows * (3 * width * cols + 2 * rows * cols),
            bytes_accessed=2 * (2 * rows * width + 3 * width * cols),
            transcendentals=rows * rows * cols // HEAD_DIM,
        ),
    )(at, x, gain, w, b)


def project_kernel(count, at_ref, own_ref, bias_ref, gain_ref, *rest):
    blocks, weights, outs = rest[:count], rest[count : 2 * count], rest[2 * count :]
    summed = own_ref[...].astype(jnp.float32) + bias_ref[...]
    for block, weight in zip(blocks, weights):
        summed = summed + dot32(block[...], weight[...])
    merged = rms_scale(summed, gain_ref[...]).astype(jnp.bfloat16)
    rows = merged.shape[0]
    size = rows // MERGE
    out_row = lax.broadcasted_iota(jnp.int32, (rows, rows), 0)
    row = lax.broadcasted_iota(jnp.int32, (rows, rows), 1)
    sort = (row == out_row % size * MERGE + ((out_row // size) ^ at_ref[0])).astype(jnp.bfloat16)
    for k, out_ref in enumerate(outs):
        out_ref[...] = dot32(sort[k * size : (k + 1) * size, :], merged).astype(jnp.bfloat16)


def project(at, own, bias, gain, blocks, weights):
    rows, width = own.shape
    count = len(blocks)
    return pl.pallas_call(
        functools.partial(project_kernel, count),
        out_shape=[jax.ShapeDtypeStruct((rows // MERGE, width), jnp.bfloat16)] * MERGE,
        in_specs=[pl.BlockSpec(memory_space=pltpu.SMEM)] + [vmem()] * (3 + 2 * count),
        out_specs=[vmem()] * MERGE,
        compiler_params=pltpu.CompilerParams(vmem_limit_bytes=VMEM_BYTES),
        cost_estimate=pl.CostEstimate(
            flops=2 * rows * width * width,
            bytes_accessed=2 * width * width + 6 * rows * width,
            transcendentals=rows,
        ),
    )(at, own, bias, gain, *blocks, *weights)


def local(
    patches,
    grids,
    dest,
    norm_gain,
    qkv_weight,
    qkv_bias,
    proj_weight,
    proj_bias,
    merge_gain,
    w_first,
    b_first,
    w_second,
    b_second,
    text_embed,
):
    dps, tensors = lax.axis_size("dp"), lax.axis_size("tensor")
    tensor_at, dp_at = lax.axis_index("tensor"), lax.axis_index("dp")
    rows, width = patches.shape
    merged = dest.shape[1]
    seq_rows = text_embed.shape[0]
    cap = merged // dps
    part = cap // tensors

    live = grids[0, 0] * grids[0, 1]
    target = jnp.where(jnp.arange(merged, dtype=jnp.int32) < live // MERGE, dest[0], -1)
    targets = [swap(target, "dp", j) if j else target for j in range(dps)]
    proj_blocks = gather_xor(proj_weight, "tensor")

    heads = qkv_bias.shape[1] // HEAD_DIM
    bias = qkv_bias.reshape(3, heads, HEAD_DIM)
    fill = jnp.broadcast_to(jnp.array([1.0, 0.0, 1.0], jnp.float32)[:, None, None], (3, heads, 1))
    bias = jnp.concatenate([bias, fill], axis=2)
    bias = jnp.pad(bias, ((0, 0), (0, 0), (0, LANES - HEAD_DIM - 1)))
    own, *blocks = attend(
        jnp.stack([live, tensor_at]),
        patches,
        norm_gain[None, :],
        jnp.swapaxes(qkv_weight, 1, 2),
        bias.reshape(3, heads * LANES),
        tensors,
    )
    blocks = [swap(block, "tensor", k) if k else block for k, block in enumerate(blocks)]
    piece = w_first.shape[0]
    splits = width // piece
    merged_in = project(
        (dp_at // splits)[None],
        own,
        proj_bias[None, :],
        merge_gain[None, :],
        blocks,
        proj_blocks,
    )

    near, far = [], []
    for j in range(dps):
        block = merged_in[j // splits]
        if splits > 1:
            at = ((dp_at ^ j) % splits) * piece
            block = lax.dynamic_slice_in_dim(block, at, piece, 1)
        if j:
            block, far[-1] = lax.optimization_barrier((swap(block, "dp", j), far[-1]))
        near.append(block)
        far.append(swap(block, "tensor", tensors // 2))
    batches = min(dps, BATCHES)
    images = dps // batches
    totals = []
    parts = []
    for stream in (near, far):
        lines = gather_low(jnp.concatenate(stream, axis=0), "tensor", tensors // 2)
        if parts:
            lines, _ = lax.optimization_barrier((lines, parts))
        parts = []
        for line in lines:
            if images > 1:
                line = line.reshape(batches, images, -1, piece)
                line = line[:, jnp.arange(images) ^ (dp_at % images)]
            part_k = dot32(line.reshape(-1, piece), w_first).astype(jnp.bfloat16)
            parts.append(part_k.reshape(batches, images, -1, part_k.shape[1]))
        totals.append(line_sum(parts, "dp"))

    image_at = jnp.arange(dps)
    targets = jnp.stack(targets)[image_at ^ dp_at]
    shard, rank = slots(targets, seq_rows, dps)
    bits = tensors.bit_length() - 1
    reverse = [int(format(k, f"0{bits}b")[::-1], 2) for k in range(tensors)]
    quarter = jnp.array(reverse, jnp.int32)[(rank // part) ^ tensor_at]
    goes = (quarter * dps + shard) * part + rank % part
    goes = jnp.where(targets >= 0, goes, -1).reshape(dps, tensors, merged // tensors)
    goes = goes[:, jnp.arange(tensors) ^ tensor_at].reshape(dps, 1, merged)
    order = (jnp.arange(merged, dtype=jnp.int32)[None, :, None] == goes).astype(jnp.bfloat16)

    columns = w_second.shape[1]
    shares = dps // tensors
    held = []
    for batch in range(batches):
        first_out = jnp.concatenate([total[batch] for total in totals], axis=0) + b_first
        hidden = jax.nn.gelu(first_out, approximate=False).astype(jnp.bfloat16)
        hidden = hidden.transpose(1, 0, 2, 3).reshape(images, merged, -1)
        sort = order[batch * images : (batch + 1) * images]
        hidden = jnp.einsum("irj,ijh->rih", sort, hidden, preferred_element_type=jnp.float32)
        hidden = hidden.astype(jnp.bfloat16)
        half = merged // 2
        block, send = None, None
        step = 1
        while step < tensors:
            if block is None:
                send = dot32(hidden[half:].reshape(half * images, -1), w_second)
                send = swap(send.astype(jnp.bfloat16), "tensor", step)
                block = dot32(hidden[:half].reshape(half * images, -1), w_second)
            else:
                half = block.shape[0] // 2
                send = swap(block[half:], "tensor", step)
                block = block[:half]
            block = add16(block, send)
            step *= 2
        held.append(block.reshape(dps, part * images, columns))
    visual = []
    for group in GROUPS:
        members = [held[batch] for batch in group]
        members = jnp.stack(members, axis=1)
        count = len(group) * part * images
        shard_blocks = []
        for j in range(dps):
            moved = pick(members, dp_at ^ j)
            shard_blocks.append(swap(moved, "dp", j) if j else moved)
        shard_blocks = jnp.stack(shard_blocks).reshape(tensors, shares, count, columns)
        for k in range(tensors):
            moved = pick(shard_blocks, (tensor_at ^ k) ^ (dp_at // shares))
            moved = swap(moved, "tensor", k) if k else moved
            if shares > 1:
                moved = jnp.concatenate(
                    [pick(moved, (dp_at % shares) ^ j) for j in range(shares)], axis=-1
                )
            visual.append(moved.reshape(count, shares * columns))
    visual = jnp.concatenate(visual, axis=0)

    slot_rows = jnp.sum(
        jnp.where(
            (shard == dp_at)[:, None, :] & (rank[:, None, :] == jnp.arange(cap)[None, :, None]),
            targets[:, None, :] % seq_rows + 1,
            0,
        ),
        axis=-1,
    )
    slot_rows = slot_rows.reshape(batches, images, tensors, part).transpose(0, 2, 3, 1) - 1
    slot_rows = slot_rows[:, jnp.arange(tensors) ^ tensor_at]
    slot_rows = jnp.concatenate(
        [slot_rows[jnp.array(group)].transpose(1, 0, 2, 3).reshape(-1) for group in GROUPS]
    )
    hit = jnp.arange(seq_rows, dtype=jnp.int32)[:, None] == slot_rows[None, :]
    covered = jnp.any(hit, axis=1)
    placed = dot32(hit.astype(jnp.bfloat16), visual) + b_second
    return jnp.where(covered[:, None], placed.astype(jnp.bfloat16), text_embed)


def solution(mesh):
    in_specs = (
        P(("groups", "dp"), None),
        P(("groups", "dp"), None),
        P(("groups", "dp"), None),
        P(),
        P(None, None, "tensor"),
        P(None, "tensor"),
        P("tensor", None),
        P(),
        P(),
        P("dp", "tensor"),
        P("tensor"),
        P("tensor", "dp"),
        P("tensor"),
        P(("groups", "dp"), "tensor"),
    )
    out_specs = P(("groups", "dp"), "tensor")
    return jax.shard_map(local, mesh=mesh, in_specs=in_specs, out_specs=out_specs, check_vma=False)
```

```python
import functools
import math

import jax
import jax.numpy as jnp
from jax import lax
from jax.experimental import pallas as pl
from jax.experimental.pallas import tpu as pltpu
from jax.sharding import PartitionSpec as P

HEAD_DIM = 80
MERGE = 4
BATCHES = 4
GROUPS = ((0, 1), (2,), (3,))
LANES = 128
QUERY_ROWS = 512
VMEM_BYTES = 48 * 1024 * 1024


def rms_scale(values, gain):
    return values * lax.rsqrt(jnp.mean(values * values, axis=-1, keepdims=True) + 1e-06) * gain


def dot32(a, b):
    return jnp.dot(a, b, preferred_element_type=jnp.float32)


def dot32t(a, b):
    return lax.dot_general(a, b, (((1,), (1,)), ((), ())), preferred_element_type=jnp.float32)


def swap(x, axis, k):
    n = lax.axis_size(axis)
    return lax.ppermute(x, axis, [(a, a ^ k) for a in range(n)])


def gather_xor(x, axis):
    n = lax.axis_size(axis)
    blocks = {0: x}
    step = n // 2
    while step:
        for k in list(blocks):
            blocks[k | step] = swap(blocks[k], axis, step)
        step //= 2
    return [blocks[k] for k in range(n)]


def gather_low(x, axis, count):
    blocks = {0: x}
    step = count // 2
    while step:
        for k in list(blocks):
            blocks[k | step] = swap(blocks[k], axis, step)
        step //= 2
    return [blocks[k] for k in range(count)]


def add16(a, b):
    return (a.astype(jnp.float32) + b.astype(jnp.float32)).astype(jnp.bfloat16)


def pick(x, at):
    return lax.dynamic_index_in_dim(x, at, 0, keepdims=False)


def line_sum(parts, axis):
    n = lax.axis_size(axis)
    here = lax.axis_index(axis)
    blocks = parts[0].shape[0]
    size = n // blocks

    def chain(place, step_to):
        sent, came = [], []
        for step in range(n + blocks - 1):
            block = jnp.clip(step - place, 0, blocks - 1) ^ (here // size)
            term = jnp.stack([pick(part, block) for part in parts])
            sent.append(add16(term, came[-1]) if came else term)
            pairs = [step_to(a) for a in range(n - 1) if 0 <= step - a < blocks]
            if pairs:
                came.append(lax.ppermute(sent[-1], axis, pairs))
        return sent, came

    up, _ = chain(here, lambda a: (a, a + 1))
    _, down = chain(n - 1 - here, lambda a: (n - 1 - a, n - 2 - a))
    sums = []
    for block in range(blocks):
        below, above = up[block + n - 1], jnp.zeros_like(up[0])
        for place in range(n - 1):
            below = jnp.where(here == place, up[block + place], below)
            above = jnp.where(here == place, down[block + n - 2 - place], above)
        sums.append(below.astype(jnp.float32) + above.astype(jnp.float32))
    return sums


def slots(target, seq_rows, shards):
    shard = jnp.where(target >= 0, target // seq_rows, shards)
    same = shard[..., :, None] == shard[..., None, :]
    count = target.shape[-1]
    earlier = jnp.arange(count)[None, :] < jnp.arange(count)[:, None]
    rank = jnp.sum((same & earlier).astype(jnp.int32), axis=-1)
    return shard, rank


def attend_kernel(grid_ref, x_hbm, gain_ref, w_hbm, b_ref, *rest):
    outs, scratch = rest[:-10], rest[-10:]
    x_ref, w_ref, n_ref, pad_ref, bias_ref, q_ref, k_ref, v_ref, att_ref, sems = scratch
    load_w = pltpu.make_async_copy(w_hbm, w_ref, sems.at[0])
    load_x = pltpu.make_async_copy(x_hbm, x_ref, sems.at[1])
    load_w.start()
    load_x.start()
    rows = x_ref.shape[0]
    heads = w_ref.shape[1] // HEAD_DIM
    live = grid_ref[0, 0] * grid_ref[0, 1]
    tensor_at = lax.axis_index("tensor")
    lane = lax.broadcasted_iota(jnp.int32, (1, heads * LANES), 1) % LANES
    for j in range(3):
        bias_ref[j : j + 1, :] = jnp.where((lane == HEAD_DIM) & (j != 1), 1.0, 0.0)
        for h in range(heads):
            low, at = h * LANES, h * HEAD_DIM
            bias_ref[j : j + 1, low : low + HEAD_DIM] = b_ref[j : j + 1, at : at + HEAD_DIM]
            pad_ref[j, low + HEAD_DIM : low + LANES, :] = jnp.zeros(
                (LANES - HEAD_DIM, w_ref.shape[2]), jnp.bfloat16
            )
    load_w.wait()
    for j in range(3):
        for h in range(heads):
            low, at = h * LANES, h * HEAD_DIM
            pad_ref[j, low : low + HEAD_DIM, :] = w_ref[j, at : at + HEAD_DIM, :]
    load_x.wait()
    step = min(QUERY_ROWS, rows)
    scale = math.log2(math.e) / math.sqrt(HEAD_DIM)
    extra = lax.broadcasted_iota(jnp.int32, (step, heads * LANES), 1) % LANES == HEAD_DIM
    row = lax.broadcasted_iota(jnp.int32, (step, heads * LANES), 0)
    gain = gain_ref[...].reshape(1, -1)
    for at in range(0, rows, step):
        span = slice(at, at + step)
        normed = rms_scale(x_ref[span, :].astype(jnp.float32), gain)
        n_ref[span, :] = normed.astype(jnp.bfloat16)
        for j, ref in enumerate((q_ref, k_ref, v_ref)):
            out = dot32t(n_ref[span, :], pad_ref[j]) + bias_ref[j : j + 1, :]
            if j == 0:
                out = out * scale
            if j == 1:
                out = jnp.where(extra & (row + at >= live), -1e30, out)
            ref[span, :] = out.astype(jnp.bfloat16)
    for at in range(0, rows, step):
        span = slice(at, at + step)
        for h in range(heads):
            lanes = slice(h * LANES, (h + 1) * LANES)
            scores = dot32t(q_ref[span, lanes], k_ref[:, lanes])
            peak = jnp.max(scores, axis=-1, keepdims=True)
            weights = jnp.exp2(scores - peak).astype(jnp.bfloat16)
            mixed = dot32(weights, v_ref[:, lanes])
            mixed = mixed[:, :HEAD_DIM] / mixed[:, HEAD_DIM : HEAD_DIM + 1]
            att_ref[span, h * HEAD_DIM : (h + 1) * HEAD_DIM] = mixed.astype(jnp.bfloat16)
    quarter = rows // len(outs)
    stores = []
    for k, out_hbm in enumerate(outs):
        low = pl.multiple_of((tensor_at ^ k) * quarter, quarter)
        store = pltpu.make_async_copy(att_ref.at[pl.ds(low, quarter)], out_hbm, sems.at[2 + k])
        store.start()
        stores.append(store)
    for store in stores:
        store.wait()


def vmem():
    return pl.BlockSpec(memory_space=pltpu.VMEM)


def smem():
    return pl.BlockSpec(memory_space=pltpu.SMEM)


def hbm():
    return pl.BlockSpec(memory_space=pltpu.HBM)


def bf16(*shape):
    return jax.ShapeDtypeStruct(shape, jnp.bfloat16)


def bf16_scratch(*shape):
    return pltpu.VMEM(shape, jnp.bfloat16)


def attend(grids, x, gain, w, b, parts):
    rows, width = x.shape
    cols = w.shape[1]
    padded = cols // HEAD_DIM * LANES
    return pl.pallas_call(
        attend_kernel,
        out_shape=[bf16(rows // parts, cols)] * parts,
        in_specs=[smem(), hbm(), vmem(), hbm(), vmem()],
        out_specs=[hbm()] * parts,
        scratch_shapes=[
            bf16_scratch(rows, width),
            bf16_scratch(3, cols, width),
            bf16_scratch(rows, width),
            bf16_scratch(3, padded, width),
            pltpu.VMEM((8, padded), jnp.float32),
            bf16_scratch(rows, padded),
            bf16_scratch(rows, padded),
            bf16_scratch(rows, padded),
            bf16_scratch(rows, cols),
            pltpu.SemaphoreType.DMA((2 + parts,)),
        ],
        compiler_params=pltpu.CompilerParams(vmem_limit_bytes=VMEM_BYTES),
        cost_estimate=pl.CostEstimate(
            flops=2 * rows * (3 * width * cols + 2 * rows * cols),
            bytes_accessed=2 * (2 * rows * width + 3 * width * cols),
            transcendentals=rows * rows * cols // HEAD_DIM,
        ),
    )(grids, x, gain, w, b)


def project_kernel(count, splits, x_hbm, bias_ref, gain_ref, *rest):
    blocks, weights, outs = rest[:count], rest[count : 2 * count], rest[2 * count : -5]
    x_ref, block_ref, weight_ref, out_ref, sems = rest[-5:]
    rows, size = x_ref.shape[0], out_ref.shape[1]
    low = pl.multiple_of(lax.axis_index("tensor") * rows, rows)
    loads = [pltpu.make_async_copy(x_hbm.at[pl.ds(low, rows)], x_ref, sems.at[0])]
    for k in range(count):
        loads.append(pltpu.make_async_copy(blocks[k], block_ref.at[k], sems.at[1 + 2 * k]))
        loads.append(pltpu.make_async_copy(weights[k], weight_ref.at[k], sems.at[2 + 2 * k]))
    for load in loads:
        load.start()
    for load in loads:
        load.wait()
    summed = x_ref[...].astype(jnp.float32) + bias_ref[...].reshape(1, -1)
    for k in range(count):
        summed = summed + dot32(block_ref[k], weight_ref[k])
    merged = rms_scale(summed, gain_ref[...].reshape(1, -1)).astype(jnp.bfloat16)
    out_row = lax.broadcasted_iota(jnp.int32, (rows, rows), 0)
    row = lax.broadcasted_iota(jnp.int32, (rows, rows), 1)
    four = (out_row // size) ^ (lax.axis_index("dp") // splits)
    sort = (row == out_row % size * MERGE + four).astype(jnp.bfloat16)
    stores = []
    for k, out_hbm in enumerate(outs):
        out_ref[k] = dot32(sort[k * size : (k + 1) * size, :], merged).astype(jnp.bfloat16)
        store = pltpu.make_async_copy(out_ref.at[k], out_hbm, sems.at[k])
        store.start()
        stores.append(store)
    for store in stores:
        store.wait()


def project(x, bias, gain, blocks, weights, splits):
    rows, cols = blocks[0].shape
    width = x.shape[1]
    count = len(blocks)
    return pl.pallas_call(
        functools.partial(project_kernel, count, splits),
        out_shape=[bf16(rows // MERGE, width)] * MERGE,
        in_specs=[hbm(), vmem(), vmem()] + [hbm()] * (2 * count),
        out_specs=[hbm()] * MERGE,
        scratch_shapes=[
            bf16_scratch(rows, width),
            bf16_scratch(count, rows, cols),
            bf16_scratch(count, cols, width),
            bf16_scratch(MERGE, rows // MERGE, width),
            pltpu.SemaphoreType.DMA((max(MERGE, 1 + 2 * count),)),
        ],
        compiler_params=pltpu.CompilerParams(vmem_limit_bytes=VMEM_BYTES),
        cost_estimate=pl.CostEstimate(
            flops=2 * rows * width * width,
            bytes_accessed=2 * width * width + 6 * rows * width,
            transcendentals=rows,
        ),
    )(x, bias, gain, *blocks, *weights)


def second_kernel(count, bias_ref, goes_ref, w_hbm, *rest):
    totals, (send_ref, keep_ref), (w_ref, h_ref, sem) = rest[:count], rest[count:-3], rest[-3:]
    load = pltpu.make_async_copy(w_hbm, w_ref, sem)
    load.start()
    rows = totals[0].shape[0]
    bias = bias_ref[...].reshape(1, -1)
    for at, total in enumerate(totals):
        value = total[...] + bias
        value = 0.5 * value * (1.0 + lax.erf(value * math.sqrt(0.5)))
        h_ref[at * rows : (at + 1) * rows, :] = value.astype(jnp.bfloat16)
    half = send_ref.shape[0]
    index = lax.broadcasted_iota(jnp.int32, (half, 2 * half), 0)
    load.wait()
    for low, out_ref in ((half, send_ref), (0, keep_ref)):
        sort = (index + low == goes_ref[...]).astype(jnp.bfloat16)
        moved = dot32(sort, h_ref[...]).astype(jnp.bfloat16)
        out_ref[...] = dot32(moved, w_ref[...]).astype(jnp.bfloat16)


def second(totals, bias, goes, w):
    rows, width = totals[0].shape
    count = len(totals)
    out = bf16(rows * count // 2, w.shape[1])
    return pl.pallas_call(
        functools.partial(second_kernel, count),
        out_shape=[out, out],
        in_specs=[vmem(), vmem(), hbm()] + [vmem()] * count,
        out_specs=[vmem(), vmem()],
        scratch_shapes=[
            bf16_scratch(*w.shape),
            bf16_scratch(rows * count, width),
            pltpu.SemaphoreType.DMA,
        ],
        compiler_params=pltpu.CompilerParams(vmem_limit_bytes=VMEM_BYTES),
        cost_estimate=pl.CostEstimate(
            flops=2 * rows * count * width * w.shape[1],
            bytes_accessed=2 * w.shape[0] * w.shape[1],
            transcendentals=rows * count * width,
        ),
    )(bias, goes, w, *totals)


def local(
    patches,
    grids,
    dest,
    norm_gain,
    qkv_weight,
    qkv_bias,
    proj_weight,
    proj_bias,
    merge_gain,
    w_first,
    b_first,
    w_second,
    b_second,
    text_embed,
):
    dps, tensors = lax.axis_size("dp"), lax.axis_size("tensor")
    tensor_at, dp_at = lax.axis_index("tensor"), lax.axis_index("dp")
    rows, width = patches.shape
    merged = dest.shape[1]
    seq_rows = text_embed.shape[0]
    cap = merged // dps
    part = cap // tensors

    proj_blocks = gather_xor(proj_weight, "tensor")
    blocks = attend(
        grids, patches, norm_gain, jnp.swapaxes(qkv_weight, 1, 2), qkv_bias, tensors
    )
    blocks = [swap(block, "tensor", k) if k else block for k, block in enumerate(blocks)]
    piece = w_first.shape[0]
    splits = width // piece
    merged_in = project(patches, proj_bias, merge_gain, blocks, proj_blocks, splits)

    near, far = [], []
    for j in range(dps):
        block = merged_in[j // splits]
        if splits > 1:
            at = ((dp_at ^ j) % splits) * piece
            block = lax.dynamic_slice_in_dim(block, at, piece, 1)
        if j:
            block = swap(block, "dp", j)
        if 0 < j < dps - 1:
            block, far[-1] = lax.optimization_barrier((block, far[-1]))
        near.append(block)
        far.append(swap(block, "tensor", tensors // 2))
    batches = min(dps, BATCHES)
    images = dps // batches
    totals = []
    parts = []
    for stream in (near, far):
        lines = gather_low(jnp.concatenate(stream, axis=0), "tensor", tensors // 2)
        if parts:
            lines, _ = lax.optimization_barrier((lines, parts))
        parts = []
        for line in lines:
            if images > 1:
                line = line.reshape(batches, images, -1, piece)
                line = line[:, jnp.arange(images) ^ (dp_at % images)]
            part_k = dot32(line.reshape(-1, piece), w_first).astype(jnp.bfloat16)
            parts.append(part_k.reshape(batches, images, -1, part_k.shape[1]))
        totals.append(line_sum(parts, "dp"))

    grids, dest, _ = lax.optimization_barrier((grids, dest, near[-1]))
    live = grids[0, 0] * grids[0, 1]
    target = jnp.where(jnp.arange(merged, dtype=jnp.int32) < live // MERGE, dest[0], -1)
    targets = jnp.stack([swap(target, "dp", j) if j else target for j in range(dps)])
    targets = targets[jnp.arange(dps) ^ dp_at]
    shard, rank = slots(targets, seq_rows, dps)
    quarter = (rank // part) ^ tensor_at
    bits = tensors.bit_length() - 1
    quarter = sum(((quarter >> k) & 1) << (bits - 1 - k) for k in range(bits))
    goes = (quarter * dps + shard) * part + rank % part
    image = jnp.arange(dps)[:, None] % images
    goes = jnp.where(targets >= 0, goes * images + image, -1)
    goes = goes.reshape(batches, images, tensors, merged // tensors).transpose(0, 2, 1, 3)
    goes = goes[:, jnp.arange(tensors) ^ tensor_at].reshape(batches, 1, images * merged)

    columns = w_second.shape[1]
    shares = dps // tensors
    held = []
    for batch in range(batches):
        rows_in = [total[batch].reshape(-1, w_second.shape[0]) for total in totals]
        send, block = second(rows_in, b_first, goes[batch], w_second)
        block = add16(block, swap(send, "tensor", 1))
        step = 2
        while step < tensors:
            half = block.shape[0] // 2
            block = add16(block[:half], swap(block[half:], "tensor", step))
            step *= 2
        held.append(block.reshape(dps, part * images, columns))
    visual = []
    for group in GROUPS:
        members = [held[batch] for batch in group]
        members = jnp.stack(members, axis=1)
        count = len(group) * part * images
        shard_blocks = []
        for j in range(dps):
            moved = pick(members, dp_at ^ j)
            shard_blocks.append(swap(moved, "dp", j) if j else moved)
        shard_blocks = jnp.stack(shard_blocks).reshape(tensors, shares, count, columns)
        for k in range(tensors):
            moved = pick(shard_blocks, (tensor_at ^ k) ^ (dp_at // shares))
            moved = swap(moved, "tensor", k) if k else moved
            if shares > 1:
                moved = jnp.concatenate(
                    [pick(moved, (dp_at % shares) ^ j) for j in range(shares)], axis=-1
                )
            visual.append(moved.reshape(count, shares * columns))
    visual = jnp.concatenate(visual, axis=0)

    slot_rows = jnp.sum(
        jnp.where(
            (shard == dp_at)[:, None, :] & (rank[:, None, :] == jnp.arange(cap)[None, :, None]),
            targets[:, None, :] % seq_rows + 1,
            0,
        ),
        axis=-1,
    )
    slot_rows = slot_rows.reshape(batches, images, tensors, part).transpose(0, 2, 3, 1) - 1
    slot_rows = slot_rows[:, jnp.arange(tensors) ^ tensor_at]
    slot_rows = jnp.concatenate(
        [slot_rows[jnp.array(group)].transpose(1, 0, 2, 3).reshape(-1) for group in GROUPS]
    )
    hit = jnp.arange(seq_rows, dtype=jnp.int32)[:, None] == slot_rows[None, :]
    covered = jnp.any(hit, axis=1)
    placed = dot32(hit.astype(jnp.bfloat16), visual) + b_second
    return jnp.where(covered[:, None], placed.astype(jnp.bfloat16), text_embed)


def solution(mesh):
    in_specs = (
        P(("groups", "dp"), None),
        P(("groups", "dp"), None),
        P(("groups", "dp"), None),
        P(),
        P(None, None, "tensor"),
        P(None, "tensor"),
        P("tensor", None),
        P(),
        P(),
        P("dp", "tensor"),
        P("tensor"),
        P("tensor", "dp"),
        P("tensor"),
        P(("groups", "dp"), "tensor"),
    )
    out_specs = P(("groups", "dp"), "tensor")
    return jax.shard_map(local, mesh=mesh, in_specs=in_specs, out_specs=out_specs, check_vma=False)
```

```python
import functools
import math

import jax
import jax.numpy as jnp
from jax import lax
from jax.experimental import pallas as pl
from jax.experimental.pallas import tpu as pltpu
from jax.sharding import PartitionSpec as P

HEAD_DIM = 80
MERGE = 4
BATCHES = 4
LEAD = 2
GROUPS = ((0, 1), (2,), (3,))
LANES = 128
QUERY_ROWS = 512
VMEM_BYTES = 48 * 1024 * 1024
ATTEND_VMEM_BYTES = 60 * 1024 * 1024


def rms_scale(values, gain):
    return values * lax.rsqrt(jnp.mean(values * values, axis=-1, keepdims=True) + 1e-06) * gain


def dot32(a, b):
    return jnp.dot(a, b, preferred_element_type=jnp.float32)


def dot32t(a, b):
    return lax.dot_general(a, b, (((1,), (1,)), ((), ())), preferred_element_type=jnp.float32)


def swap(x, axis, k):
    n = lax.axis_size(axis)
    return lax.ppermute(x, axis, [(a, a ^ k) for a in range(n)])


def gather_low(x, axis, count):
    blocks = {0: x}
    step = count // 2
    while step:
        for k in list(blocks):
            blocks[k | step] = swap(blocks[k], axis, step)
        step //= 2
    return [blocks[k] for k in range(count)]


def add16(a, b):
    return (a.astype(jnp.float32) + b.astype(jnp.float32)).astype(jnp.bfloat16)


def pick(x, at):
    return lax.dynamic_index_in_dim(x, at, 0, keepdims=False)


def line_sums(streams, axis, prepare, finish):
    n = lax.axis_size(axis)
    here = lax.axis_index(axis)
    terms = [streams[0](None)]
    blocks = terms[0][0].shape[0]
    size = n // blocks
    ways = (
        (here, lambda a: (a, a + 1)),
        (n - 1 - here, lambda a: (n - 1 - a, n - 2 - a)),
    )
    sent = [[[] for _ in ways] for _ in streams]
    came = [[[] for _ in ways] for _ in streams]
    results = []
    for step in range(n + blocks - 1):
        for s in range(len(streams)):
            if s == len(terms):
                terms.append(streams[s](came[s - 1][0][0]))
            parts = terms[s]
            for w, (place, step_to) in enumerate(ways):
                block = jnp.clip(step - place, 0, blocks - 1) ^ (here // size)
                term = jnp.stack([pick(part, block) for part in parts])
                value = add16(term, came[s][w][-1]) if step else term
                sent[s][w].append(value)
                if s == 0 and step >= LEAD:
                    value, _ = lax.optimization_barrier((value, sent[-1][w][step - LEAD]))
                if s == len(streams) - 1 and w == 0 and step == n + blocks - 3:
                    early = results[: blocks - 2]
                    value, results[: blocks - 2] = lax.optimization_barrier((value, early))
                pairs = [step_to(a) for a in range(n - 1) if 0 <= step - a < blocks]
                if pairs:
                    came[s][w].append(lax.ppermute(value, axis, pairs))
        if step == 1:
            prepared = prepare(came[-1][0][0])
        done = step - (n - 1)
        if done >= 0:
            sums = []
            for s in range(len(streams)):
                up, down = sent[s][0], came[s][1]
                below, above = up[done + n - 1], jnp.zeros_like(up[0])
                for place in range(n - 1):
                    below = jnp.where(here == place, up[done + place], below)
                    above = jnp.where(here == place, down[done + n - 2 - place], above)
                sums.append(below.astype(jnp.float32) + above.astype(jnp.float32))
            results.append(finish(done, sums, prepared))
    return results


def slots(target, seq_rows, shards):
    shard = jnp.where(target >= 0, target // seq_rows, shards)
    same = shard[..., :, None] == shard[..., None, :]
    count = target.shape[-1]
    earlier = jnp.arange(count)[None, :] < jnp.arange(count)[:, None]
    rank = jnp.sum((same & earlier).astype(jnp.int32), axis=-1)
    return shard, rank


def attend_kernel(grid_ref, x_hbm, gain_ref, w_hbm, b_ref, *rest):
    outs, scratch = rest[:-10], rest[-10:]
    x_ref, w_ref, n_ref, pad_ref, bias_ref, q_ref, k_ref, v_ref, att_ref, sems = scratch
    load_w = pltpu.make_async_copy(w_hbm, w_ref, sems.at[0])
    load_x = pltpu.make_async_copy(x_hbm, x_ref, sems.at[1])
    load_w.start()
    load_x.start()
    rows = x_ref.shape[0]
    heads = w_ref.shape[1] // HEAD_DIM
    live = grid_ref[0, 0] * grid_ref[0, 1]
    tensor_at = lax.axis_index("tensor")
    lane = lax.broadcasted_iota(jnp.int32, (1, heads * LANES), 1) % LANES
    for j in range(3):
        bias_ref[j : j + 1, :] = jnp.where((lane == HEAD_DIM) & (j != 1), 1.0, 0.0)
        for h in range(heads):
            low, at = h * LANES, h * HEAD_DIM
            bias_ref[j : j + 1, low : low + HEAD_DIM] = b_ref[j : j + 1, at : at + HEAD_DIM]
            pad_ref[j, low + HEAD_DIM : low + LANES, :] = jnp.zeros(
                (LANES - HEAD_DIM, w_ref.shape[2]), jnp.bfloat16
            )
    load_w.wait()
    for j in range(3):
        for h in range(heads):
            low, at = h * LANES, h * HEAD_DIM
            pad_ref[j, low : low + HEAD_DIM, :] = w_ref[j, at : at + HEAD_DIM, :]
    load_x.wait()
    step = min(QUERY_ROWS, rows)
    scale = math.log2(math.e) / math.sqrt(HEAD_DIM)
    extra = lax.broadcasted_iota(jnp.int32, (step, heads * LANES), 1) % LANES == HEAD_DIM
    row = lax.broadcasted_iota(jnp.int32, (step, heads * LANES), 0)
    gain = gain_ref[...].reshape(1, -1)
    for at in range(0, rows, step):
        span = slice(at, at + step)
        normed = rms_scale(x_ref[span, :].astype(jnp.float32), gain)
        n_ref[span, :] = normed.astype(jnp.bfloat16)
        for j, ref in enumerate((q_ref, k_ref, v_ref)):
            out = dot32t(n_ref[span, :], pad_ref[j]) + bias_ref[j : j + 1, :]
            if j == 0:
                out = out * scale
            if j == 1:
                out = jnp.where(extra & (row + at >= live), -1e30, out)
            ref[span, :] = out.astype(jnp.bfloat16)
    for at in range(0, rows, step):
        span = slice(at, at + step)
        for h in range(heads):
            lanes = slice(h * LANES, (h + 1) * LANES)
            scores = dot32t(q_ref[span, lanes], k_ref[:, lanes])
            peak = jnp.max(scores, axis=-1, keepdims=True)
            weights = jnp.exp2(scores - peak).astype(jnp.bfloat16)
            mixed = dot32(weights, v_ref[:, lanes])
            mixed = mixed[:, :HEAD_DIM] / mixed[:, HEAD_DIM : HEAD_DIM + 1]
            att_ref[span, h * HEAD_DIM : (h + 1) * HEAD_DIM] = mixed.astype(jnp.bfloat16)
    quarter = rows // len(outs)
    stores = []
    for k, out_hbm in enumerate(outs):
        low = pl.multiple_of((tensor_at ^ k) * quarter, quarter)
        store = pltpu.make_async_copy(att_ref.at[pl.ds(low, quarter)], out_hbm, sems.at[2 + k])
        store.start()
        stores.append(store)
    for store in stores:
        store.wait()


def vmem():
    return pl.BlockSpec(memory_space=pltpu.VMEM)


def smem():
    return pl.BlockSpec(memory_space=pltpu.SMEM)


def hbm():
    return pl.BlockSpec(memory_space=pltpu.HBM)


def anywhere():
    return pl.BlockSpec(memory_space=pl.ANY)


def bf16(*shape):
    return jax.ShapeDtypeStruct(shape, jnp.bfloat16)


def bf16_scratch(*shape):
    return pltpu.VMEM(shape, jnp.bfloat16)


def attend(grids, x, gain, w, b, parts):
    rows, width = x.shape
    cols = w.shape[1]
    padded = cols // HEAD_DIM * LANES
    return pl.pallas_call(
        attend_kernel,
        out_shape=[bf16(rows // parts, cols)] * parts,
        in_specs=[smem(), anywhere(), vmem(), anywhere(), vmem()],
        out_specs=[hbm()] * parts,
        scratch_shapes=[
            bf16_scratch(rows, width),
            bf16_scratch(3, cols, width),
            bf16_scratch(rows, width),
            bf16_scratch(3, padded, width),
            pltpu.VMEM((8, padded), jnp.float32),
            bf16_scratch(rows, padded),
            bf16_scratch(rows, padded),
            bf16_scratch(rows, padded),
            bf16_scratch(rows, cols),
            pltpu.SemaphoreType.DMA((2 + parts,)),
        ],
        compiler_params=pltpu.CompilerParams(vmem_limit_bytes=ATTEND_VMEM_BYTES),
        cost_estimate=pl.CostEstimate(
            flops=2 * rows * (3 * width * cols + 2 * rows * cols),
            bytes_accessed=2 * (2 * rows * width + 3 * width * cols),
            transcendentals=rows * rows * cols // HEAD_DIM,
        ),
    )(grids, x, gain, w, b)


def project_kernel(count, splits, x_hbm, bias_ref, gain_ref, *rest):
    blocks, weights, outs = rest[:count], rest[count : 2 * count], rest[2 * count : -5]
    x_ref, block_ref, weight_ref, out_ref, sems = rest[-5:]
    rows, size = x_ref.shape[0], out_ref.shape[1]
    low = pl.multiple_of(lax.axis_index("tensor") * rows, rows)
    loads = [pltpu.make_async_copy(x_hbm.at[pl.ds(low, rows)], x_ref, sems.at[0])]
    for k in range(count):
        loads.append(pltpu.make_async_copy(blocks[k], block_ref.at[k], sems.at[1 + 2 * k]))
        loads.append(pltpu.make_async_copy(weights[k], weight_ref.at[k], sems.at[2 + 2 * k]))
    for load in loads:
        load.start()
    loads[0].wait()
    summed = x_ref[...].astype(jnp.float32) + bias_ref[...].reshape(1, -1)
    for k in range(count):
        loads[1 + 2 * k].wait()
        loads[2 + 2 * k].wait()
        summed = summed + dot32(block_ref[k], weight_ref[k])
    merged = rms_scale(summed, gain_ref[...].reshape(1, -1)).astype(jnp.bfloat16)
    out_row = lax.broadcasted_iota(jnp.int32, (rows, rows), 0)
    row = lax.broadcasted_iota(jnp.int32, (rows, rows), 1)
    four = (out_row // size) ^ (lax.axis_index("dp") // splits)
    sort = (row == out_row % size * MERGE + four).astype(jnp.bfloat16)
    stores = []
    for k, out_hbm in enumerate(outs):
        out_ref[k] = dot32(sort[k * size : (k + 1) * size, :], merged).astype(jnp.bfloat16)
        store = pltpu.make_async_copy(out_ref.at[k], out_hbm, sems.at[k])
        store.start()
        stores.append(store)
    for store in stores:
        store.wait()


def project(x, bias, gain, blocks, weights, splits):
    rows, cols = blocks[0].shape
    width = x.shape[1]
    count = len(blocks)
    return pl.pallas_call(
        functools.partial(project_kernel, count, splits),
        out_shape=[bf16(rows // MERGE, width)] * MERGE,
        in_specs=[anywhere(), vmem(), vmem()] + [anywhere()] * (2 * count),
        out_specs=[hbm()] * MERGE,
        scratch_shapes=[
            bf16_scratch(rows, width),
            bf16_scratch(count, rows, cols),
            bf16_scratch(count, cols, width),
            bf16_scratch(MERGE, rows // MERGE, width),
            pltpu.SemaphoreType.DMA((max(MERGE, 1 + 2 * count),)),
        ],
        compiler_params=pltpu.CompilerParams(vmem_limit_bytes=VMEM_BYTES),
        cost_estimate=pl.CostEstimate(
            flops=2 * rows * width * width,
            bytes_accessed=2 * width * width + 6 * rows * width,
            transcendentals=rows,
        ),
    )(x, bias, gain, *blocks, *weights)


def first_kernel(count, w_ref, *rest):
    blocks, (out_ref, cat_hbm), (cat_ref, sems) = rest[:count], rest[count:-2], rest[-2:]
    rows = cat_ref.shape[0] // count
    loads = []
    for k, block in enumerate(blocks):
        place = cat_ref.at[k * rows : (k + 1) * rows]
        loads.append(pltpu.make_async_copy(block, place, sems.at[k]))
        loads[-1].start()
    for load in loads:
        load.wait()
    store = pltpu.make_async_copy(cat_ref, cat_hbm, sems.at[0])
    store.start()
    out_ref[...] = dot32(cat_ref[...], w_ref[...]).astype(jnp.bfloat16)
    store.wait()


def first(blocks, w):
    count = len(blocks)
    rows, depth = blocks[0].shape
    rows = rows * count
    return pl.pallas_call(
        functools.partial(first_kernel, count),
        out_shape=[bf16(rows, w.shape[1]), bf16(rows, depth)],
        in_specs=[vmem()] + [anywhere()] * count,
        out_specs=[vmem(), hbm()],
        scratch_shapes=[bf16_scratch(rows, depth), pltpu.SemaphoreType.DMA((count,))],
        compiler_params=pltpu.CompilerParams(vmem_limit_bytes=VMEM_BYTES // 2),
        cost_estimate=pl.CostEstimate(
            flops=2 * rows * depth * w.shape[1],
            bytes_accessed=2 * depth * w.shape[1] + 6 * rows * depth,
            transcendentals=0,
        ),
    )(w, *blocks)


def second_kernel(count, bias_ref, goes_ref, w_hbm, *rest):
    totals, (send_ref, keep_ref), (w_ref, h_ref, sem) = rest[:count], rest[count:-3], rest[-3:]
    load = pltpu.make_async_copy(w_hbm, w_ref, sem)
    load.start()
    rows = totals[0].shape[0]
    bias = bias_ref[...].reshape(1, -1)
    for at, total in enumerate(totals):
        value = total[...] + bias
        value = 0.5 * value * (1.0 + lax.erf(value * math.sqrt(0.5)))
        h_ref[at * rows : (at + 1) * rows, :] = value.astype(jnp.bfloat16)
    half = send_ref.shape[0]
    index = lax.broadcasted_iota(jnp.int32, (half, 2 * half), 0)
    load.wait()
    for low, out_ref in ((half, send_ref), (0, keep_ref)):
        sort = (index + low == goes_ref[...]).astype(jnp.bfloat16)
        moved = dot32(sort, h_ref[...]).astype(jnp.bfloat16)
        out_ref[...] = dot32(moved, w_ref[...]).astype(jnp.bfloat16)


def second(totals, bias, goes, w):
    rows, width = totals[0].shape
    count = len(totals)
    out = bf16(rows * count // 2, w.shape[1])
    return pl.pallas_call(
        functools.partial(second_kernel, count),
        out_shape=[out, out],
        in_specs=[vmem(), vmem(), anywhere()] + [vmem()] * count,
        out_specs=[vmem(), vmem()],
        scratch_shapes=[
            bf16_scratch(*w.shape),
            bf16_scratch(rows * count, width),
            pltpu.SemaphoreType.DMA,
        ],
        compiler_params=pltpu.CompilerParams(vmem_limit_bytes=VMEM_BYTES),
        cost_estimate=pl.CostEstimate(
            flops=2 * rows * count * width * w.shape[1],
            bytes_accessed=2 * w.shape[0] * w.shape[1],
            transcendentals=rows * count * width,
        ),
    )(bias, goes, w, *totals)


def local(
    patches,
    grids,
    dest,
    norm_gain,
    qkv_weight,
    qkv_bias,
    proj_weight,
    proj_bias,
    merge_gain,
    w_first,
    b_first,
    w_second,
    b_second,
    text_embed,
):
    dps, tensors = lax.axis_size("dp"), lax.axis_size("tensor")
    tensor_at, dp_at = lax.axis_index("tensor"), lax.axis_index("dp")
    rows, width = patches.shape
    merged = dest.shape[1]
    seq_rows = text_embed.shape[0]
    cap = merged // dps
    part = cap // tensors

    proj_high = {0: proj_weight, tensors // 2: swap(proj_weight, "tensor", tensors // 2)}
    blocks = attend(
        grids, patches, norm_gain, jnp.swapaxes(qkv_weight, 1, 2), qkv_bias, tensors
    )
    blocks, proj_high = lax.optimization_barrier((list(blocks), proj_high))
    proj_blocks = {}
    for k, high in proj_high.items():
        for j, block in enumerate(gather_low(high, "tensor", tensors // 2)):
            proj_blocks[k | j] = block
    proj_blocks = [proj_blocks[k] for k in range(tensors)]
    blocks = [swap(block, "tensor", k) if k else block for k, block in enumerate(blocks)]
    piece = w_first.shape[0]
    splits = width // piece
    merged_in = project(patches, proj_bias, merge_gain, blocks, proj_blocks, splits)

    near, far = [], []
    for j in range(dps):
        block = merged_in[j // splits]
        if splits > 1:
            at = ((dp_at ^ j) % splits) * piece
            block = lax.dynamic_slice_in_dim(block, at, piece, 1)
        if j:
            block = swap(block, "dp", j)
        if 0 < j < dps - 1:
            block, far[-1] = lax.optimization_barrier((block, far[-1]))
        near.append(block)
        far.append(swap(block, "tensor", tensors // 2))
    batches = min(dps, BATCHES)
    images = dps // batches

    def product(stream, after):
        if after is not None:
            stream, _ = lax.optimization_barrier((stream, after))
        if images > 1:
            stream = [
                pick(jnp.stack(stream).reshape(batches, images, -1, piece)[k // images], at)
                for k, at in enumerate([j % images ^ (dp_at % images) for j in range(dps)])
            ]
        part_0, joined = first(stream, w_first)
        parts = [part_0]
        for line in gather_low(joined, "tensor", tensors // 2)[1:]:
            parts.append(dot32(line, w_first).astype(jnp.bfloat16))
        return [part.reshape(batches, images, -1, part.shape[1]) for part in parts]

    def places(after):
        (sides, rows_to), _ = lax.optimization_barrier(((grids, dest), after))
        live = sides[0, 0] * sides[0, 1]
        target = jnp.where(jnp.arange(merged, dtype=jnp.int32) * MERGE < live, rows_to[0], -1)
        targets = jnp.stack([swap(target, "dp", j) if j else target for j in range(dps)])
        targets = targets[jnp.arange(dps) ^ dp_at]
        shard, rank = slots(targets, seq_rows, dps)
        quarter = (rank // part) ^ tensor_at
        bits = tensors.bit_length() - 1
        quarter = sum(((quarter >> k) & 1) << (bits - 1 - k) for k in range(bits))
        goes = (quarter * dps + shard) * part + rank % part
        image = jnp.arange(dps)[:, None] % images
        goes = jnp.where(targets >= 0, goes * images + image, -1)
        goes = goes.reshape(batches, images, tensors, merged // tensors).transpose(0, 2, 1, 3)
        goes = goes[:, jnp.arange(tensors) ^ tensor_at].reshape(batches, 1, images * merged)
        slot_rows = jnp.sum(
            jnp.where(
                (shard == dp_at)[:, None, :]
                & (rank[:, None, :] == jnp.arange(cap)[None, :, None]),
                targets[:, None, :] % seq_rows + 1,
                0,
            ),
            axis=-1,
        )
        slot_rows = slot_rows.reshape(batches, images, tensors, part).transpose(2, 0, 3, 1) - 1
        slot_rows = slot_rows[jnp.arange(tensors) ^ tensor_at].reshape(1, -1)
        rows_out = jnp.arange(seq_rows, dtype=jnp.int32)[:, None]
        return goes, (rows_out == slot_rows).astype(jnp.bfloat16)

    columns = w_second.shape[1]
    shares = dps // tensors

    def finish(batch, sums, prepared):
        rows_in = [part.reshape(-1, w_second.shape[0]) for part in sums]
        send, block = second(rows_in, b_first, prepared[0][batch], w_second)
        block = add16(block, swap(send, "tensor", 1))
        step = 2
        while step < tensors:
            half = block.shape[0] // 2
            block = add16(block[:half], swap(block[half:], "tensor", step))
            step *= 2
        return block.reshape(dps, part * images, columns), prepared[1]

    streams = [functools.partial(product, near), functools.partial(product, far)]
    held = line_sums(streams, "dp", places, finish)
    hit = held[0][1]
    arrived = []
    for group in GROUPS:
        members = jnp.stack([held[batch][0] for batch in group], axis=1)
        blocks = []
        for j in range(dps):
            moved = pick(members, dp_at ^ j)
            blocks.append(swap(moved, "dp", j) if j else moved)
        arrived.append(jnp.stack(blocks))
    arrived = jnp.concatenate(arrived, axis=1).reshape(tensors, shares, -1, columns)
    visual = []
    for k in range(tensors):
        moved = pick(arrived, (tensor_at ^ k) ^ (dp_at // shares))
        moved = swap(moved, "tensor", k) if k else moved
        if shares > 1:
            moved = jnp.concatenate(
                [pick(moved, (dp_at % shares) ^ j) for j in range(shares)], axis=-1
            )
        visual.append(moved.reshape(-1, shares * columns))
    visual = jnp.concatenate(visual, axis=0)

    covered = jnp.sum(hit, axis=1, keepdims=True, dtype=jnp.float32) > 0
    placed = dot32(hit, visual) + b_second
    return jnp.where(covered, placed.astype(jnp.bfloat16), text_embed)


def solution(mesh):
    in_specs = (
        P(("groups", "dp"), None),
        P(("groups", "dp"), None),
        P(("groups", "dp"), None),
        P(),
        P(None, None, "tensor"),
        P(None, "tensor"),
        P("tensor", None),
        P(),
        P(),
        P("dp", "tensor"),
        P("tensor"),
        P("tensor", "dp"),
        P("tensor"),
        P(("groups", "dp"), "tensor"),
    )
    out_specs = P(("groups", "dp"), "tensor")
    return jax.shard_map(local, mesh=mesh, in_specs=in_specs, out_specs=out_specs, check_vma=False)
```

```python
import functools
import math

import jax
import jax.numpy as jnp
from jax import lax
from jax.experimental import pallas as pl
from jax.experimental.pallas import tpu as pltpu
from jax.sharding import PartitionSpec as P

HEAD_DIM = 80
MERGE = 4
BATCHES = 4
LANES = 128
QUERY_ROWS = 512
VMEM_BYTES = 48 * 1024 * 1024
ATTEND_VMEM_BYTES = 60 * 1024 * 1024


def rms_scale(values, gain):
    return values * lax.rsqrt(jnp.mean(values * values, axis=-1, keepdims=True) + 1e-06) * gain


def dot32(a, b):
    return jnp.dot(a, b, preferred_element_type=jnp.float32)


def dot32t(a, b):
    return lax.dot_general(a, b, (((1,), (1,)), ((), ())), preferred_element_type=jnp.float32)


def swap(x, axis, k):
    n = lax.axis_size(axis)
    return lax.ppermute(x, axis, [(a, a ^ k) for a in range(n)])


def gather_low(x, axis, count):
    blocks = {0: x}
    step = count // 2
    while step:
        for k in list(blocks):
            blocks[k | step] = swap(blocks[k], axis, step)
        step //= 2
    return [blocks[k] for k in range(count)]


def add16(a, b):
    return (a.astype(jnp.float32) + b.astype(jnp.float32)).astype(jnp.bfloat16)


def pick(x, at):
    return lax.dynamic_index_in_dim(x, at, 0, keepdims=False)


def line_sums(streams, axis, finish):
    n = lax.axis_size(axis)
    here = lax.axis_index(axis)
    blocks = streams[0][0].shape[0]
    steps = ((lambda a: (a, a + 1)), (lambda a: (n - 1 - a, n - 2 - a)))
    sent = [[[] for _ in steps] for _ in streams]
    came = [[[] for _ in steps] for _ in streams]
    results, waits = [], {}
    for step in range(n + blocks - 1):
        for s, terms in enumerate(streams):
            for w, step_to in enumerate(steps):
                value = terms[w][step % blocks]
                if step:
                    value = add16(value, came[s][w][-1])
                sent[s][w].append(value)
                if s and step in waits:
                    value, _ = lax.optimization_barrier((value, waits[step]))
                pairs = [step_to(a) for a in range(n - 1) if 0 <= step - a < blocks]
                if pairs:
                    came[s][w].append(lax.ppermute(value, axis, pairs))
        done = step - (n - 1)
        if done >= 0:
            sums = []
            for s in range(len(streams)):
                up, down = sent[s][0], came[s][1]
                below, above = up[done + n - 1], jnp.zeros_like(up[0])
                for place in range(n - 1):
                    below = jnp.where(here == place, up[done + place], below)
                    above = jnp.where(here == place, down[done + n - 2 - place], above)
                sums.append(below.astype(jnp.float32) + above.astype(jnp.float32))
            after = came[0][0][done + n - 1] if done + n - 1 < len(came[0][0]) else None
            waits[done + n], result = finish(done, sums, after, results)
            results.append(result)
    return results


def slots(target, seq_rows, shards, each):
    shard = jnp.where(target >= 0, target // seq_rows, shards)
    same = shard[..., :, None] == shard[..., None, :]
    earlier = each[None, :] < each[:, None]
    rank = jnp.sum((same & earlier).astype(jnp.int32), axis=-1)
    return shard, rank


def attend_kernel(grid_ref, x_hbm, gain_ref, w_hbm, b_ref, *rest):
    outs, scratch = rest[:-10], rest[-10:]
    x_ref, w_ref, n_ref, pad_ref, bias_ref, q_ref, k_ref, v_ref, att_ref, sems = scratch
    load_w = pltpu.make_async_copy(w_hbm, w_ref, sems.at[0])
    load_x = pltpu.make_async_copy(x_hbm, x_ref, sems.at[1])
    load_w.start()
    load_x.start()
    rows = x_ref.shape[0]
    heads = w_ref.shape[1] // HEAD_DIM
    live = grid_ref[0, 0] * grid_ref[0, 1]
    tensor_at = lax.axis_index("tensor")
    lane = lax.broadcasted_iota(jnp.int32, (1, heads * LANES), 1) % LANES
    for j in range(3):
        bias_ref[j : j + 1, :] = jnp.where((lane == HEAD_DIM) & (j != 1), 1.0, 0.0)
        for h in range(heads):
            low, at = h * LANES, h * HEAD_DIM
            bias_ref[j : j + 1, low : low + HEAD_DIM] = b_ref[j : j + 1, at : at + HEAD_DIM]
            pad_ref[j, low + HEAD_DIM : low + LANES, :] = jnp.zeros(
                (LANES - HEAD_DIM, w_ref.shape[2]), jnp.bfloat16
            )
    load_w.wait()
    for j in range(3):
        for h in range(heads):
            low, at = h * LANES, h * HEAD_DIM
            pad_ref[j, low : low + HEAD_DIM, :] = w_ref[j, at : at + HEAD_DIM, :]
    load_x.wait()
    step = min(QUERY_ROWS, rows)
    scale = math.log2(math.e) / math.sqrt(HEAD_DIM)
    extra = lax.broadcasted_iota(jnp.int32, (step, heads * LANES), 1) % LANES == HEAD_DIM
    row = lax.broadcasted_iota(jnp.int32, (step, heads * LANES), 0)
    gain = gain_ref[...].reshape(1, -1)
    for at in range(0, rows, step):
        span = slice(at, at + step)
        normed = rms_scale(x_ref[span, :].astype(jnp.float32), gain)
        n_ref[span, :] = normed.astype(jnp.bfloat16)
        for j, ref in enumerate((q_ref, k_ref, v_ref)):
            out = dot32t(n_ref[span, :], pad_ref[j]) + bias_ref[j : j + 1, :]
            if j == 0:
                out = out * scale
            if j == 1:
                out = jnp.where(extra & (row + at >= live), -1e30, out)
            ref[span, :] = out.astype(jnp.bfloat16)
    for at in range(0, rows, step):
        span = slice(at, at + step)
        for h in range(heads):
            lanes = slice(h * LANES, (h + 1) * LANES)
            scores = dot32t(q_ref[span, lanes], k_ref[:, lanes])
            peak = jnp.max(scores, axis=-1, keepdims=True)
            weights = jnp.exp2(scores - peak).astype(jnp.bfloat16)
            mixed = dot32(weights, v_ref[:, lanes])
            mixed = mixed[:, :HEAD_DIM] / mixed[:, HEAD_DIM : HEAD_DIM + 1]
            att_ref[span, h * HEAD_DIM : (h + 1) * HEAD_DIM] = mixed.astype(jnp.bfloat16)
    quarter = rows // len(outs)
    stores = []
    for k, out_hbm in enumerate(outs):
        low = pl.multiple_of((tensor_at ^ k) * quarter, quarter)
        store = pltpu.make_async_copy(att_ref.at[pl.ds(low, quarter)], out_hbm, sems.at[2 + k])
        store.start()
        stores.append(store)
    for store in stores:
        store.wait()


def vmem():
    return pl.BlockSpec(memory_space=pltpu.VMEM)


def smem():
    return pl.BlockSpec(memory_space=pltpu.SMEM)


def hbm():
    return pl.BlockSpec(memory_space=pltpu.HBM)


def anywhere():
    return pl.BlockSpec(memory_space=pl.ANY)


def bf16(*shape):
    return jax.ShapeDtypeStruct(shape, jnp.bfloat16)


def bf16_scratch(*shape):
    return pltpu.VMEM(shape, jnp.bfloat16)


def attend(grids, x, gain, w, b, parts):
    rows, width = x.shape
    cols = w.shape[1]
    padded = cols // HEAD_DIM * LANES
    return pl.pallas_call(
        attend_kernel,
        out_shape=[bf16(rows // parts, cols)] * parts,
        in_specs=[smem(), anywhere(), vmem(), anywhere(), vmem()],
        out_specs=[hbm()] * parts,
        scratch_shapes=[
            bf16_scratch(rows, width),
            bf16_scratch(3, cols, width),
            bf16_scratch(rows, width),
            bf16_scratch(3, padded, width),
            pltpu.VMEM((8, padded), jnp.float32),
            bf16_scratch(rows, padded),
            bf16_scratch(rows, padded),
            bf16_scratch(rows, padded),
            bf16_scratch(rows, cols),
            pltpu.SemaphoreType.DMA((2 + parts,)),
        ],
        compiler_params=pltpu.CompilerParams(vmem_limit_bytes=ATTEND_VMEM_BYTES),
        cost_estimate=pl.CostEstimate(
            flops=2 * rows * (3 * width * cols + 2 * rows * cols),
            bytes_accessed=2 * (2 * rows * width + 3 * width * cols),
            transcendentals=rows * rows * cols // HEAD_DIM,
        ),
    )(grids, x, gain, w, b)


def project_kernel(count, splits, x_hbm, bias_ref, gain_ref, *rest):
    blocks, weights, outs = rest[:count], rest[count : 2 * count], rest[2 * count : -5]
    x_ref, block_ref, weight_ref, out_ref, sems = rest[-5:]
    rows, size = x_ref.shape[0], out_ref.shape[1]
    low = pl.multiple_of(lax.axis_index("tensor") * rows, rows)
    loads = [pltpu.make_async_copy(x_hbm.at[pl.ds(low, rows)], x_ref, sems.at[0])]
    for k in range(count):
        loads.append(pltpu.make_async_copy(blocks[k], block_ref.at[k], sems.at[1 + 2 * k]))
        loads.append(pltpu.make_async_copy(weights[k], weight_ref.at[k], sems.at[2 + 2 * k]))
    for load in loads:
        load.start()
    loads[0].wait()
    summed = x_ref[...].astype(jnp.float32) + bias_ref[...].reshape(1, -1)
    for k in range(count):
        loads[1 + 2 * k].wait()
        loads[2 + 2 * k].wait()
        summed = summed + dot32(block_ref[k], weight_ref[k])
    merged = rms_scale(summed, gain_ref[...].reshape(1, -1)).astype(jnp.bfloat16)
    out_row = lax.broadcasted_iota(jnp.int32, (rows, rows), 0)
    row = lax.broadcasted_iota(jnp.int32, (rows, rows), 1)
    four = (out_row // size) ^ (lax.axis_index("dp") // splits)
    sort = (row == out_row % size * MERGE + four).astype(jnp.bfloat16)
    stores = []
    for k, out_hbm in enumerate(outs):
        out_ref[k] = dot32(sort[k * size : (k + 1) * size, :], merged).astype(jnp.bfloat16)
        store = pltpu.make_async_copy(out_ref.at[k], out_hbm, sems.at[k])
        store.start()
        stores.append(store)
    for store in stores:
        store.wait()


def project(x, bias, gain, blocks, weights, splits):
    rows, cols = blocks[0].shape
    width = x.shape[1]
    count = len(blocks)
    return pl.pallas_call(
        functools.partial(project_kernel, count, splits),
        out_shape=[bf16(rows // MERGE, width)] * MERGE,
        in_specs=[anywhere(), vmem(), vmem()] + [anywhere()] * (2 * count),
        out_specs=[hbm()] * MERGE,
        scratch_shapes=[
            bf16_scratch(rows, width),
            bf16_scratch(count, rows, cols),
            bf16_scratch(count, cols, width),
            bf16_scratch(MERGE, rows // MERGE, width),
            pltpu.SemaphoreType.DMA((max(MERGE, 1 + 2 * count),)),
        ],
        compiler_params=pltpu.CompilerParams(vmem_limit_bytes=VMEM_BYTES),
        cost_estimate=pl.CostEstimate(
            flops=2 * rows * width * width,
            bytes_accessed=2 * width * width + 6 * rows * width,
            transcendentals=rows,
        ),
    )(x, bias, gain, *blocks, *weights)


def first_kernel(groups, batches, images, w_ref, *rest):
    blocks, (up_ref, down_ref), (cat_ref, sems) = rest[:-4], rest[-4:-2], rest[-2:]
    count = len(blocks) // groups
    size = cat_ref.shape[0] // len(blocks)
    here, line = lax.axis_index("dp"), lax.axis_size("dp")
    loads = []
    for g in range(groups):
        for j in range(count):
            image = j ^ (here % images) if images > 1 else j
            low = (g * count + image) * size
            low = pl.multiple_of(low, size) if images > 1 else low
            place = cat_ref.at[pl.ds(low, size)]
            k = g * count + j
            loads.append(pltpu.make_async_copy(blocks[k], place, sems.at[k]))
            loads[-1].start()
    for load in loads:
        load.wait()
    rows = count // batches * size
    for g in range(groups):
        low = g * count * size
        out = dot32(cat_ref[low : low + count * size, :], w_ref[...]).astype(jnp.bfloat16)
        for j in range(batches):
            batch = j ^ (here // images)
            part = out[j * rows : (j + 1) * rows]
            up_ref[(batch + here) % batches, g] = part
            down_ref[(batch + line - 1 - here) % batches, g] = part


def first(groups, batches, w):
    count = len(groups[0])
    blocks = [block for group in groups for block in group]
    rows, depth = blocks[0].shape
    images = count // batches
    out = bf16(batches, len(groups), images * rows, w.shape[1])
    return pl.pallas_call(
        functools.partial(first_kernel, len(groups), batches, images),
        out_shape=[out, out],
        in_specs=[vmem()] + [anywhere()] * len(blocks),
        out_specs=[vmem(), vmem()],
        scratch_shapes=[
            bf16_scratch(rows * len(blocks), depth),
            pltpu.SemaphoreType.DMA((len(blocks),)),
        ],
        compiler_params=pltpu.CompilerParams(vmem_limit_bytes=VMEM_BYTES // 2),
        cost_estimate=pl.CostEstimate(
            flops=2 * rows * len(blocks) * depth * w.shape[1],
            bytes_accessed=2 * depth * w.shape[1] + 6 * rows * len(blocks) * depth,
            transcendentals=0,
        ),
    )(w, *blocks)


def second_kernel(count, bias_ref, goes_ref, w_hbm, *rest):
    totals, (send_ref, keep_ref), (w_ref, h_ref, sem) = rest[:count], rest[count:-3], rest[-3:]
    load = pltpu.make_async_copy(w_hbm, w_ref, sem)
    load.start()
    rows = totals[0].shape[0]
    bias = bias_ref[...].reshape(1, -1)
    for at, total in enumerate(totals):
        value = total[...] + bias
        value = 0.5 * value * (1.0 + lax.erf(value * math.sqrt(0.5)))
        h_ref[at * rows : (at + 1) * rows, :] = value.astype(jnp.bfloat16)
    half = send_ref.shape[0]
    index = lax.broadcasted_iota(jnp.int32, (half, 2 * half), 0)
    load.wait()
    for low, out_ref in ((half, send_ref), (0, keep_ref)):
        sort = (index + low == goes_ref[...]).astype(jnp.bfloat16)
        moved = dot32(sort, h_ref[...]).astype(jnp.bfloat16)
        out_ref[...] = dot32(moved, w_ref[...]).astype(jnp.bfloat16)


def second(totals, bias, goes, w):
    rows, width = totals[0].shape
    count = len(totals)
    out = bf16(rows * count // 2, w.shape[1])
    return pl.pallas_call(
        functools.partial(second_kernel, count),
        out_shape=[out, out],
        in_specs=[vmem(), vmem(), anywhere()] + [vmem()] * count,
        out_specs=[vmem(), vmem()],
        scratch_shapes=[
            bf16_scratch(*w.shape),
            bf16_scratch(rows * count, width),
            pltpu.SemaphoreType.DMA,
        ],
        compiler_params=pltpu.CompilerParams(vmem_limit_bytes=VMEM_BYTES),
        cost_estimate=pl.CostEstimate(
            flops=2 * rows * count * width * w.shape[1],
            bytes_accessed=2 * w.shape[0] * w.shape[1],
            transcendentals=rows * count * width,
        ),
    )(bias, goes, w, *totals)


def local(
    patches,
    grids,
    dest,
    norm_gain,
    qkv_weight,
    qkv_bias,
    proj_weight,
    proj_bias,
    merge_gain,
    w_first,
    b_first,
    w_second,
    b_second,
    text_embed,
):
    dps, tensors = lax.axis_size("dp"), lax.axis_size("tensor")
    tensor_at, dp_at = lax.axis_index("tensor"), lax.axis_index("dp")
    rows, width = patches.shape
    merged = dest.shape[1]
    seq_rows = text_embed.shape[0]
    cap = merged // dps
    part = cap // tensors

    proj_high = {0: proj_weight, tensors // 2: swap(proj_weight, "tensor", tensors // 2)}
    batches = min(dps, BATCHES)
    images = dps // batches
    blocks = attend(
        grids, patches, norm_gain, jnp.swapaxes(qkv_weight, 1, 2), qkv_bias, tensors
    )
    def places(after):
        early = (grids, dest, dp_at, tensor_at, jnp.arange(merged, dtype=jnp.int32))
        (sides, rows_to, here, there, each), _ = lax.optimization_barrier((early, after))
        live = sides[0, 0] * sides[0, 1]
        target = jnp.where(each * MERGE < live, rows_to[0], -1)
        targets = jnp.stack([swap(target, "dp", j) if j else target for j in range(dps)])
        targets = targets[jnp.arange(dps) ^ here]
        shard, rank = slots(targets, seq_rows, dps, each)
        quarter = (rank // part) ^ there
        bits = tensors.bit_length() - 1
        quarter = sum(((quarter >> k) & 1) << (bits - 1 - k) for k in range(bits))
        goes = (quarter * dps + shard) * part + rank % part
        image = jnp.arange(dps)[:, None] % images
        goes = jnp.where(targets >= 0, goes * images + image, -1)
        goes = goes.reshape(batches, images, tensors, merged // tensors).transpose(0, 2, 1, 3)
        goes = goes[:, jnp.arange(tensors) ^ there].reshape(batches, 1, images * merged)
        slot_rows = jnp.sum(
            jnp.where(
                (shard == here)[:, None, :]
                & (rank[:, None, :] == jnp.arange(cap)[None, :, None]),
                targets[:, None, :] % seq_rows + 1,
                0,
            ),
            axis=-1,
        )
        slot_rows = slot_rows.reshape(batches, images, tensors, part).transpose(2, 0, 3, 1) - 1
        slot_rows = slot_rows[jnp.arange(tensors) ^ there].reshape(1, -1)
        rows_out = jnp.arange(seq_rows, dtype=jnp.int32)[:, None]
        return goes, (rows_out == slot_rows).astype(jnp.bfloat16)

    blocks, proj_high = lax.optimization_barrier((list(blocks), proj_high))
    goes, hit = places(blocks[0])
    blocks = [swap(block, "tensor", k) if k else block for k, block in enumerate(blocks)]
    proj_blocks = {}
    for k, high in proj_high.items():
        for j, block in enumerate(gather_low(high, "tensor", tensors // 2)):
            proj_blocks[k | j] = block
    proj_blocks = [proj_blocks[k] for k in range(tensors)]
    proj_bias, goes, hit = lax.optimization_barrier((proj_bias, goes, hit))
    piece = w_first.shape[0]
    splits = width // piece
    merged_in = project(patches, proj_bias, merge_gain, blocks, proj_blocks, splits)

    near, far = ([[] for _ in range(tensors // 2)] for _ in range(2))
    for j in range(dps):
        block = merged_in[j // splits]
        if splits > 1:
            at = ((dp_at ^ j) % splits) * piece
            block = lax.dynamic_slice_in_dim(block, at, piece, 1)
        if j:
            block = swap(block, "dp", j)
        for k, line in enumerate(gather_low(block, "tensor", tensors // 2)):
            near[k].append(line)
        high = swap(block, "tensor", tensors // 2)
        for k, line in enumerate(gather_low(high, "tensor", tensors // 2)):
            far[k].append(line)
    streams = [first(near, batches, w_first), first(far, batches, w_first)]

    columns = w_second.shape[1]
    shares = dps // tensors

    def to_shards(members):
        members = jnp.stack(members, axis=1)
        blocks = []
        for j in range(dps):
            moved = pick(members, dp_at ^ j)
            blocks.append(swap(moved, "dp", j) if j else moved)
        return blocks

    arrived = []

    def finish(batch, sums, after, results):
        if batch == batches - 1:
            arrived.append(to_shards(results[: batches - 2]))
            after = arrived[0][1]
        if after is not None:
            sums, _ = lax.optimization_barrier((sums, after))
        rows_in = [part.reshape(-1, w_second.shape[0]) for part in sums]
        send, block = second(rows_in, b_first, goes[batch], w_second)
        wait = send
        block = add16(block, swap(send, "tensor", 1))
        step = 2
        while step < tensors:
            half = block.shape[0] // 2
            block = add16(block[:half], swap(block[half:], "tensor", step))
            step *= 2
        return wait, block.reshape(dps, part * images, columns)

    held = line_sums(streams, "dp", finish)
    for block in held[batches - 2 :]:
        arrived.append(to_shards([block]))
    arrived = jnp.concatenate([jnp.stack(blocks) for blocks in arrived], axis=1)
    arrived = arrived.reshape(tensors, shares, -1, columns)
    visual = []
    for k in range(tensors):
        moved = pick(arrived, (tensor_at ^ k) ^ (dp_at // shares))
        moved = swap(moved, "tensor", k) if k else moved
        if shares > 1:
            moved = jnp.concatenate(
                [pick(moved, (dp_at % shares) ^ j) for j in range(shares)], axis=-1
            )
        visual.append(moved.reshape(-1, shares * columns))
    visual = jnp.concatenate(visual, axis=0)

    covered = jnp.sum(hit, axis=1, keepdims=True, dtype=jnp.float32) > 0
    placed = dot32(hit, visual) + b_second
    return jnp.where(covered, placed.astype(jnp.bfloat16), text_embed)


def solution(mesh):
    in_specs = (
        P(("groups", "dp"), None),
        P(("groups", "dp"), None),
        P(("groups", "dp"), None),
        P(),
        P(None, None, "tensor"),
        P(None, "tensor"),
        P("tensor", None),
        P(),
        P(),
        P("dp", "tensor"),
        P("tensor"),
        P("tensor", "dp"),
        P("tensor"),
        P(("groups", "dp"), "tensor"),
    )
    out_specs = P(("groups", "dp"), "tensor")
    return jax.shard_map(local, mesh=mesh, in_specs=in_specs, out_specs=out_specs, check_vma=False)
```

```python
import functools
import math

import jax
import jax.numpy as jnp
from jax import lax
from jax.experimental import pallas as pl
from jax.experimental.pallas import tpu as pltpu
from jax.sharding import PartitionSpec as P

HEAD_DIM = 80
MERGE = 4
BATCHES = 4
LANES = 128
QUERY_ROWS = 512
VMEM_BYTES = 48 * 1024 * 1024
ATTEND_VMEM_BYTES = 60 * 1024 * 1024


def rms_scale(values, gain):
    return values * lax.rsqrt(jnp.mean(values * values, axis=-1, keepdims=True) + 1e-06) * gain


def dot32(a, b):
    return jnp.dot(a, b, preferred_element_type=jnp.float32)


def dot32t(a, b):
    return lax.dot_general(a, b, (((1,), (1,)), ((), ())), preferred_element_type=jnp.float32)


def swap(x, axis, k):
    n = lax.axis_size(axis)
    return lax.ppermute(x, axis, [(a, a ^ k) for a in range(n)])


def gather_low(x, axis, count):
    blocks = {0: x}
    step = count // 2
    while step:
        for k in list(blocks):
            blocks[k | step] = swap(blocks[k], axis, step)
        step //= 2
    return [blocks[k] for k in range(count)]


def add16(a, b):
    return (a.astype(jnp.float32) + b.astype(jnp.float32)).astype(jnp.bfloat16)


def pick(x, at):
    return lax.dynamic_index_in_dim(x, at, 0, keepdims=False)


def line_sums(streams, axis, finish):
    n = lax.axis_size(axis)
    here = lax.axis_index(axis)
    blocks = streams[0][0].shape[0]
    steps = ((lambda a: (a, a + 1)), (lambda a: (n - 1 - a, n - 2 - a)))
    sent = [[[] for _ in steps] for _ in streams]
    came = [[[] for _ in steps] for _ in streams]
    results, waits, ready = [], {}, []

    def drain(step):
        while ready:
            done, sums = ready.pop()
            waits[step], result = finish(done, sums, [values[-1] for values in sent[0]], results)
            results.append(result)

    for step in range(n + blocks - 1):
        for s, terms in enumerate(streams):
            if s:
                drain(step)
            for w, step_to in enumerate(steps):
                value = terms[w][step % blocks]
                if step:
                    last = came[s][w][-1]
                    if s and step in waits:
                        last, _ = lax.optimization_barrier((last, waits[step]))
                    value = add16(value, last)
                sent[s][w].append(value)
                pairs = [step_to(a) for a in range(n - 1) if 0 <= step - a < blocks]
                if pairs:
                    came[s][w].append(lax.ppermute(value, axis, pairs))
        done = step - (n - 1)
        if done >= 0:
            sums = []
            for s in range(len(streams)):
                up, down = sent[s][0], came[s][1]
                below, above = up[done + n - 1], jnp.zeros_like(up[0])
                for place in range(n - 1):
                    below = jnp.where(here == place, up[done + place], below)
                    above = jnp.where(here == place, down[done + n - 2 - place], above)
                sums.append(below.astype(jnp.float32) + above.astype(jnp.float32))
            ready.append((done, sums))
    drain(n + blocks - 1)
    return results


def slots(target, seq_rows, shards, each):
    shard = jnp.where(target >= 0, target // seq_rows, shards)
    same = shard[..., :, None] == shard[..., None, :]
    earlier = each[None, :] < each[:, None]
    rank = jnp.sum((same & earlier).astype(jnp.int32), axis=-1)
    return shard, rank


def attend_kernel(grid_ref, x_hbm, gain_ref, w_hbm, b_ref, *rest):
    outs, scratch = rest[:-10], rest[-10:]
    x_ref, w_ref, n_ref, pad_ref, bias_ref, q_ref, k_ref, v_ref, att_ref, sems = scratch
    load_w = pltpu.make_async_copy(w_hbm, w_ref, sems.at[0])
    load_x = pltpu.make_async_copy(x_hbm, x_ref, sems.at[1])
    load_w.start()
    load_x.start()
    rows = x_ref.shape[0]
    heads = w_ref.shape[1] // HEAD_DIM
    live = grid_ref[0, 0] * grid_ref[0, 1]
    tensor_at = lax.axis_index("tensor")
    lane = lax.broadcasted_iota(jnp.int32, (1, heads * LANES), 1) % LANES
    for j in range(3):
        bias_ref[j : j + 1, :] = jnp.where((lane == HEAD_DIM) & (j != 1), 1.0, 0.0)
        for h in range(heads):
            low, at = h * LANES, h * HEAD_DIM
            bias_ref[j : j + 1, low : low + HEAD_DIM] = b_ref[j : j + 1, at : at + HEAD_DIM]
            pad_ref[j, low + HEAD_DIM : low + LANES, :] = jnp.zeros(
                (LANES - HEAD_DIM, w_ref.shape[2]), jnp.bfloat16
            )
    load_w.wait()
    for j in range(3):
        for h in range(heads):
            low, at = h * LANES, h * HEAD_DIM
            pad_ref[j, low : low + HEAD_DIM, :] = w_ref[j, at : at + HEAD_DIM, :]
    load_x.wait()
    step = min(QUERY_ROWS, rows)
    scale = math.log2(math.e) / math.sqrt(HEAD_DIM)
    extra = lax.broadcasted_iota(jnp.int32, (step, heads * LANES), 1) % LANES == HEAD_DIM
    row = lax.broadcasted_iota(jnp.int32, (step, heads * LANES), 0)
    gain = gain_ref[...].reshape(1, -1)
    for at in range(0, rows, step):
        span = slice(at, at + step)
        normed = rms_scale(x_ref[span, :].astype(jnp.float32), gain)
        n_ref[span, :] = normed.astype(jnp.bfloat16)
        for j, ref in enumerate((q_ref, k_ref, v_ref)):
            out = dot32t(n_ref[span, :], pad_ref[j]) + bias_ref[j : j + 1, :]
            if j == 0:
                out = out * scale
            if j == 1:
                out = jnp.where(extra & (row + at >= live), -1e30, out)
            ref[span, :] = out.astype(jnp.bfloat16)
    for at in range(0, rows, step):
        span = slice(at, at + step)
        for h in range(heads):
            lanes = slice(h * LANES, (h + 1) * LANES)
            scores = dot32t(q_ref[span, lanes], k_ref[:, lanes])
            peak = jnp.max(scores, axis=-1, keepdims=True)
            weights = jnp.exp2(scores - peak).astype(jnp.bfloat16)
            mixed = dot32(weights, v_ref[:, lanes])
            mixed = mixed[:, :HEAD_DIM] / mixed[:, HEAD_DIM : HEAD_DIM + 1]
            att_ref[span, h * HEAD_DIM : (h + 1) * HEAD_DIM] = mixed.astype(jnp.bfloat16)
    quarter = rows // len(outs)
    stores = []
    for k, out_hbm in enumerate(outs):
        low = pl.multiple_of((tensor_at ^ k) * quarter, quarter)
        store = pltpu.make_async_copy(att_ref.at[pl.ds(low, quarter)], out_hbm, sems.at[2 + k])
        store.start()
        stores.append(store)
    for store in stores:
        store.wait()


def vmem():
    return pl.BlockSpec(memory_space=pltpu.VMEM)


def smem():
    return pl.BlockSpec(memory_space=pltpu.SMEM)


def hbm():
    return pl.BlockSpec(memory_space=pltpu.HBM)


def anywhere():
    return pl.BlockSpec(memory_space=pl.ANY)


def bf16(*shape):
    return jax.ShapeDtypeStruct(shape, jnp.bfloat16)


def bf16_scratch(*shape):
    return pltpu.VMEM(shape, jnp.bfloat16)


def attend(grids, x, gain, w, b, parts):
    rows, width = x.shape
    cols = w.shape[1]
    padded = cols // HEAD_DIM * LANES
    return pl.pallas_call(
        attend_kernel,
        out_shape=[bf16(rows // parts, cols)] * parts,
        in_specs=[smem(), anywhere(), vmem(), anywhere(), vmem()],
        out_specs=[hbm()] * parts,
        scratch_shapes=[
            bf16_scratch(rows, width),
            bf16_scratch(3, cols, width),
            bf16_scratch(rows, width),
            bf16_scratch(3, padded, width),
            pltpu.VMEM((8, padded), jnp.float32),
            bf16_scratch(rows, padded),
            bf16_scratch(rows, padded),
            bf16_scratch(rows, padded),
            bf16_scratch(rows, cols),
            pltpu.SemaphoreType.DMA((2 + parts,)),
        ],
        compiler_params=pltpu.CompilerParams(vmem_limit_bytes=ATTEND_VMEM_BYTES),
        cost_estimate=pl.CostEstimate(
            flops=2 * rows * (3 * width * cols + 2 * rows * cols),
            bytes_accessed=2 * (2 * rows * width + 3 * width * cols),
            transcendentals=rows * rows * cols // HEAD_DIM,
        ),
    )(grids, x, gain, w, b)


def project_kernel(count, splits, x_hbm, bias_ref, gain_ref, *rest):
    blocks, weights, outs = rest[:count], rest[count : 2 * count], rest[2 * count : -5]
    x_ref, block_ref, weight_ref, out_ref, sems = rest[-5:]
    rows, size = x_ref.shape[0], out_ref.shape[1]
    low = pl.multiple_of(lax.axis_index("tensor") * rows, rows)
    loads = [pltpu.make_async_copy(x_hbm.at[pl.ds(low, rows)], x_ref, sems.at[0])]
    for k in range(count):
        loads.append(pltpu.make_async_copy(blocks[k], block_ref.at[k], sems.at[1 + 2 * k]))
        loads.append(pltpu.make_async_copy(weights[k], weight_ref.at[k], sems.at[2 + 2 * k]))
    for load in loads:
        load.start()
    loads[0].wait()
    summed = x_ref[...].astype(jnp.float32) + bias_ref[...].reshape(1, -1)
    for k in range(count):
        loads[1 + 2 * k].wait()
        loads[2 + 2 * k].wait()
        summed = summed + dot32(block_ref[k], weight_ref[k])
    merged = rms_scale(summed, gain_ref[...].reshape(1, -1)).astype(jnp.bfloat16)
    out_row = lax.broadcasted_iota(jnp.int32, (rows, rows), 0)
    row = lax.broadcasted_iota(jnp.int32, (rows, rows), 1)
    four = (out_row // size) ^ (lax.axis_index("dp") // splits)
    sort = (row == out_row % size * MERGE + four).astype(jnp.bfloat16)
    stores = []
    for k, out_hbm in enumerate(outs):
        out_ref[k] = dot32(sort[k * size : (k + 1) * size, :], merged).astype(jnp.bfloat16)
        store = pltpu.make_async_copy(out_ref.at[k], out_hbm, sems.at[k])
        store.start()
        stores.append(store)
    for store in stores:
        store.wait()


def project(x, bias, gain, blocks, weights, splits):
    rows, cols = blocks[0].shape
    width = x.shape[1]
    count = len(blocks)
    return pl.pallas_call(
        functools.partial(project_kernel, count, splits),
        out_shape=[bf16(rows // MERGE, width)] * MERGE,
        in_specs=[anywhere(), vmem(), vmem()] + [anywhere()] * (2 * count),
        out_specs=[hbm()] * MERGE,
        scratch_shapes=[
            bf16_scratch(rows, width),
            bf16_scratch(count, rows, cols),
            bf16_scratch(count, cols, width),
            bf16_scratch(MERGE, rows // MERGE, width),
            pltpu.SemaphoreType.DMA((max(MERGE, 1 + 2 * count),)),
        ],
        compiler_params=pltpu.CompilerParams(vmem_limit_bytes=VMEM_BYTES),
        cost_estimate=pl.CostEstimate(
            flops=2 * rows * width * width,
            bytes_accessed=2 * width * width + 6 * rows * width,
            transcendentals=rows,
        ),
    )(x, bias, gain, *blocks, *weights)


def first_kernel(groups, batches, images, w_ref, *rest):
    blocks, (up_ref, down_ref), (cat_ref, sems) = rest[:-4], rest[-4:-2], rest[-2:]
    count = len(blocks) // groups
    size = cat_ref.shape[0] // len(blocks)
    here, line = lax.axis_index("dp"), lax.axis_size("dp")
    loads = []
    for g in range(groups):
        for j in range(count):
            image = j ^ (here % images) if images > 1 else j
            low = (g * count + image) * size
            low = pl.multiple_of(low, size) if images > 1 else low
            place = cat_ref.at[pl.ds(low, size)]
            k = g * count + j
            loads.append(pltpu.make_async_copy(blocks[k], place, sems.at[k]))
            loads[-1].start()
    for load in loads:
        load.wait()
    rows = count // batches * size
    for g in range(groups):
        low = g * count * size
        out = dot32(cat_ref[low : low + count * size, :], w_ref[...]).astype(jnp.bfloat16)
        for j in range(batches):
            batch = j ^ (here // images)
            part = out[j * rows : (j + 1) * rows]
            up_ref[(batch + here) % batches, g] = part
            down_ref[(batch + line - 1 - here) % batches, g] = part


def first(groups, batches, w, own):
    count = len(groups[0])
    blocks = [block for group in groups for block in group]
    rows, depth = blocks[0].shape
    images = count // batches
    out = bf16(batches, len(groups), images * rows, w.shape[1])
    return pl.pallas_call(
        functools.partial(first_kernel, len(groups), batches, images),
        out_shape=[out, out],
        in_specs=[vmem(), own] + [anywhere()] * (len(blocks) - 1),
        out_specs=[vmem(), vmem()],
        scratch_shapes=[
            bf16_scratch(rows * len(blocks), depth),
            pltpu.SemaphoreType.DMA((len(blocks),)),
        ],
        compiler_params=pltpu.CompilerParams(vmem_limit_bytes=VMEM_BYTES // 2),
        cost_estimate=pl.CostEstimate(
            flops=2 * rows * len(blocks) * depth * w.shape[1],
            bytes_accessed=2 * depth * w.shape[1] + 6 * rows * len(blocks) * depth,
            transcendentals=0,
        ),
    )(w, *blocks)


def second_kernel(count, bias_ref, goes_ref, w_hbm, *rest):
    totals, (send_ref, keep_ref), (w_ref, h_ref, sem) = rest[:count], rest[count:-3], rest[-3:]
    load = pltpu.make_async_copy(w_hbm, w_ref, sem)
    load.start()
    rows = totals[0].shape[0]
    bias = bias_ref[...].reshape(1, -1)
    for at, total in enumerate(totals):
        value = total[...] + bias
        value = 0.5 * value * (1.0 + lax.erf(value * math.sqrt(0.5)))
        h_ref[at * rows : (at + 1) * rows, :] = value.astype(jnp.bfloat16)
    half = send_ref.shape[0]
    index = lax.broadcasted_iota(jnp.int32, (half, 2 * half), 0)
    load.wait()
    for low, out_ref in ((half, send_ref), (0, keep_ref)):
        sort = (index + low == goes_ref[...]).astype(jnp.bfloat16)
        moved = dot32(sort, h_ref[...]).astype(jnp.bfloat16)
        out_ref[...] = dot32(moved, w_ref[...]).astype(jnp.bfloat16)


def second(totals, bias, goes, w):
    rows, width = totals[0].shape
    count = len(totals)
    out = bf16(rows * count // 2, w.shape[1])
    return pl.pallas_call(
        functools.partial(second_kernel, count),
        out_shape=[out, out],
        in_specs=[vmem(), vmem(), anywhere()] + [vmem()] * count,
        out_specs=[vmem(), vmem()],
        scratch_shapes=[
            bf16_scratch(*w.shape),
            bf16_scratch(rows * count, width),
            pltpu.SemaphoreType.DMA,
        ],
        compiler_params=pltpu.CompilerParams(vmem_limit_bytes=VMEM_BYTES),
        cost_estimate=pl.CostEstimate(
            flops=2 * rows * count * width * w.shape[1],
            bytes_accessed=2 * w.shape[0] * w.shape[1],
            transcendentals=rows * count * width,
        ),
    )(bias, goes, w, *totals)


def place_kernel(count, hit_ref, bias_ref, text_ref, *rest):
    blocks, out_ref, (cat_ref, sems) = rest[:count], rest[count], rest[-2:]
    loads, low = [], 0
    for k, block in enumerate(blocks):
        place = cat_ref.at[low : low + block.shape[0]]
        loads.append(pltpu.make_async_copy(block, place, sems.at[k]))
        loads[-1].start()
        low += block.shape[0]
    hit = hit_ref[...]
    covered = jnp.sum(hit.astype(jnp.float32), axis=1, keepdims=True) > 0
    for load in loads:
        load.wait()
    placed = dot32(hit, cat_ref[...]) + bias_ref[...].reshape(1, -1)
    out_ref[...] = jnp.where(covered, placed.astype(jnp.bfloat16), text_ref[...])


def place_rows(blocks, hit, bias, text):
    count = len(blocks)
    return pl.pallas_call(
        functools.partial(place_kernel, count),
        out_shape=bf16(*text.shape),
        in_specs=[vmem()] * 3 + [anywhere()] * count,
        out_specs=vmem(),
        scratch_shapes=[
            bf16_scratch(hit.shape[1], text.shape[1]),
            pltpu.SemaphoreType.DMA((count,)),
        ],
        compiler_params=pltpu.CompilerParams(vmem_limit_bytes=VMEM_BYTES // 2),
        cost_estimate=pl.CostEstimate(
            flops=2 * hit.shape[0] * hit.shape[1] * text.shape[1],
            bytes_accessed=4 * text.shape[0] * text.shape[1],
            transcendentals=0,
        ),
    )(hit, bias, text, *blocks)


def local(
    patches,
    grids,
    dest,
    norm_gain,
    qkv_weight,
    qkv_bias,
    proj_weight,
    proj_bias,
    merge_gain,
    w_first,
    b_first,
    w_second,
    b_second,
    text_embed,
):
    dps, tensors = lax.axis_size("dp"), lax.axis_size("tensor")
    tensor_at, dp_at = lax.axis_index("tensor"), lax.axis_index("dp")
    rows, width = patches.shape
    merged = dest.shape[1]
    seq_rows = text_embed.shape[0]
    cap = merged // dps
    part = cap // tensors

    proj_high = {0: proj_weight, tensors // 2: swap(proj_weight, "tensor", tensors // 2)}
    batches = min(dps, BATCHES)
    images = dps // batches
    blocks = attend(
        grids, patches, norm_gain, jnp.swapaxes(qkv_weight, 1, 2), qkv_bias, tensors
    )
    def places(after):
        early = (grids, dest, dp_at, tensor_at, jnp.arange(merged, dtype=jnp.int32))
        (sides, rows_to, here, there, each), _ = lax.optimization_barrier((early, after))
        live = sides[0, 0] * sides[0, 1]
        target = jnp.where(each * MERGE < live, rows_to[0], -1)
        targets = jnp.stack([swap(target, "dp", j) if j else target for j in range(dps)])
        targets = targets[jnp.arange(dps) ^ here]
        shard, rank = slots(targets, seq_rows, dps, each)
        quarter = (rank // part) ^ there
        bits = tensors.bit_length() - 1
        quarter = sum(((quarter >> k) & 1) << (bits - 1 - k) for k in range(bits))
        goes = (quarter * dps + shard) * part + rank % part
        image = jnp.arange(dps)[:, None] % images
        goes = jnp.where(targets >= 0, goes * images + image, -1)
        goes = goes.reshape(batches, images, tensors, merged // tensors).transpose(0, 2, 1, 3)
        goes = goes[:, jnp.arange(tensors) ^ there].reshape(batches, 1, images * merged)
        slot_rows = jnp.sum(
            jnp.where(
                (shard == here)[:, None, :]
                & (rank[:, None, :] == jnp.arange(cap)[None, :, None]),
                targets[:, None, :] % seq_rows + 1,
                0,
            ),
            axis=-1,
        )
        slot_rows = slot_rows.reshape(batches, images, tensors, part).transpose(2, 0, 3, 1) - 1
        slot_rows = slot_rows[jnp.arange(tensors) ^ there].reshape(1, -1)
        rows_out = jnp.arange(seq_rows, dtype=jnp.int32)[:, None]
        return goes, (rows_out == slot_rows).astype(jnp.bfloat16)

    blocks = [swap(block, "tensor", k) if k else block for k, block in enumerate(blocks)]
    blocks[1], proj_high = lax.optimization_barrier((blocks[1], proj_high))
    goes, hit = places(proj_high[tensors // 2])
    proj_blocks = {}
    for k, high in proj_high.items():
        for j, block in enumerate(gather_low(high, "tensor", tensors // 2)):
            proj_blocks[k | j] = block
    proj_blocks = [proj_blocks[k] for k in range(tensors)]
    proj_bias, goes, hit = lax.optimization_barrier((proj_bias, goes, hit))
    piece = w_first.shape[0]
    splits = width // piece
    merged_in = project(patches, proj_bias, merge_gain, blocks, proj_blocks, splits)

    near, far = ([[] for _ in range(tensors // 2)] for _ in range(2))
    for j in range(dps):
        block = merged_in[j // splits]
        if splits > 1:
            at = ((dp_at ^ j) % splits) * piece
            block = lax.dynamic_slice_in_dim(block, at, piece, 1)
        if j:
            block = swap(block, "dp", j)
        for k, line in enumerate(gather_low(block, "tensor", tensors // 2)):
            near[k].append(line)
        high = swap(block, "tensor", tensors // 2)
        for k, line in enumerate(gather_low(high, "tensor", tensors // 2)):
            far[k].append(line)
    near[0][1], _ = lax.optimization_barrier((near[0][1], far[0][:2]))
    streams = [first(near, batches, w_first, hbm()), first(far, batches, w_first, anywhere())]

    columns = w_second.shape[1]
    shares = dps // tensors

    def to_shards(members):
        members = jnp.stack(members, axis=1)
        blocks = []
        for j in range(dps):
            moved = pick(members, dp_at ^ j)
            blocks.append(swap(moved, "dp", j) if j else moved)
        return blocks

    arrived, pair_sums = [], []

    def finish(batch, sums, after, results):
        if batch == batches - 2:
            after = [after, results[-1]]
        if batch == batches - 1:
            arrived.append(to_shards(results[: batches - 2]))
            after = arrived[0][1:3]
        sums, _ = lax.optimization_barrier((sums, (after, pair_sums[-1:])))
        rows_in = [part.reshape(-1, w_second.shape[0]) for part in sums]
        send, block = second(rows_in, b_first, goes[batch], w_second)
        if batch == batches - 1:
            send, results[-1] = lax.optimization_barrier((send, results[-1]))
        wait = send
        block = add16(block, swap(send, "tensor", 1))
        pair_sums.append(block)
        step = 2
        while step < tensors:
            half = block.shape[0] // 2
            block = add16(block[:half], swap(block[half:], "tensor", step))
            step *= 2
        return wait, block.reshape(dps, part * images, columns)

    held = line_sums(streams, "dp", finish)
    arrived.append(to_shards(held[batches - 2 :]))
    visual = [[] for _ in range(tensors)]
    for group in (arrived[:-1], arrived[-1:]):
        group = jnp.concatenate([jnp.stack(blocks) for blocks in group], axis=1)
        group = group.reshape(tensors, shares, -1, columns)
        for k in range(tensors):
            moved = pick(group, (tensor_at ^ k) ^ (dp_at // shares))
            moved = swap(moved, "tensor", k) if k else moved
            if shares > 1:
                moved = jnp.concatenate(
                    [pick(moved, (dp_at % shares) ^ j) for j in range(shares)], axis=-1
                )
            visual[k].append(moved.reshape(-1, shares * columns))
    visual = [block for blocks in visual for block in blocks]
    if any(block.shape[0] % 16 for block in visual):
        visual = [jnp.concatenate(visual, axis=0)]
    return place_rows(visual, hit, b_second, text_embed)


def solution(mesh):
    in_specs = (
        P(("groups", "dp"), None),
        P(("groups", "dp"), None),
        P(("groups", "dp"), None),
        P(),
        P(None, None, "tensor"),
        P(None, "tensor"),
        P("tensor", None),
        P(),
        P(),
        P("dp", "tensor"),
        P("tensor"),
        P("tensor", "dp"),
        P("tensor"),
        P(("groups", "dp"), "tensor"),
    )
    out_specs = P(("groups", "dp"), "tensor")
    return jax.shard_map(local, mesh=mesh, in_specs=in_specs, out_specs=out_specs, check_vma=False)
```

```python
import functools
import math

import jax
import jax.numpy as jnp
from jax import lax
from jax.experimental import pallas as pl
from jax.experimental.pallas import tpu as pltpu
from jax.sharding import PartitionSpec as P

HEAD_DIM = 80
MERGE = 4
BATCHES = 4
LANES = 128
QUERY_ROWS = 512
VMEM_BYTES = 48 * 1024 * 1024
ATTEND_VMEM_BYTES = 60 * 1024 * 1024


def rms_scale(values, gain):
    return values * lax.rsqrt(jnp.mean(values * values, axis=-1, keepdims=True) + 1e-06) * gain


def dot32(a, b):
    return jnp.dot(a, b, preferred_element_type=jnp.float32)


def dot32t(a, b):
    return lax.dot_general(a, b, (((1,), (1,)), ((), ())), preferred_element_type=jnp.float32)


def swap(x, axis, k):
    n = lax.axis_size(axis)
    return lax.ppermute(x, axis, [(a, a ^ k) for a in range(n)])


def gather_low(x, axis, count):
    blocks = {0: x}
    step = count // 2
    while step:
        for k in list(blocks):
            blocks[k | step] = swap(blocks[k], axis, step)
        step //= 2
    return [blocks[k] for k in range(count)]


def add16(a, b):
    return (a.astype(jnp.float32) + b.astype(jnp.float32)).astype(jnp.bfloat16)


def pick(x, at):
    return lax.dynamic_index_in_dim(x, at, 0, keepdims=False)


def line_sums(streams, axis, finish):
    n = lax.axis_size(axis)
    here = lax.axis_index(axis)
    blocks = streams[0][0].shape[0]
    steps = ((lambda a: (a, a + 1)), (lambda a: (n - 1 - a, n - 2 - a)))
    sent = [[[] for _ in steps] for _ in streams]
    came = [[[] for _ in steps] for _ in streams]
    results, waits, ready = [], {}, []

    def drain(step):
        while ready:
            done, sums = ready.pop()
            after = [values[-1] for ways in sent for values in ways]
            waits[step], result = finish(done, sums, after, results, came[-1])
            results.append(result)

    for step in range(n + blocks - 1):
        for s, terms in enumerate(streams):
            if s:
                drain(step)
            for w, step_to in enumerate(steps):
                value = terms[w][step % blocks]
                if step:
                    last = came[s][w][-1]
                    if s and step in waits:
                        last, _ = lax.optimization_barrier((last, waits[step]))
                    value = add16(value, last)
                sent[s][w].append(value)
                pairs = [step_to(a) for a in range(n - 1) if 0 <= step - a < blocks]
                if pairs:
                    came[s][w].append(lax.ppermute(value, axis, pairs))
        done = step - (n - 1)
        if done >= 0:
            sums = []
            for s in range(len(streams)):
                up, down = sent[s][0], came[s][1]
                below, above = up[done + n - 1], jnp.zeros_like(up[0])
                for place in range(n - 1):
                    below = jnp.where(here == place, up[done + place], below)
                    above = jnp.where(here == place, down[done + n - 2 - place], above)
                sums.append(below.astype(jnp.float32) + above.astype(jnp.float32))
            ready.append((done, sums))
    drain(n + blocks - 1)
    return results


def slots(target, seq_rows, shards, each):
    shard = jnp.where(target >= 0, target // seq_rows, shards)
    same = shard[..., :, None] == shard[..., None, :]
    earlier = each[None, :] < each[:, None]
    rank = jnp.sum((same & earlier).astype(jnp.int32), axis=-1)
    return shard, rank


def attend_kernel(grid_ref, x_hbm, gain_ref, w_hbm, b_ref, *rest):
    outs, scratch = rest[:-10], rest[-10:]
    x_ref, w_ref, n_ref, pad_ref, bias_ref, q_ref, k_ref, v_ref, att_ref, sems = scratch
    load_w = pltpu.make_async_copy(w_hbm, w_ref, sems.at[0])
    load_x = pltpu.make_async_copy(x_hbm, x_ref, sems.at[1])
    load_w.start()
    load_x.start()
    rows = x_ref.shape[0]
    heads = w_ref.shape[1] // HEAD_DIM
    live = grid_ref[0, 0] * grid_ref[0, 1]
    tensor_at = lax.axis_index("tensor")
    lane = lax.broadcasted_iota(jnp.int32, (1, heads * LANES), 1) % LANES
    for j in range(3):
        bias_ref[j : j + 1, :] = jnp.where((lane == HEAD_DIM) & (j != 1), 1.0, 0.0)
        for h in range(heads):
            low, at = h * LANES, h * HEAD_DIM
            bias_ref[j : j + 1, low : low + HEAD_DIM] = b_ref[j : j + 1, at : at + HEAD_DIM]
            pad_ref[j, low + HEAD_DIM : low + LANES, :] = jnp.zeros(
                (LANES - HEAD_DIM, w_ref.shape[2]), jnp.bfloat16
            )
    load_w.wait()
    for j in range(3):
        for h in range(heads):
            low, at = h * LANES, h * HEAD_DIM
            pad_ref[j, low : low + HEAD_DIM, :] = w_ref[j, at : at + HEAD_DIM, :]
    load_x.wait()
    step = min(QUERY_ROWS, rows)
    scale = math.log2(math.e) / math.sqrt(HEAD_DIM)
    extra = lax.broadcasted_iota(jnp.int32, (step, heads * LANES), 1) % LANES == HEAD_DIM
    row = lax.broadcasted_iota(jnp.int32, (step, heads * LANES), 0)
    gain = gain_ref[...].reshape(1, -1)
    for at in range(0, rows, step):
        span = slice(at, at + step)
        normed = rms_scale(x_ref[span, :].astype(jnp.float32), gain)
        n_ref[span, :] = normed.astype(jnp.bfloat16)
        for j, ref in enumerate((q_ref, k_ref, v_ref)):
            out = dot32t(n_ref[span, :], pad_ref[j]) + bias_ref[j : j + 1, :]
            if j == 0:
                out = out * scale
            if j == 1:
                out = jnp.where(extra & (row + at >= live), -1e30, out)
            ref[span, :] = out.astype(jnp.bfloat16)
    for at in range(0, rows, step):
        span = slice(at, at + step)
        for h in range(heads):
            lanes = slice(h * LANES, (h + 1) * LANES)
            scores = dot32t(q_ref[span, lanes], k_ref[:, lanes])
            peak = jnp.max(scores, axis=-1, keepdims=True)
            weights = jnp.exp2(scores - peak).astype(jnp.bfloat16)
            mixed = dot32(weights, v_ref[:, lanes])
            mixed = mixed[:, :HEAD_DIM] / mixed[:, HEAD_DIM : HEAD_DIM + 1]
            att_ref[span, h * HEAD_DIM : (h + 1) * HEAD_DIM] = mixed.astype(jnp.bfloat16)
    quarter = rows // len(outs)
    stores = []
    for k, out_hbm in enumerate(outs):
        low = pl.multiple_of((tensor_at ^ k) * quarter, quarter)
        store = pltpu.make_async_copy(att_ref.at[pl.ds(low, quarter)], out_hbm, sems.at[2 + k])
        store.start()
        stores.append(store)
    for store in stores:
        store.wait()


def vmem():
    return pl.BlockSpec(memory_space=pltpu.VMEM)


def smem():
    return pl.BlockSpec(memory_space=pltpu.SMEM)


def hbm():
    return pl.BlockSpec(memory_space=pltpu.HBM)


def anywhere():
    return pl.BlockSpec(memory_space=pl.ANY)


def bf16(*shape):
    return jax.ShapeDtypeStruct(shape, jnp.bfloat16)


def bf16_scratch(*shape):
    return pltpu.VMEM(shape, jnp.bfloat16)


def attend(grids, x, gain, w, b, parts):
    rows, width = x.shape
    cols = w.shape[1]
    padded = cols // HEAD_DIM * LANES
    return pl.pallas_call(
        attend_kernel,
        out_shape=[bf16(rows // parts, cols)] * parts,
        in_specs=[smem(), anywhere(), vmem(), anywhere(), vmem()],
        out_specs=[hbm()] * parts,
        scratch_shapes=[
            bf16_scratch(rows, width),
            bf16_scratch(3, cols, width),
            bf16_scratch(rows, width),
            bf16_scratch(3, padded, width),
            pltpu.VMEM((8, padded), jnp.float32),
            bf16_scratch(rows, padded),
            bf16_scratch(rows, padded),
            bf16_scratch(rows, padded),
            bf16_scratch(rows, cols),
            pltpu.SemaphoreType.DMA((2 + parts,)),
        ],
        compiler_params=pltpu.CompilerParams(vmem_limit_bytes=ATTEND_VMEM_BYTES),
        cost_estimate=pl.CostEstimate(
            flops=2 * rows * (3 * width * cols + 2 * rows * cols),
            bytes_accessed=2 * (2 * rows * width + 3 * width * cols),
            transcendentals=rows * rows * cols // HEAD_DIM,
        ),
    )(grids, x, gain, w, b)


def project_kernel(count, splits, x_hbm, bias_ref, gain_ref, *rest):
    blocks, weights, outs = rest[:count], rest[count : 2 * count], rest[2 * count : -5]
    x_ref, block_ref, weight_ref, out_ref, sems = rest[-5:]
    rows, size = x_ref.shape[0], out_ref.shape[1]
    low = pl.multiple_of(lax.axis_index("tensor") * rows, rows)
    loads = [pltpu.make_async_copy(x_hbm.at[pl.ds(low, rows)], x_ref, sems.at[0])]
    for k in range(count):
        loads.append(pltpu.make_async_copy(blocks[k], block_ref.at[k], sems.at[1 + 2 * k]))
        loads.append(pltpu.make_async_copy(weights[k], weight_ref.at[k], sems.at[2 + 2 * k]))
    for load in loads:
        load.start()
    loads[0].wait()
    summed = x_ref[...].astype(jnp.float32) + bias_ref[...].reshape(1, -1)
    for k in range(count):
        loads[1 + 2 * k].wait()
        loads[2 + 2 * k].wait()
        summed = summed + dot32(block_ref[k], weight_ref[k])
    merged = rms_scale(summed, gain_ref[...].reshape(1, -1)).astype(jnp.bfloat16)
    out_row = lax.broadcasted_iota(jnp.int32, (rows, rows), 0)
    row = lax.broadcasted_iota(jnp.int32, (rows, rows), 1)
    four = (out_row // size) ^ (lax.axis_index("dp") // splits)
    sort = (row == out_row % size * MERGE + four).astype(jnp.bfloat16)
    stores = []
    for k, out_hbm in enumerate(outs):
        out_ref[k] = dot32(sort[k * size : (k + 1) * size, :], merged).astype(jnp.bfloat16)
        store = pltpu.make_async_copy(out_ref.at[k], out_hbm, sems.at[k])
        store.start()
        stores.append(store)
    for store in stores:
        store.wait()


def project(x, bias, gain, blocks, weights, splits):
    rows, cols = blocks[0].shape
    width = x.shape[1]
    count = len(blocks)
    return pl.pallas_call(
        functools.partial(project_kernel, count, splits),
        out_shape=[bf16(rows // MERGE, width)] * MERGE,
        in_specs=[anywhere(), vmem(), vmem()] + [anywhere()] * (2 * count),
        out_specs=[hbm()] * MERGE,
        scratch_shapes=[
            bf16_scratch(rows, width),
            bf16_scratch(count, rows, cols),
            bf16_scratch(count, cols, width),
            bf16_scratch(MERGE, rows // MERGE, width),
            pltpu.SemaphoreType.DMA((max(MERGE, 1 + 2 * count),)),
        ],
        compiler_params=pltpu.CompilerParams(vmem_limit_bytes=VMEM_BYTES),
        cost_estimate=pl.CostEstimate(
            flops=2 * rows * width * width,
            bytes_accessed=2 * width * width + 6 * rows * width,
            transcendentals=rows,
        ),
    )(x, bias, gain, *blocks, *weights)


def first_kernel(groups, batches, images, w_ref, *rest):
    blocks, (up_ref, down_ref), (cat_ref, sems) = rest[:-4], rest[-4:-2], rest[-2:]
    count = len(blocks) // groups
    size = cat_ref.shape[0] // len(blocks)
    here, line = lax.axis_index("dp"), lax.axis_size("dp")
    loads = []
    for g in range(groups):
        for j in range(count):
            image = j ^ (here % images) if images > 1 else j
            low = (g * count + image) * size
            low = pl.multiple_of(low, size) if images > 1 else low
            place = cat_ref.at[pl.ds(low, size)]
            k = g * count + j
            loads.append(pltpu.make_async_copy(blocks[k], place, sems.at[k]))
            loads[-1].start()
    for load in loads:
        load.wait()
    rows = count // batches * size
    for g in range(groups):
        low = g * count * size
        out = dot32(cat_ref[low : low + count * size, :], w_ref[...]).astype(jnp.bfloat16)
        for j in range(batches):
            batch = j ^ (here // images)
            part = out[j * rows : (j + 1) * rows]
            up_ref[(batch + here) % batches, g] = part
            down_ref[(batch + line - 1 - here) % batches, g] = part


def first(groups, batches, w, own):
    count = len(groups[0])
    blocks = [block for group in groups for block in group]
    rows, depth = blocks[0].shape
    images = count // batches
    out = bf16(batches, len(groups), images * rows, w.shape[1])
    return pl.pallas_call(
        functools.partial(first_kernel, len(groups), batches, images),
        out_shape=[out, out],
        in_specs=[vmem(), own] + [anywhere()] * (len(blocks) - 1),
        out_specs=[vmem(), vmem()],
        scratch_shapes=[
            bf16_scratch(rows * len(blocks), depth),
            pltpu.SemaphoreType.DMA((len(blocks),)),
        ],
        compiler_params=pltpu.CompilerParams(vmem_limit_bytes=VMEM_BYTES // 2),
        cost_estimate=pl.CostEstimate(
            flops=2 * rows * len(blocks) * depth * w.shape[1],
            bytes_accessed=2 * depth * w.shape[1] + 6 * rows * len(blocks) * depth,
            transcendentals=0,
        ),
    )(w, *blocks)


def second_kernel(count, bias_ref, goes_ref, w_hbm, *rest):
    totals, (send_ref, keep_ref), (w_ref, h_ref, sem) = rest[:count], rest[count:-3], rest[-3:]
    load = pltpu.make_async_copy(w_hbm, w_ref, sem)
    load.start()
    rows = totals[0].shape[0]
    bias = bias_ref[...].reshape(1, -1)
    for at, total in enumerate(totals):
        value = total[...] + bias
        value = 0.5 * value * (1.0 + lax.erf(value * math.sqrt(0.5)))
        h_ref[at * rows : (at + 1) * rows, :] = value.astype(jnp.bfloat16)
    half = send_ref.shape[0]
    index = lax.broadcasted_iota(jnp.int32, (half, 2 * half), 0)
    load.wait()
    for low, out_ref in ((half, send_ref), (0, keep_ref)):
        sort = (index + low == goes_ref[...]).astype(jnp.bfloat16)
        moved = dot32(sort, h_ref[...]).astype(jnp.bfloat16)
        out_ref[...] = dot32(moved, w_ref[...]).astype(jnp.bfloat16)


def second(totals, bias, goes, w):
    rows, width = totals[0].shape
    count = len(totals)
    out = bf16(rows * count // 2, w.shape[1])
    return pl.pallas_call(
        functools.partial(second_kernel, count),
        out_shape=[out, out],
        in_specs=[vmem(), vmem(), anywhere()] + [vmem()] * count,
        out_specs=[vmem(), vmem()],
        scratch_shapes=[
            bf16_scratch(*w.shape),
            bf16_scratch(rows * count, width),
            pltpu.SemaphoreType.DMA,
        ],
        compiler_params=pltpu.CompilerParams(vmem_limit_bytes=VMEM_BYTES),
        cost_estimate=pl.CostEstimate(
            flops=2 * rows * count * width * w.shape[1],
            bytes_accessed=2 * w.shape[0] * w.shape[1],
            transcendentals=rows * count * width,
        ),
    )(bias, goes, w, *totals)


def place_kernel(count, hit_ref, bias_ref, text_ref, *rest):
    blocks, out_ref, (cat_ref, sems) = rest[:count], rest[count], rest[-2:]
    loads, low = [], 0
    for k, block in enumerate(blocks):
        place = cat_ref.at[low : low + block.shape[0]]
        loads.append(pltpu.make_async_copy(block, place, sems.at[k]))
        loads[-1].start()
        low += block.shape[0]
    hit = hit_ref[...]
    covered = jnp.sum(hit.astype(jnp.float32), axis=1, keepdims=True) > 0
    for load in loads:
        load.wait()
    placed = dot32(hit, cat_ref[...]) + bias_ref[...].reshape(1, -1)
    out_ref[...] = jnp.where(covered, placed.astype(jnp.bfloat16), text_ref[...])


def place_rows(blocks, hit, bias, text):
    count = len(blocks)
    return pl.pallas_call(
        functools.partial(place_kernel, count),
        out_shape=bf16(*text.shape),
        in_specs=[vmem()] * 3 + [anywhere()] * count,
        out_specs=vmem(),
        scratch_shapes=[
            bf16_scratch(hit.shape[1], text.shape[1]),
            pltpu.SemaphoreType.DMA((count,)),
        ],
        compiler_params=pltpu.CompilerParams(vmem_limit_bytes=VMEM_BYTES // 2),
        cost_estimate=pl.CostEstimate(
            flops=2 * hit.shape[0] * hit.shape[1] * text.shape[1],
            bytes_accessed=4 * text.shape[0] * text.shape[1],
            transcendentals=0,
        ),
    )(hit, bias, text, *blocks)


def local(
    patches,
    grids,
    dest,
    norm_gain,
    qkv_weight,
    qkv_bias,
    proj_weight,
    proj_bias,
    merge_gain,
    w_first,
    b_first,
    w_second,
    b_second,
    text_embed,
):
    dps, tensors = lax.axis_size("dp"), lax.axis_size("tensor")
    tensor_at, dp_at = lax.axis_index("tensor"), lax.axis_index("dp")
    rows, width = patches.shape
    merged = dest.shape[1]
    seq_rows = text_embed.shape[0]
    cap = merged // dps
    part = cap // tensors

    proj_high = {0: proj_weight, tensors // 2: swap(proj_weight, "tensor", tensors // 2)}
    batches = min(dps, BATCHES)
    images = dps // batches
    blocks = attend(
        grids, patches, norm_gain, jnp.swapaxes(qkv_weight, 1, 2), qkv_bias, tensors
    )
    def places(after):
        early = (grids, dest, dp_at, tensor_at, jnp.arange(merged, dtype=jnp.int32))
        (sides, rows_to, here, there, each), _ = lax.optimization_barrier((early, after))
        live = sides[0, 0] * sides[0, 1]
        target = jnp.where(each * MERGE < live, rows_to[0], -1)
        targets = jnp.stack([swap(target, "dp", j) if j else target for j in range(dps)])
        targets = targets[jnp.arange(dps) ^ here]
        shard, rank = slots(targets, seq_rows, dps, each)
        quarter = (rank // part) ^ there
        bits = tensors.bit_length() - 1
        quarter = sum(((quarter >> k) & 1) << (bits - 1 - k) for k in range(bits))
        goes = (quarter * dps + shard) * part + rank % part
        image = jnp.arange(dps)[:, None] % images
        goes = jnp.where(targets >= 0, goes * images + image, -1)
        goes = goes.reshape(batches, images, tensors, merged // tensors).transpose(0, 2, 1, 3)
        goes = goes[:, jnp.arange(tensors) ^ there].reshape(batches, 1, images * merged)
        slot_rows = jnp.sum(
            jnp.where(
                (shard == here)[:, None, :]
                & (rank[:, None, :] == jnp.arange(cap)[None, :, None]),
                targets[:, None, :] % seq_rows + 1,
                0,
            ),
            axis=-1,
        )
        slot_rows = slot_rows.reshape(batches, images, tensors, part).transpose(2, 0, 3, 1) - 1
        slot_rows = slot_rows[jnp.arange(tensors) ^ there].reshape(1, -1)
        rows_out = jnp.arange(seq_rows, dtype=jnp.int32)[:, None]
        return goes, (rows_out == slot_rows).astype(jnp.bfloat16)

    blocks = [swap(block, "tensor", k) if k else block for k, block in enumerate(blocks)]
    blocks[1], proj_high = lax.optimization_barrier((blocks[1], proj_high))
    goes, hit = places(proj_high[tensors // 2])
    proj_blocks = {}
    for k, high in proj_high.items():
        for j, block in enumerate(gather_low(high, "tensor", tensors // 2)):
            proj_blocks[k | j] = block
    proj_blocks = [proj_blocks[k] for k in range(tensors)]
    proj_bias, goes, hit = lax.optimization_barrier((proj_bias, goes, hit))
    piece = w_first.shape[0]
    splits = width // piece
    merged_in = project(patches, proj_bias, merge_gain, blocks, proj_blocks, splits)

    near, far = ([[] for _ in range(tensors // 2)] for _ in range(2))
    for j in range(dps):
        block = merged_in[j // splits]
        if splits > 1:
            at = ((dp_at ^ j) % splits) * piece
            block = lax.dynamic_slice_in_dim(block, at, piece, 1)
        if j:
            block = swap(block, "dp", j)
        for k, line in enumerate(gather_low(block, "tensor", tensors // 2)):
            near[k].append(line)
        high = swap(block, "tensor", tensors // 2)
        for k, line in enumerate(gather_low(high, "tensor", tensors // 2)):
            far[k].append(line)
    near[0][1], _ = lax.optimization_barrier((near[0][1], far[0][:2]))
    streams = [first(near, batches, w_first, hbm()), first(far, batches, w_first, anywhere())]

    columns = w_second.shape[1]
    shares = dps // tensors

    def to_shards(members):
        members = jnp.stack(members, axis=1)
        blocks = []
        for j in range(dps):
            moved = pick(members, dp_at ^ j)
            blocks.append(swap(moved, "dp", j) if j else moved)
        return blocks

    pair_sums, early = [], []

    def finish(batch, sums, after, results, last):
        sums, _ = lax.optimization_barrier((sums, (after, pair_sums[-1:])))
        rows_in = [part.reshape(-1, w_second.shape[0]) for part in sums]
        send, block = second(rows_in, b_first, goes[batch], w_second)
        if batch == batches - 2:
            ends = [last[0][-1], last[1][-1], results[-1]]
            send, ends = lax.optimization_barrier((send, ends))
            last[0][-1], last[1][-1], results[-1] = ends
        if batch == batches - 1:
            early.extend(to_shards(results[: batches - 2]))
            ends = [results[-1], *early[1:3]]
            send, ends = lax.optimization_barrier((send, ends))
            results[-1], *early[1:3] = ends
        wait = send
        block = add16(block, swap(send, "tensor", 1))
        pair_sums.append(block)
        step = 2
        while step < tensors:
            half = block.shape[0] // 2
            block = add16(block[:half], swap(block[half:], "tensor", step))
            step *= 2
        return wait, block.reshape(dps, part * images, columns)

    held = line_sums(streams, "dp", finish)
    arrived = [early, to_shards(held[batches - 2 :])]
    visual = [[] for _ in range(tensors)]
    for group in (arrived[:-1], arrived[-1:]):
        group = jnp.concatenate([jnp.stack(blocks) for blocks in group], axis=1)
        group = group.reshape(tensors, shares, -1, columns)
        for k in range(tensors):
            moved = pick(group, (tensor_at ^ k) ^ (dp_at // shares))
            moved = swap(moved, "tensor", k) if k else moved
            if shares > 1:
                moved = jnp.concatenate(
                    [pick(moved, (dp_at % shares) ^ j) for j in range(shares)], axis=-1
                )
            visual[k].append(moved.reshape(-1, shares * columns))
    visual = [block for blocks in visual for block in blocks]
    if any(block.shape[0] % 16 for block in visual):
        visual = [jnp.concatenate(visual, axis=0)]
    return place_rows(visual, hit, b_second, text_embed)


def solution(mesh):
    in_specs = (
        P(("groups", "dp"), None),
        P(("groups", "dp"), None),
        P(("groups", "dp"), None),
        P(),
        P(None, None, "tensor"),
        P(None, "tensor"),
        P("tensor", None),
        P(),
        P(),
        P("dp", "tensor"),
        P("tensor"),
        P("tensor", "dp"),
        P("tensor"),
        P(("groups", "dp"), "tensor"),
    )
    out_specs = P(("groups", "dp"), "tensor")
    return jax.shard_map(local, mesh=mesh, in_specs=in_specs, out_specs=out_specs, check_vma=False)
```

```python
import functools
import math

import jax
import jax.numpy as jnp
from jax import lax
from jax.experimental import pallas as pl
from jax.experimental.pallas import tpu as pltpu
from jax.sharding import PartitionSpec as P

HEAD_DIM = 80
MERGE = 4
BATCHES = 4
LANES = 128
QUERY_ROWS = 512
VMEM_BYTES = 48 * 1024 * 1024
ATTEND_VMEM_BYTES = 60 * 1024 * 1024


def rms_scale(values, gain):
    return values * lax.rsqrt(jnp.mean(values * values, axis=-1, keepdims=True) + 1e-06) * gain


def dot32(a, b):
    return jnp.dot(a, b, preferred_element_type=jnp.float32)


def dot32t(a, b):
    return lax.dot_general(a, b, (((1,), (1,)), ((), ())), preferred_element_type=jnp.float32)


def swap(x, axis, k):
    n = lax.axis_size(axis)
    return lax.ppermute(x, axis, [(a, a ^ k) for a in range(n)])


def gather_low(x, axis, count):
    blocks = {0: x}
    step = count // 2
    while step:
        for k in list(blocks):
            blocks[k | step] = swap(blocks[k], axis, step)
        step //= 2
    return [blocks[k] for k in range(count)]


def add16(a, b):
    return (a.astype(jnp.float32) + b.astype(jnp.float32)).astype(jnp.bfloat16)


def pick(x, at):
    return lax.dynamic_index_in_dim(x, at, 0, keepdims=False)


def line_sums(streams, axis, finish, prepare):
    n = lax.axis_size(axis)
    here = lax.axis_index(axis)
    blocks = streams[0][0].shape[0]
    steps = ((lambda a: (a, a + 1)), (lambda a: (n - 1 - a, n - 2 - a)))
    sent = [[[] for _ in steps] for _ in streams]
    came = [[[] for _ in steps] for _ in streams]
    results, waits, ready = [], {}, []

    def drain(step):
        while ready:
            done, sums = ready.pop()
            after = [values[-1] for ways in sent for values in ways]
            waits[step], result = finish(done, sums, after, results, came[-1])
            results.append(result)

    for step in range(n + blocks - 1):
        for s, terms in enumerate(streams):
            if s:
                drain(step)
            for w, step_to in enumerate(steps):
                value = terms[w][step % blocks]
                if step:
                    last = came[s][w][-1]
                    if step == 2 and not s:
                        last = prepare(last)
                    if s and step in waits:
                        last, _ = lax.optimization_barrier((last, waits[step]))
                    value = add16(value, last)
                sent[s][w].append(value)
                pairs = [step_to(a) for a in range(n - 1) if 0 <= step - a < blocks]
                if pairs:
                    came[s][w].append(lax.ppermute(value, axis, pairs))
        done = step - (n - 1)
        if done >= 0:
            sums = []
            for s in range(len(streams)):
                up, down = sent[s][0], came[s][1]
                below, above = up[done + n - 1], jnp.zeros_like(up[0])
                for place in range(n - 1):
                    below = jnp.where(here == place, up[done + place], below)
                    above = jnp.where(here == place, down[done + n - 2 - place], above)
                sums.append(below.astype(jnp.float32) + above.astype(jnp.float32))
            ready.append((done, sums))
    drain(n + blocks - 1)
    return results


def slots(target, seq_rows, shards, each):
    shard = jnp.where(target >= 0, target // seq_rows, shards)
    same = shard[..., :, None] == shard[..., None, :]
    earlier = each[None, :] < each[:, None]
    rank = jnp.sum((same & earlier).astype(jnp.int32), axis=-1)
    return shard, rank


def attend_kernel(grid_ref, x_hbm, gain_ref, w_hbm, b_ref, *rest):
    outs, scratch = rest[:-10], rest[-10:]
    x_ref, w_ref, n_ref, pad_ref, bias_ref, q_ref, k_ref, v_ref, att_ref, sems = scratch
    load_w = pltpu.make_async_copy(w_hbm, w_ref, sems.at[0])
    load_x = pltpu.make_async_copy(x_hbm, x_ref, sems.at[1])
    load_w.start()
    load_x.start()
    rows = x_ref.shape[0]
    heads = w_ref.shape[1] // HEAD_DIM
    live = grid_ref[0, 0] * grid_ref[0, 1]
    tensor_at = lax.axis_index("tensor")
    lane = lax.broadcasted_iota(jnp.int32, (1, heads * LANES), 1) % LANES
    for j in range(3):
        bias_ref[j : j + 1, :] = jnp.where((lane == HEAD_DIM) & (j != 1), 1.0, 0.0)
        for h in range(heads):
            low, at = h * LANES, h * HEAD_DIM
            bias_ref[j : j + 1, low : low + HEAD_DIM] = b_ref[j : j + 1, at : at + HEAD_DIM]
            pad_ref[j, low + HEAD_DIM : low + LANES, :] = jnp.zeros(
                (LANES - HEAD_DIM, w_ref.shape[2]), jnp.bfloat16
            )
    load_w.wait()
    for j in range(3):
        for h in range(heads):
            low, at = h * LANES, h * HEAD_DIM
            pad_ref[j, low : low + HEAD_DIM, :] = w_ref[j, at : at + HEAD_DIM, :]
    load_x.wait()
    step = min(QUERY_ROWS, rows)
    scale = math.log2(math.e) / math.sqrt(HEAD_DIM)
    extra = lax.broadcasted_iota(jnp.int32, (step, heads * LANES), 1) % LANES == HEAD_DIM
    row = lax.broadcasted_iota(jnp.int32, (step, heads * LANES), 0)
    gain = gain_ref[...].reshape(1, -1)
    for at in range(0, rows, step):
        span = slice(at, at + step)
        normed = rms_scale(x_ref[span, :].astype(jnp.float32), gain)
        n_ref[span, :] = normed.astype(jnp.bfloat16)
        for j, ref in enumerate((q_ref, k_ref, v_ref)):
            out = dot32t(n_ref[span, :], pad_ref[j]) + bias_ref[j : j + 1, :]
            if j == 0:
                out = out * scale
            if j == 1:
                out = jnp.where(extra & (row + at >= live), -1e30, out)
            ref[span, :] = out.astype(jnp.bfloat16)
    for at in range(0, rows, step):
        span = slice(at, at + step)
        for h in range(heads):
            lanes = slice(h * LANES, (h + 1) * LANES)
            scores = dot32t(q_ref[span, lanes], k_ref[:, lanes])
            peak = jnp.max(scores, axis=-1, keepdims=True)
            weights = jnp.exp2(scores - peak).astype(jnp.bfloat16)
            mixed = dot32(weights, v_ref[:, lanes])
            mixed = mixed[:, :HEAD_DIM] / mixed[:, HEAD_DIM : HEAD_DIM + 1]
            att_ref[span, h * HEAD_DIM : (h + 1) * HEAD_DIM] = mixed.astype(jnp.bfloat16)
    quarter = rows // len(outs)
    stores = []
    for k, out_hbm in enumerate(outs):
        low = pl.multiple_of((tensor_at ^ k) * quarter, quarter)
        store = pltpu.make_async_copy(att_ref.at[pl.ds(low, quarter)], out_hbm, sems.at[2 + k])
        store.start()
        stores.append(store)
    for store in stores:
        store.wait()


def vmem():
    return pl.BlockSpec(memory_space=pltpu.VMEM)


def smem():
    return pl.BlockSpec(memory_space=pltpu.SMEM)


def hbm():
    return pl.BlockSpec(memory_space=pltpu.HBM)


def anywhere():
    return pl.BlockSpec(memory_space=pl.ANY)


def bf16(*shape):
    return jax.ShapeDtypeStruct(shape, jnp.bfloat16)


def bf16_scratch(*shape):
    return pltpu.VMEM(shape, jnp.bfloat16)


def attend(grids, x, gain, w, b, parts):
    rows, width = x.shape
    cols = w.shape[1]
    padded = cols // HEAD_DIM * LANES
    return pl.pallas_call(
        attend_kernel,
        out_shape=[bf16(rows // parts, cols)] * parts,
        in_specs=[smem(), anywhere(), vmem(), anywhere(), vmem()],
        out_specs=[hbm()] * parts,
        scratch_shapes=[
            bf16_scratch(rows, width),
            bf16_scratch(3, cols, width),
            bf16_scratch(rows, width),
            bf16_scratch(3, padded, width),
            pltpu.VMEM((8, padded), jnp.float32),
            bf16_scratch(rows, padded),
            bf16_scratch(rows, padded),
            bf16_scratch(rows, padded),
            bf16_scratch(rows, cols),
            pltpu.SemaphoreType.DMA((2 + parts,)),
        ],
        compiler_params=pltpu.CompilerParams(vmem_limit_bytes=ATTEND_VMEM_BYTES),
        cost_estimate=pl.CostEstimate(
            flops=2 * rows * (3 * width * cols + 2 * rows * cols),
            bytes_accessed=2 * (2 * rows * width + 3 * width * cols),
            transcendentals=rows * rows * cols // HEAD_DIM,
        ),
    )(grids, x, gain, w, b)


def project_kernel(count, splits, x_hbm, bias_ref, gain_ref, *rest):
    blocks, weights, outs = rest[:count], rest[count : 2 * count], rest[2 * count : -5]
    x_ref, block_ref, weight_ref, out_ref, sems = rest[-5:]
    rows, size = x_ref.shape[0], out_ref.shape[1]
    low = pl.multiple_of(lax.axis_index("tensor") * rows, rows)
    loads = [pltpu.make_async_copy(x_hbm.at[pl.ds(low, rows)], x_ref, sems.at[0])]
    for k in range(count):
        loads.append(pltpu.make_async_copy(blocks[k], block_ref.at[k], sems.at[1 + 2 * k]))
        loads.append(pltpu.make_async_copy(weights[k], weight_ref.at[k], sems.at[2 + 2 * k]))
    for load in loads:
        load.start()
    loads[0].wait()
    summed = x_ref[...].astype(jnp.float32) + bias_ref[...].reshape(1, -1)
    for k in range(count):
        loads[1 + 2 * k].wait()
        loads[2 + 2 * k].wait()
        summed = summed + dot32(block_ref[k], weight_ref[k])
    merged = rms_scale(summed, gain_ref[...].reshape(1, -1)).astype(jnp.bfloat16)
    out_row = lax.broadcasted_iota(jnp.int32, (rows, rows), 0)
    row = lax.broadcasted_iota(jnp.int32, (rows, rows), 1)
    four = (out_row // size) ^ (lax.axis_index("dp") // splits)
    sort = (row == out_row % size * MERGE + four).astype(jnp.bfloat16)
    stores = []
    for k, out_hbm in enumerate(outs):
        out_ref[k] = dot32(sort[k * size : (k + 1) * size, :], merged).astype(jnp.bfloat16)
        store = pltpu.make_async_copy(out_ref.at[k], out_hbm, sems.at[k])
        store.start()
        stores.append(store)
    for store in stores:
        store.wait()


def project(x, bias, gain, blocks, weights, splits):
    rows, cols = blocks[0].shape
    width = x.shape[1]
    count = len(blocks)
    return pl.pallas_call(
        functools.partial(project_kernel, count, splits),
        out_shape=[bf16(rows // MERGE, width)] * MERGE,
        in_specs=[hbm(), vmem(), vmem()] + ([hbm()] + [anywhere()] * (count - 1)) * 2,
        out_specs=[hbm()] * MERGE,
        scratch_shapes=[
            bf16_scratch(rows, width),
            bf16_scratch(count, rows, cols),
            bf16_scratch(count, cols, width),
            bf16_scratch(MERGE, rows // MERGE, width),
            pltpu.SemaphoreType.DMA((max(MERGE, 1 + 2 * count),)),
        ],
        compiler_params=pltpu.CompilerParams(vmem_limit_bytes=VMEM_BYTES),
        cost_estimate=pl.CostEstimate(
            flops=2 * rows * width * width,
            bytes_accessed=2 * width * width + 6 * rows * width,
            transcendentals=rows,
        ),
    )(x, bias, gain, *blocks, *weights)


def first_kernel(groups, batches, images, w_ref, *rest):
    blocks, (up_ref, down_ref), (cat_ref, sems) = rest[:-4], rest[-4:-2], rest[-2:]
    count = len(blocks) // groups
    size = cat_ref.shape[0] // len(blocks)
    here, line = lax.axis_index("dp"), lax.axis_size("dp")
    loads = []
    for g in range(groups):
        for j in range(count):
            image = j ^ (here % images) if images > 1 else j
            low = (g * count + image) * size
            low = pl.multiple_of(low, size) if images > 1 else low
            place = cat_ref.at[pl.ds(low, size)]
            k = g * count + j
            loads.append(pltpu.make_async_copy(blocks[k], place, sems.at[k]))
            loads[-1].start()
    for load in loads:
        load.wait()
    rows = count // batches * size
    for g in range(groups):
        low = g * count * size
        out = dot32(cat_ref[low : low + count * size, :], w_ref[...]).astype(jnp.bfloat16)
        for j in range(batches):
            batch = j ^ (here // images)
            part = out[j * rows : (j + 1) * rows]
            up_ref[(batch + here) % batches, g] = part
            down_ref[(batch + line - 1 - here) % batches, g] = part


def first(groups, batches, w, own):
    count = len(groups[0])
    blocks = [block for group in groups for block in group]
    rows, depth = blocks[0].shape
    images = count // batches
    out = bf16(batches, len(groups), images * rows, w.shape[1])
    return pl.pallas_call(
        functools.partial(first_kernel, len(groups), batches, images),
        out_shape=[out, out],
        in_specs=[vmem(), own] + [anywhere()] * (len(blocks) - 1),
        out_specs=[vmem(), vmem()],
        scratch_shapes=[
            bf16_scratch(rows * len(blocks), depth),
            pltpu.SemaphoreType.DMA((len(blocks),)),
        ],
        compiler_params=pltpu.CompilerParams(vmem_limit_bytes=VMEM_BYTES // 2),
        cost_estimate=pl.CostEstimate(
            flops=2 * rows * len(blocks) * depth * w.shape[1],
            bytes_accessed=2 * depth * w.shape[1] + 6 * rows * len(blocks) * depth,
            transcendentals=0,
        ),
    )(w, *blocks)


def second_kernel(count, bias_ref, goes_ref, w_hbm, *rest):
    totals, (send_ref, keep_ref), (w_ref, h_ref, sem) = rest[:count], rest[count:-3], rest[-3:]
    load = pltpu.make_async_copy(w_hbm, w_ref, sem)
    load.start()
    rows = totals[0].shape[0]
    bias = bias_ref[...].reshape(1, -1)
    for at, total in enumerate(totals):
        value = total[...] + bias
        value = 0.5 * value * (1.0 + lax.erf(value * math.sqrt(0.5)))
        h_ref[at * rows : (at + 1) * rows, :] = value.astype(jnp.bfloat16)
    half = send_ref.shape[0]
    index = lax.broadcasted_iota(jnp.int32, (half, 2 * half), 0)
    load.wait()
    for low, out_ref in ((half, send_ref), (0, keep_ref)):
        sort = (index + low == goes_ref[...]).astype(jnp.bfloat16)
        moved = dot32(sort, h_ref[...]).astype(jnp.bfloat16)
        out_ref[...] = dot32(moved, w_ref[...]).astype(jnp.bfloat16)


def second(totals, bias, goes, w):
    rows, width = totals[0].shape
    count = len(totals)
    out = bf16(rows * count // 2, w.shape[1])
    return pl.pallas_call(
        functools.partial(second_kernel, count),
        out_shape=[out, out],
        in_specs=[vmem(), vmem(), anywhere()] + [vmem()] * count,
        out_specs=[vmem(), vmem()],
        scratch_shapes=[
            bf16_scratch(*w.shape),
            bf16_scratch(rows * count, width),
            pltpu.SemaphoreType.DMA,
        ],
        compiler_params=pltpu.CompilerParams(vmem_limit_bytes=VMEM_BYTES),
        cost_estimate=pl.CostEstimate(
            flops=2 * rows * count * width * w.shape[1],
            bytes_accessed=2 * w.shape[0] * w.shape[1],
            transcendentals=rows * count * width,
        ),
    )(bias, goes, w, *totals)


def place_kernel(count, hit_ref, bias_ref, text_ref, *rest):
    blocks, out_ref, (cat_ref, sems) = rest[:count], rest[count], rest[-2:]
    loads, low = [], 0
    for k, block in enumerate(blocks):
        place = cat_ref.at[low : low + block.shape[0]]
        loads.append(pltpu.make_async_copy(block, place, sems.at[k]))
        loads[-1].start()
        low += block.shape[0]
    hit = hit_ref[...]
    covered = jnp.sum(hit.astype(jnp.float32), axis=1, keepdims=True) > 0
    for load in loads:
        load.wait()
    placed = dot32(hit, cat_ref[...]) + bias_ref[...].reshape(1, -1)
    out_ref[...] = jnp.where(covered, placed.astype(jnp.bfloat16), text_ref[...])


def place_rows(blocks, hit, bias, text):
    count = len(blocks)
    return pl.pallas_call(
        functools.partial(place_kernel, count),
        out_shape=bf16(*text.shape),
        in_specs=[vmem()] * 3 + [anywhere()] * count,
        out_specs=vmem(),
        scratch_shapes=[
            bf16_scratch(hit.shape[1], text.shape[1]),
            pltpu.SemaphoreType.DMA((count,)),
        ],
        compiler_params=pltpu.CompilerParams(vmem_limit_bytes=VMEM_BYTES // 2),
        cost_estimate=pl.CostEstimate(
            flops=2 * hit.shape[0] * hit.shape[1] * text.shape[1],
            bytes_accessed=4 * text.shape[0] * text.shape[1],
            transcendentals=0,
        ),
    )(hit, bias, text, *blocks)


def local(
    patches,
    grids,
    dest,
    norm_gain,
    qkv_weight,
    qkv_bias,
    proj_weight,
    proj_bias,
    merge_gain,
    w_first,
    b_first,
    w_second,
    b_second,
    text_embed,
):
    dps, tensors = lax.axis_size("dp"), lax.axis_size("tensor")
    tensor_at, dp_at = lax.axis_index("tensor"), lax.axis_index("dp")
    rows, width = patches.shape
    merged = dest.shape[1]
    seq_rows = text_embed.shape[0]
    cap = merged // dps
    part = cap // tensors

    proj_high = {0: proj_weight, tensors // 2: swap(proj_weight, "tensor", tensors // 2)}
    batches = min(dps, BATCHES)
    images = dps // batches
    live = grids[0, 0] * grids[0, 1]
    target = jnp.where(jnp.arange(merged, dtype=jnp.int32) * MERGE < live, dest[0], -1)
    targets = [swap(target, "dp", j) if j else target for j in range(dps)]
    blocks = attend(
        grids, patches, norm_gain, jnp.swapaxes(qkv_weight, 1, 2), qkv_bias, tensors
    )
    def places(targets, after):
        early = (targets, dp_at, tensor_at, jnp.arange(merged, dtype=jnp.int32))
        (targets, here, there, each), after = lax.optimization_barrier((early, after))
        targets = jnp.stack(targets)
        targets = targets[jnp.arange(dps) ^ here]
        shard, rank = slots(targets, seq_rows, dps, each)
        quarter = (rank // part) ^ there
        bits = tensors.bit_length() - 1
        quarter = sum(((quarter >> k) & 1) << (bits - 1 - k) for k in range(bits))
        goes = (quarter * dps + shard) * part + rank % part
        image = jnp.arange(dps)[:, None] % images
        goes = jnp.where(targets >= 0, goes * images + image, -1)
        goes = goes.reshape(batches, images, tensors, merged // tensors).transpose(0, 2, 1, 3)
        goes = goes[:, jnp.arange(tensors) ^ there].reshape(batches, 1, images * merged)
        slot_rows = jnp.sum(
            jnp.where(
                (shard == here)[:, None, :]
                & (rank[:, None, :] == jnp.arange(cap)[None, :, None]),
                targets[:, None, :] % seq_rows + 1,
                0,
            ),
            axis=-1,
        )
        slot_rows = slot_rows.reshape(batches, images, tensors, part).transpose(2, 0, 3, 1) - 1
        slot_rows = slot_rows[jnp.arange(tensors) ^ there].reshape(1, -1)
        rows_out = jnp.arange(seq_rows, dtype=jnp.int32)[:, None]
        return [goes, (rows_out == slot_rows).astype(jnp.bfloat16)], after

    blocks, targets = lax.optimization_barrier((list(blocks), targets))
    blocks = [swap(block, "tensor", k) if k else block for k, block in enumerate(blocks)]
    blocks, proj_high = lax.optimization_barrier((blocks, proj_high))
    proj_blocks = {}
    for k, high in proj_high.items():
        for j, block in enumerate(gather_low(high, "tensor", tensors // 2)):
            proj_blocks[k | j] = block
    proj_blocks = [proj_blocks[k] for k in range(tensors)]
    piece = w_first.shape[0]
    splits = width // piece
    merged_in = project(patches, proj_bias, merge_gain, blocks, proj_blocks, splits)

    near, far = ([[] for _ in range(tensors // 2)] for _ in range(2))
    for j in range(dps):
        block = merged_in[j // splits]
        if splits > 1:
            at = ((dp_at ^ j) % splits) * piece
            block = lax.dynamic_slice_in_dim(block, at, piece, 1)
        if j:
            block = swap(block, "dp", j)
        for k, line in enumerate(gather_low(block, "tensor", tensors // 2)):
            near[k].append(line)
        high = swap(block, "tensor", tensors // 2)
        for k, line in enumerate(gather_low(high, "tensor", tensors // 2)):
            far[k].append(line)
    near[0][1], _ = lax.optimization_barrier((near[0][1], far[0][:2]))
    streams = [first(near, batches, w_first, hbm()), first(far, batches, w_first, anywhere())]

    columns = w_second.shape[1]
    shares = dps // tensors

    def to_shards(members):
        members = jnp.stack(members, axis=1)
        blocks = []
        for j in range(dps):
            moved = pick(members, dp_at ^ j)
            blocks.append(swap(moved, "dp", j) if j else moved)
        return blocks

    pair_sums, early = [], []

    def finish(batch, sums, after, results, last):
        sums, _ = lax.optimization_barrier((sums, (after, pair_sums[-1:])))
        rows_in = [part.reshape(-1, w_second.shape[0]) for part in sums]
        send, block = second(rows_in, b_first, plan[0][batch], w_second)
        if batch == batches - 2:
            ends = [last[0][-1], last[1][-1], results[-1]]
            send, ends = lax.optimization_barrier((send, ends))
            last[0][-1], last[1][-1], results[-1] = ends
        if batch == batches - 1:
            early.extend(to_shards(results[: batches - 2]))
            ends = [results[-1], *early[1:3]]
            send, ends = lax.optimization_barrier((send, ends))
            results[-1], *early[1:3] = ends
        wait = send
        block = add16(block, swap(send, "tensor", 1))
        pair_sums.append(block)
        step = 2
        while step < tensors:
            half = block.shape[0] // 2
            block = add16(block[:half], swap(block[half:], "tensor", step))
            step *= 2
        return wait, block.reshape(dps, part * images, columns)

    plan = []

    def prepare(arrival):
        if not plan:
            plan.extend(places(targets, arrival)[0])
            return arrival
        arrival, plan[0] = lax.optimization_barrier((arrival, plan[0]))
        return arrival

    held = line_sums(streams, "dp", finish, prepare)
    arrived = [early, to_shards(held[batches - 2 :])]
    visual = [[] for _ in range(tensors)]
    for group in (arrived[:-1], arrived[-1:]):
        group = jnp.concatenate([jnp.stack(blocks) for blocks in group], axis=1)
        group = group.reshape(tensors, shares, -1, columns)
        for k in range(tensors):
            moved = pick(group, (tensor_at ^ k) ^ (dp_at // shares))
            moved = swap(moved, "tensor", k) if k else moved
            if shares > 1:
                moved = jnp.concatenate(
                    [pick(moved, (dp_at % shares) ^ j) for j in range(shares)], axis=-1
                )
            visual[k].append(moved.reshape(-1, shares * columns))
    visual = [block for blocks in visual for block in blocks]
    if any(block.shape[0] % 16 for block in visual):
        visual = [jnp.concatenate(visual, axis=0)]
    return place_rows(visual, plan[1], b_second, text_embed)


def solution(mesh):
    in_specs = (
        P(("groups", "dp"), None),
        P(("groups", "dp"), None),
        P(("groups", "dp"), None),
        P(),
        P(None, None, "tensor"),
        P(None, "tensor"),
        P("tensor", None),
        P(),
        P(),
        P("dp", "tensor"),
        P("tensor"),
        P("tensor", "dp"),
        P("tensor"),
        P(("groups", "dp"), "tensor"),
    )
    out_specs = P(("groups", "dp"), "tensor")
    return jax.shard_map(local, mesh=mesh, in_specs=in_specs, out_specs=out_specs, check_vma=False)
```

```python
import functools
import math

import jax
import jax.numpy as jnp
from jax import lax
from jax.experimental import pallas as pl
from jax.experimental.pallas import tpu as pltpu
from jax.sharding import PartitionSpec as P

HEAD_DIM = 80
MERGE = 4
BATCHES = 4
LANES = 128
QUERY_ROWS = 512
VMEM_BYTES = 48 * 1024 * 1024
ATTEND_VMEM_BYTES = 60 * 1024 * 1024


def rms_scale(values, gain):
    return values * lax.rsqrt(jnp.mean(values * values, axis=-1, keepdims=True) + 1e-06) * gain


def dot32(a, b):
    return jnp.dot(a, b, preferred_element_type=jnp.float32)


def dot32t(a, b):
    return lax.dot_general(a, b, (((1,), (1,)), ((), ())), preferred_element_type=jnp.float32)


def swap(x, axis, k):
    n = lax.axis_size(axis)
    return lax.ppermute(x, axis, [(a, a ^ k) for a in range(n)])


def gather_low(x, axis, count):
    blocks = {0: x}
    step = count // 2
    while step:
        for k in list(blocks):
            blocks[k | step] = swap(blocks[k], axis, step)
        step //= 2
    return [blocks[k] for k in range(count)]


def add16(a, b):
    return (a.astype(jnp.float32) + b.astype(jnp.float32)).astype(jnp.bfloat16)


def pick(x, at):
    return lax.dynamic_index_in_dim(x, at, 0, keepdims=False)


def line_sums(streams, axis, finish):
    n = lax.axis_size(axis)
    here = lax.axis_index(axis)
    blocks = streams[0][0].shape[0]
    steps = ((lambda a: (a, a + 1)), (lambda a: (n - 1 - a, n - 2 - a)))
    sent = [[[] for _ in steps] for _ in streams]
    came = [[[] for _ in steps] for _ in streams]
    results, waits, ready = [], {}, []

    def drain(step):
        while ready:
            done, sums = ready.pop()
            after = [values[-1] for ways in sent for values in ways]
            waits[step], result = finish(done, sums, after, results, came[-1])
            results.append(result)

    for step in range(n + blocks - 1):
        for s, terms in enumerate(streams):
            if s:
                drain(step)
            for w, step_to in enumerate(steps):
                value = terms[w][step % blocks]
                if step:
                    last = came[s][w][-1]
                    if s and step in waits:
                        last, _ = lax.optimization_barrier((last, waits[step]))
                    value = add16(value, last)
                sent[s][w].append(value)
                pairs = [step_to(a) for a in range(n - 1) if 0 <= step - a < blocks]
                if pairs:
                    came[s][w].append(lax.ppermute(value, axis, pairs))
        done = step - (n - 1)
        if done >= 0:
            sums = []
            for s in range(len(streams)):
                up, down = sent[s][0], came[s][1]
                below, above = up[done + n - 1], jnp.zeros_like(up[0])
                for place in range(n - 1):
                    below = jnp.where(here == place, up[done + place], below)
                    above = jnp.where(here == place, down[done + n - 2 - place], above)
                sums.append(below.astype(jnp.float32) + above.astype(jnp.float32))
            ready.append((done, sums))
    drain(n + blocks - 1)
    return results


def slots(target, seq_rows, shards, each):
    shard = jnp.where(target >= 0, target // seq_rows, shards)
    same = shard[..., :, None] == shard[..., None, :]
    earlier = each[None, :] < each[:, None]
    rank = jnp.sum((same & earlier).astype(jnp.int32), axis=-1)
    return shard, rank


def attend_kernel(grid_ref, x_hbm, gain_ref, w_hbm, b_ref, *rest):
    outs, scratch = rest[:-10], rest[-10:]
    x_ref, w_ref, n_ref, pad_ref, bias_ref, q_ref, k_ref, v_ref, att_ref, sems = scratch
    load_w = pltpu.make_async_copy(w_hbm, w_ref, sems.at[0])
    load_x = pltpu.make_async_copy(x_hbm, x_ref, sems.at[1])
    load_w.start()
    load_x.start()
    rows = x_ref.shape[0]
    heads = w_ref.shape[1] // HEAD_DIM
    live = grid_ref[0, 0] * grid_ref[0, 1]
    tensor_at = lax.axis_index("tensor")
    lane = lax.broadcasted_iota(jnp.int32, (1, heads * LANES), 1) % LANES
    for j in range(3):
        bias_ref[j : j + 1, :] = jnp.where((lane == HEAD_DIM) & (j != 1), 1.0, 0.0)
        for h in range(heads):
            low, at = h * LANES, h * HEAD_DIM
            bias_ref[j : j + 1, low : low + HEAD_DIM] = b_ref[j : j + 1, at : at + HEAD_DIM]
            pad_ref[j, low + HEAD_DIM : low + LANES, :] = jnp.zeros(
                (LANES - HEAD_DIM, w_ref.shape[2]), jnp.bfloat16
            )
    load_w.wait()
    for j in range(3):
        for h in range(heads):
            low, at = h * LANES, h * HEAD_DIM
            pad_ref[j, low : low + HEAD_DIM, :] = w_ref[j, at : at + HEAD_DIM, :]
    load_x.wait()
    step = min(QUERY_ROWS, rows)
    scale = math.log2(math.e) / math.sqrt(HEAD_DIM)
    extra = lax.broadcasted_iota(jnp.int32, (step, heads * LANES), 1) % LANES == HEAD_DIM
    row = lax.broadcasted_iota(jnp.int32, (step, heads * LANES), 0)
    gain = gain_ref[...].reshape(1, -1)
    for at in range(0, rows, step):
        span = slice(at, at + step)
        normed = rms_scale(x_ref[span, :].astype(jnp.float32), gain)
        n_ref[span, :] = normed.astype(jnp.bfloat16)
        for j, ref in enumerate((q_ref, k_ref, v_ref)):
            out = dot32t(n_ref[span, :], pad_ref[j]) + bias_ref[j : j + 1, :]
            if j == 0:
                out = out * scale
            if j == 1:
                out = jnp.where(extra & (row + at >= live), -1e30, out)
            ref[span, :] = out.astype(jnp.bfloat16)
    for at in range(0, rows, step):
        span = slice(at, at + step)
        for h in range(heads):
            lanes = slice(h * LANES, (h + 1) * LANES)
            scores = dot32t(q_ref[span, lanes], k_ref[:, lanes])
            peak = jnp.max(scores, axis=-1, keepdims=True)
            weights = jnp.exp2(scores - peak).astype(jnp.bfloat16)
            mixed = dot32(weights, v_ref[:, lanes])
            mixed = mixed[:, :HEAD_DIM] / mixed[:, HEAD_DIM : HEAD_DIM + 1]
            att_ref[span, h * HEAD_DIM : (h + 1) * HEAD_DIM] = mixed.astype(jnp.bfloat16)
    quarter = rows // len(outs)
    stores = []
    for k, out_hbm in enumerate(outs):
        low = pl.multiple_of((tensor_at ^ k) * quarter, quarter)
        store = pltpu.make_async_copy(att_ref.at[pl.ds(low, quarter)], out_hbm, sems.at[2 + k])
        store.start()
        stores.append(store)
    for store in stores:
        store.wait()


def vmem():
    return pl.BlockSpec(memory_space=pltpu.VMEM)


def smem():
    return pl.BlockSpec(memory_space=pltpu.SMEM)


def hbm():
    return pl.BlockSpec(memory_space=pltpu.HBM)


def anywhere():
    return pl.BlockSpec(memory_space=pl.ANY)


def bf16(*shape):
    return jax.ShapeDtypeStruct(shape, jnp.bfloat16)


def bf16_scratch(*shape):
    return pltpu.VMEM(shape, jnp.bfloat16)


def attend(grids, x, gain, w, b, parts):
    rows, width = x.shape
    cols = w.shape[1]
    padded = cols // HEAD_DIM * LANES
    return pl.pallas_call(
        attend_kernel,
        out_shape=[bf16(rows // parts, cols)] * parts,
        in_specs=[smem(), anywhere(), vmem(), anywhere(), vmem()],
        out_specs=[hbm()] * parts,
        scratch_shapes=[
            bf16_scratch(rows, width),
            bf16_scratch(3, cols, width),
            bf16_scratch(rows, width),
            bf16_scratch(3, padded, width),
            pltpu.VMEM((8, padded), jnp.float32),
            bf16_scratch(rows, padded),
            bf16_scratch(rows, padded),
            bf16_scratch(rows, padded),
            bf16_scratch(rows, cols),
            pltpu.SemaphoreType.DMA((2 + parts,)),
        ],
        compiler_params=pltpu.CompilerParams(vmem_limit_bytes=ATTEND_VMEM_BYTES),
        cost_estimate=pl.CostEstimate(
            flops=2 * rows * (3 * width * cols + 2 * rows * cols),
            bytes_accessed=2 * (2 * rows * width + 3 * width * cols),
            transcendentals=rows * rows * cols // HEAD_DIM,
        ),
    )(grids, x, gain, w, b)


def project_kernel(count, splits, x_hbm, bias_ref, gain_ref, *rest):
    blocks, weights, outs = rest[:count], rest[count : 2 * count], rest[2 * count : -5]
    x_ref, block_ref, weight_ref, out_ref, sems = rest[-5:]
    rows, size = x_ref.shape[0], out_ref.shape[1]
    low = pl.multiple_of(lax.axis_index("tensor") * rows, rows)
    loads = [pltpu.make_async_copy(x_hbm.at[pl.ds(low, rows)], x_ref, sems.at[0])]
    for k in range(count):
        loads.append(pltpu.make_async_copy(blocks[k], block_ref.at[k], sems.at[1 + 2 * k]))
        loads.append(pltpu.make_async_copy(weights[k], weight_ref.at[k], sems.at[2 + 2 * k]))
    for load in loads:
        load.start()
    loads[0].wait()
    summed = x_ref[...].astype(jnp.float32) + bias_ref[...].reshape(1, -1)
    for k in range(count):
        loads[1 + 2 * k].wait()
        loads[2 + 2 * k].wait()
        summed = summed + dot32(block_ref[k], weight_ref[k])
    merged = rms_scale(summed, gain_ref[...].reshape(1, -1)).astype(jnp.bfloat16)
    out_row = lax.broadcasted_iota(jnp.int32, (rows, rows), 0)
    row = lax.broadcasted_iota(jnp.int32, (rows, rows), 1)
    four = (out_row // size) ^ (lax.axis_index("dp") // splits)
    sort = (row == out_row % size * MERGE + four).astype(jnp.bfloat16)
    stores = []
    for k, out_hbm in enumerate(outs):
        out_ref[k] = dot32(sort[k * size : (k + 1) * size, :], merged).astype(jnp.bfloat16)
        store = pltpu.make_async_copy(out_ref.at[k], out_hbm, sems.at[k])
        store.start()
        stores.append(store)
    for store in stores:
        store.wait()


def project(x, bias, gain, blocks, weights, splits):
    rows, cols = blocks[0].shape
    width = x.shape[1]
    count = len(blocks)
    return pl.pallas_call(
        functools.partial(project_kernel, count, splits),
        out_shape=[bf16(rows // MERGE, width)] * MERGE,
        in_specs=[hbm(), vmem(), vmem()] + ([hbm()] + [anywhere()] * (count - 1)) * 2,
        out_specs=[hbm()] * MERGE,
        scratch_shapes=[
            bf16_scratch(rows, width),
            bf16_scratch(count, rows, cols),
            bf16_scratch(count, cols, width),
            bf16_scratch(MERGE, rows // MERGE, width),
            pltpu.SemaphoreType.DMA((max(MERGE, 1 + 2 * count),)),
        ],
        compiler_params=pltpu.CompilerParams(vmem_limit_bytes=VMEM_BYTES),
        cost_estimate=pl.CostEstimate(
            flops=2 * rows * width * width,
            bytes_accessed=2 * width * width + 6 * rows * width,
            transcendentals=rows,
        ),
    )(x, bias, gain, *blocks, *weights)


def first_kernel(groups, batches, images, w_ref, *rest):
    blocks, (up_ref, down_ref), (cat_ref, sems) = rest[:-4], rest[-4:-2], rest[-2:]
    count = len(blocks) // groups
    size = cat_ref.shape[0] // len(blocks)
    here, line = lax.axis_index("dp"), lax.axis_size("dp")
    loads = []
    for g in range(groups):
        for j in range(count):
            image = j ^ (here % images) if images > 1 else j
            low = (g * count + image) * size
            low = pl.multiple_of(low, size) if images > 1 else low
            place = cat_ref.at[pl.ds(low, size)]
            k = g * count + j
            loads.append(pltpu.make_async_copy(blocks[k], place, sems.at[k]))
            loads[-1].start()
    for load in loads:
        load.wait()
    rows = count // batches * size
    for g in range(groups):
        low = g * count * size
        out = dot32(cat_ref[low : low + count * size, :], w_ref[...]).astype(jnp.bfloat16)
        for j in range(batches):
            batch = j ^ (here // images)
            part = out[j * rows : (j + 1) * rows]
            up_ref[(batch + here) % batches, g] = part
            down_ref[(batch + line - 1 - here) % batches, g] = part


def first(groups, batches, w, own):
    count = len(groups[0])
    blocks = [block for group in groups for block in group]
    rows, depth = blocks[0].shape
    images = count // batches
    out = bf16(batches, len(groups), images * rows, w.shape[1])
    return pl.pallas_call(
        functools.partial(first_kernel, len(groups), batches, images),
        out_shape=[out, out],
        in_specs=[vmem(), own] + [anywhere()] * (len(blocks) - 1),
        out_specs=[vmem(), vmem()],
        scratch_shapes=[
            bf16_scratch(rows * len(blocks), depth),
            pltpu.SemaphoreType.DMA((len(blocks),)),
        ],
        compiler_params=pltpu.CompilerParams(vmem_limit_bytes=VMEM_BYTES // 2),
        cost_estimate=pl.CostEstimate(
            flops=2 * rows * len(blocks) * depth * w.shape[1],
            bytes_accessed=2 * depth * w.shape[1] + 6 * rows * len(blocks) * depth,
            transcendentals=0,
        ),
    )(w, *blocks)


def second_kernel(count, bias_ref, goes_ref, w_hbm, *rest):
    totals, (send_ref, keep_ref), (w_ref, h_ref, sem) = rest[:count], rest[count:-3], rest[-3:]
    load = pltpu.make_async_copy(w_hbm, w_ref, sem)
    load.start()
    rows = totals[0].shape[0]
    bias = bias_ref[...].reshape(1, -1)
    for at, total in enumerate(totals):
        value = total[...] + bias
        value = 0.5 * value * (1.0 + lax.erf(value * math.sqrt(0.5)))
        h_ref[at * rows : (at + 1) * rows, :] = value.astype(jnp.bfloat16)
    half = send_ref.shape[0]
    index = lax.broadcasted_iota(jnp.int32, (half, 2 * half), 0)
    load.wait()
    for low, out_ref in ((half, send_ref), (0, keep_ref)):
        sort = (index + low == goes_ref[...]).astype(jnp.bfloat16)
        moved = dot32(sort, h_ref[...]).astype(jnp.bfloat16)
        out_ref[...] = dot32(moved, w_ref[...]).astype(jnp.bfloat16)


def second(totals, bias, goes, w):
    rows, width = totals[0].shape
    count = len(totals)
    out = bf16(rows * count // 2, w.shape[1])
    return pl.pallas_call(
        functools.partial(second_kernel, count),
        out_shape=[out, out],
        in_specs=[vmem(), vmem(), anywhere()] + [vmem()] * count,
        out_specs=[vmem(), vmem()],
        scratch_shapes=[
            bf16_scratch(*w.shape),
            bf16_scratch(rows * count, width),
            pltpu.SemaphoreType.DMA,
        ],
        compiler_params=pltpu.CompilerParams(vmem_limit_bytes=VMEM_BYTES),
        cost_estimate=pl.CostEstimate(
            flops=2 * rows * count * width * w.shape[1],
            bytes_accessed=2 * w.shape[0] * w.shape[1],
            transcendentals=rows * count * width,
        ),
    )(bias, goes, w, *totals)


def place_kernel(count, hit_ref, bias_ref, text_ref, *rest):
    blocks, out_ref, (cat_ref, sems) = rest[:count], rest[count], rest[-2:]
    loads, low = [], 0
    for k, block in enumerate(blocks):
        place = cat_ref.at[low : low + block.shape[0]]
        loads.append(pltpu.make_async_copy(block, place, sems.at[k]))
        loads[-1].start()
        low += block.shape[0]
    hit = hit_ref[...]
    covered = jnp.sum(hit.astype(jnp.float32), axis=1, keepdims=True) > 0
    for load in loads:
        load.wait()
    placed = dot32(hit, cat_ref[...]) + bias_ref[...].reshape(1, -1)
    out_ref[...] = jnp.where(covered, placed.astype(jnp.bfloat16), text_ref[...])


def place_rows(blocks, hit, bias, text):
    count = len(blocks)
    return pl.pallas_call(
        functools.partial(place_kernel, count),
        out_shape=bf16(*text.shape),
        in_specs=[vmem()] * 3 + [anywhere()] * count,
        out_specs=vmem(),
        scratch_shapes=[
            bf16_scratch(hit.shape[1], text.shape[1]),
            pltpu.SemaphoreType.DMA((count,)),
        ],
        compiler_params=pltpu.CompilerParams(vmem_limit_bytes=VMEM_BYTES // 2),
        cost_estimate=pl.CostEstimate(
            flops=2 * hit.shape[0] * hit.shape[1] * text.shape[1],
            bytes_accessed=4 * text.shape[0] * text.shape[1],
            transcendentals=0,
        ),
    )(hit, bias, text, *blocks)


def local(
    patches,
    grids,
    dest,
    norm_gain,
    qkv_weight,
    qkv_bias,
    proj_weight,
    proj_bias,
    merge_gain,
    w_first,
    b_first,
    w_second,
    b_second,
    text_embed,
):
    dps, tensors = lax.axis_size("dp"), lax.axis_size("tensor")
    tensor_at, dp_at = lax.axis_index("tensor"), lax.axis_index("dp")
    rows, width = patches.shape
    merged = dest.shape[1]
    seq_rows = text_embed.shape[0]
    cap = merged // dps
    part = cap // tensors

    proj_high = {0: proj_weight, tensors // 2: swap(proj_weight, "tensor", tensors // 2)}
    batches = min(dps, BATCHES)
    images = dps // batches
    blocks = attend(
        grids, patches, norm_gain, jnp.swapaxes(qkv_weight, 1, 2), qkv_bias, tensors
    )
    def places(after):
        early = (grids, dest, dp_at, tensor_at, jnp.arange(merged, dtype=jnp.int32))
        (sides, rows_to, here, there, each), _ = lax.optimization_barrier((early, after))
        live = sides[0, 0] * sides[0, 1]
        target = jnp.where(each * MERGE < live, rows_to[0], -1)
        targets = jnp.stack([swap(target, "dp", j) if j else target for j in range(dps)])
        targets = targets[jnp.arange(dps) ^ here]
        shard, rank = slots(targets, seq_rows, dps, each)
        quarter = (rank // part) ^ there
        bits = tensors.bit_length() - 1
        quarter = sum(((quarter >> k) & 1) << (bits - 1 - k) for k in range(bits))
        goes = (quarter * dps + shard) * part + rank % part
        image = jnp.arange(dps)[:, None] % images
        goes = jnp.where(targets >= 0, goes * images + image, -1)
        goes = goes.reshape(batches, images, tensors, merged // tensors).transpose(0, 2, 1, 3)
        goes = goes[:, jnp.arange(tensors) ^ there].reshape(batches, 1, images * merged)
        slot_rows = jnp.sum(
            jnp.where(
                (shard == here)[:, None, :]
                & (rank[:, None, :] == jnp.arange(cap)[None, :, None]),
                targets[:, None, :] % seq_rows + 1,
                0,
            ),
            axis=-1,
        )
        slot_rows = slot_rows.reshape(batches, images, tensors, part).transpose(2, 0, 3, 1) - 1
        slot_rows = slot_rows[jnp.arange(tensors) ^ there].reshape(1, -1)
        rows_out = jnp.arange(seq_rows, dtype=jnp.int32)[:, None]
        return goes, (rows_out == slot_rows).astype(jnp.bfloat16)

    blocks = [swap(block, "tensor", k) if k else block for k, block in enumerate(blocks)]
    blocks[1], proj_high = lax.optimization_barrier((blocks[1], proj_high))
    goes, hit = places(blocks[1])
    proj_blocks = {}
    for k, high in proj_high.items():
        for j, block in enumerate(gather_low(high, "tensor", tensors // 2)):
            proj_blocks[k | j] = block
    proj_blocks = [proj_blocks[k] for k in range(tensors)]
    proj_bias, goes, hit = lax.optimization_barrier((proj_bias, goes, hit))
    piece = w_first.shape[0]
    splits = width // piece
    merged_in = project(patches, proj_bias, merge_gain, blocks, proj_blocks, splits)

    near, far = ([[] for _ in range(tensors // 2)] for _ in range(2))
    for j in range(dps):
        block = merged_in[j // splits]
        if splits > 1:
            at = ((dp_at ^ j) % splits) * piece
            block = lax.dynamic_slice_in_dim(block, at, piece, 1)
        if j:
            block = swap(block, "dp", j)
        for k, line in enumerate(gather_low(block, "tensor", tensors // 2)):
            near[k].append(line)
        high = swap(block, "tensor", tensors // 2)
        for k, line in enumerate(gather_low(high, "tensor", tensors // 2)):
            far[k].append(line)
    near[0][1], _ = lax.optimization_barrier((near[0][1], far[0][:2]))
    streams = [first(near, batches, w_first, hbm()), first(far, batches, w_first, anywhere())]

    columns = w_second.shape[1]
    shares = dps // tensors

    def to_shards(members):
        members = jnp.stack(members, axis=1)
        blocks = []
        for j in range(dps):
            moved = pick(members, dp_at ^ j)
            blocks.append(swap(moved, "dp", j) if j else moved)
        return blocks

    pair_sums, early = [], []

    def finish(batch, sums, after, results, last):
        sums, _ = lax.optimization_barrier((sums, (after, pair_sums[-1:])))
        rows_in = [part.reshape(-1, w_second.shape[0]) for part in sums]
        send, block = second(rows_in, b_first, goes[batch], w_second)
        if batch == batches - 2:
            ends = [last[0][-1], last[1][-1], results[-1]]
            send, ends = lax.optimization_barrier((send, ends))
            last[0][-1], last[1][-1], results[-1] = ends
        if batch == batches - 1:
            early.extend(to_shards(results[: batches - 2]))
            ends = [results[-1], *early[1:3]]
            send, ends = lax.optimization_barrier((send, ends))
            results[-1], *early[1:3] = ends
        wait = send
        block = add16(block, swap(send, "tensor", 1))
        pair_sums.append(block)
        step = 2
        while step < tensors:
            half = block.shape[0] // 2
            block = add16(block[:half], swap(block[half:], "tensor", step))
            step *= 2
        return wait, block.reshape(dps, part * images, columns)

    held = line_sums(streams, "dp", finish)
    arrived = [early, to_shards(held[batches - 2 :])]
    visual = [[] for _ in range(tensors)]
    for group in (arrived[:-1], arrived[-1:]):
        group = jnp.concatenate([jnp.stack(blocks) for blocks in group], axis=1)
        group = group.reshape(tensors, shares, -1, columns)
        for k in range(tensors):
            moved = pick(group, (tensor_at ^ k) ^ (dp_at // shares))
            moved = swap(moved, "tensor", k) if k else moved
            if shares > 1:
                moved = jnp.concatenate(
                    [pick(moved, (dp_at % shares) ^ j) for j in range(shares)], axis=-1
                )
            visual[k].append(moved.reshape(-1, shares * columns))
    visual = [block for blocks in visual for block in blocks]
    if any(block.shape[0] % 16 for block in visual):
        visual = [jnp.concatenate(visual, axis=0)]
    return place_rows(visual, hit, b_second, text_embed)


def solution(mesh):
    in_specs = (
        P(("groups", "dp"), None),
        P(("groups", "dp"), None),
        P(("groups", "dp"), None),
        P(),
        P(None, None, "tensor"),
        P(None, "tensor"),
        P("tensor", None),
        P(),
        P(),
        P("dp", "tensor"),
        P("tensor"),
        P("tensor", "dp"),
        P("tensor"),
        P(("groups", "dp"), "tensor"),
    )
    out_specs = P(("groups", "dp"), "tensor")
    return jax.shard_map(local, mesh=mesh, in_specs=in_specs, out_specs=out_specs, check_vma=False)
```
